32 devices in a mesh: grp: 8 (over y, x, core), seq: 4 (over z).
Axes of the slice: x: 2, y: 2, z: 4, core: 2. Of those that a mesh axis runs over, the one named last changes fastest.
Arguments:
- tokens: bfloat16 [32, 512, 1024], P('grp', 'seq'), may hold values from -6 to 6
- segment_ids: int32 [32, 512], P('grp'), may hold values from 0 to 17, as said below
- w_query: bfloat16 [1024, 1024], P(('grp', 'seq')), may hold values from -0.375 to 0.375
- w_key: bfloat16 [1024, 1024], P(('grp', 'seq')), may hold values from -0.1875 to 0.1875
- w_value: bfloat16 [1024, 1024], P(('grp', 'seq')), may hold values from -0.1875 to 0.1875
- w_output: bfloat16 [1024, 1024], P(('grp', 'seq')), may hold values from -0.5 to 0.5
- w_inner: bfloat16 [1024, 4096], P(('grp', 'seq')), may hold values from -0.1875 to 0.1875
- w_outer: bfloat16 [4096, 1024], P(('grp', 'seq')), may hold values from -0.125 to 0.125
- b_query: bfloat16 [1024], P(('grp', 'seq')), may hold values from -3 to 3
- b_value: bfloat16 [1024], P(('grp', 'seq')), may hold values from -3 to 3
- b_output: bfloat16 [1024], P(('grp', 'seq')), may hold values from -3 to 3
- b_inner: bfloat16 [4096], P(('grp', 'seq')), may hold values from -3 to 3
- b_outer: bfloat16 [1024], P(('grp', 'seq')), may hold values from -3 to 3
- norm1_gain: bfloat16 [1024], P(('grp', 'seq')), may hold values from 0.099609375 to 1.8984375
- norm1_bias: bfloat16 [1024], P(('grp', 'seq')), may hold values from -3 to 3
- norm2_gain: bfloat16 [1024], P(('grp', 'seq')), may hold values from 0.099609375 to 1.8984375
- norm2_bias: bfloat16 [1024], P(('grp', 'seq')), may hold values from -3 to 3
- cotangent: bfloat16 [32, 512, 1024], P('grp', 'seq'), may hold values from -6 to 6
Outputs:
- layer_out: bfloat16 [32, 512, 1024], P('grp', 'seq')
- grad_tokens: bfloat16 [32, 512, 1024], P('grp', 'seq')
- grad_w_query: float32 [1024, 1024], P('grp')
- grad_w_key: float32 [1024, 1024], P('grp')
- grad_w_value: float32 [1024, 1024], P('grp')
- grad_w_output: float32 [1024, 1024], P('grp')
- grad_w_inner: float32 [1024, 4096], P('grp')
- grad_w_outer: float32 [4096, 1024], P('grp')
- grad_b_query: float32 [1024], P('grp')
- grad_b_value: float32 [1024], P('grp')
- grad_b_output: float32 [1024], P('grp')
- grad_b_inner: float32 [4096], P('grp')
- grad_b_outer: float32 [1024], P('grp')
- grad_norm1_gain: float32 [1024], P('grp')
- grad_norm1_bias: float32 [1024], P('grp')
- grad_norm2_gain: float32 [1024], P('grp')
- grad_norm2_bias: float32 [1024], P('grp')
The draws below stay inside these ranges and needn't reach their ends.
Inputs may be any that keep to these rules, and one draw needn't show every extreme that they name: `segment_ids`: within a sequence equal nonzero ids form one run of positions (a document), ids never fall except to 0, and 0 marks padding at the sequence's end.
All inputs are finite; a program needn't handle non-finite values.
Results may differ from the reference program's by a relative error of at most 0.02.
Values may be sent and summed in bfloat16 or wider, within the bound.
A program may use at most 192 MiB of HBM per device.

```python
import math
import jax
import jax.numpy as jnp
from jax import lax

D = 1024
H = 16
HD = 64
FF = 4096
LEN = 512
SEQ_DEV = 4
SEQS = 32


def draw_segment_ids(key, part):
    key = jax.random.fold_in(key, 7)
    doc_slots = 16
    key_exp, key_span, key_long, key_pick, key_pad = jax.random.split(key, 5)
    exponents = jax.random.randint(key_exp, (SEQS, doc_slots), 1, 6)
    spans = jax.random.randint(key_span, (SEQS, doc_slots), 0, 1 << 20)
    limits = jnp.maximum(jnp.right_shift(jnp.int32(LEN), exponents), 1)
    doc_lengths = 1 + spans % limits
    long_length = LEN - 1 - jax.random.randint(key_long, (SEQS,), 0, LEN // 16)
    picks = jax.random.randint(key_pick, (SEQS // SEQ_DEV,), 0, SEQ_DEV)
    is_long = jnp.arange(SEQS) % SEQ_DEV == jnp.repeat(picks, SEQ_DEV)
    first_slot = (jnp.arange(doc_slots) == 0)[None, :]
    doc_lengths = jnp.where(is_long[:, None] & first_slot, long_length[:, None], doc_lengths)
    ends = jnp.cumsum(doc_lengths, axis=1)
    places = jnp.arange(LEN)
    labels = 1 + jnp.sum((ends[:, None, :] <= places[None, :, None]).astype(jnp.int32), axis=2)
    padding = jax.random.randint(key_pad, (SEQS,), 0, LEN // 4 + 1)
    padding = jnp.where(is_long, 0, padding)
    labels = jnp.where(places[None, :] >= LEN - padding[:, None], 0, labels)
    last_place = places[None, :] == LEN - 1
    labels = jnp.where(is_long[:, None] & last_place, doc_slots + 1, labels)
    return labels.astype(jnp.int32)


def block_scale(rng, shape, cuts, smallest, top_value):
    loudness = 1.0
    for dim, blocks in cuts:
        steps = jax.random.uniform(jax.random.fold_in(jax.random.fold_in(rng, 6), dim), (blocks,), jnp.float32, smallest / len(cuts), top_value / len(cuts))
        loudness = loudness * jnp.repeat(jnp.exp(steps), shape[dim] // blocks).reshape((-1,) + (1,) * (len(shape) - 1 - dim))
    return loudness


def centred(rng, dims, width, reach, cuts=(), kind=jnp.bfloat16):
    drawn = jax.random.normal(rng, dims, jnp.float32) * width
    if len(cuts) > 0:
        drawn = block_scale(rng, dims, cuts, -0.22, 0.18) * drawn
    return jnp.clip(drawn, min=-reach, max=reach).astype(kind)


def setup_inputs(seed: int = 0) -> dict:
    arg_keys = jax.random.split(jax.random.key(seed), 19)
    return {
        "tokens": centred(arg_keys[0], (SEQS, LEN, D), 1.0, 6.0, ((0, 8), (1, 4))),
        "segment_ids": draw_segment_ids(jax.random.fold_in(arg_keys[18], 71), 0),
        "w_query": centred(arg_keys[2], (D, D), (D // 4) ** -0.5, 0.375, ((0, 32),)),
        "w_key": centred(arg_keys[3], (D, D), D ** -0.5, 0.1875, ((0, 32),)),
        "w_value": centred(arg_keys[4], (D, D), D ** -0.5, 0.1875, ((0, 32),)),
        "w_output": centred(arg_keys[5], (D, D), (D // 8) ** -0.5, 0.5, ((0, 32),)),
        "w_inner": centred(arg_keys[6], (D, FF), D ** -0.5, 0.1875, ((0, 32),)),
        "w_outer": centred(arg_keys[7], (FF, D), (FF // 2) ** -0.5, 0.125, ((0, 32),)),
        "b_query": centred(arg_keys[8], (D,), 0.5, 3.0, ((0, 32),)),
        "b_value": centred(arg_keys[9], (D,), 0.5, 3.0, ((0, 32),)),
        "b_output": centred(arg_keys[10], (D,), 0.5, 3.0, ((0, 32),)),
        "b_inner": centred(arg_keys[11], (FF,), 0.5, 3.0, ((0, 32),)),
        "b_outer": centred(arg_keys[12], (D,), 0.5, 3.0, ((0, 32),)),
        "norm1_gain": jnp.clip(1.0 + 0.18 * jax.random.normal(arg_keys[13], (D,), jnp.float32), 0.099609375, 1.8984375).astype(jnp.bfloat16),
        "norm1_bias": centred(arg_keys[14], (D,), 0.5, 3.0, ((0, 32),)),
        "norm2_gain": jnp.clip(1.0 + 0.18 * jax.random.normal(arg_keys[15], (D,), jnp.float32), 0.099609375, 1.8984375).astype(jnp.bfloat16),
        "norm2_bias": centred(arg_keys[16], (D,), 0.5, 3.0, ((0, 32),)),
        "cotangent": centred(arg_keys[17], (SEQS, LEN, D), 1.0, 6.0, ((0, 8), (1, 4))),
    }


@jax.custom_vjp
def low(v):
    return lax.optimization_barrier(v.astype(jnp.bfloat16)).astype(jnp.float32)

@jax.custom_vjp
def low_back(v):
    return v

def low_keep(v):
    return (low(v), None)

def low_pass(kept, grad):
    return (grad,)

def back_keep(v):
    return (v, None)

def back_low(kept, grad):
    return (low(grad),)
low.defvjp(low_keep, low_pass)
low_back.defvjp(back_keep, back_low)

def matmul(left, right):
    return jnp.einsum('bld,de->ble', left, right, precision=lax.Precision.HIGHEST)

def normalize(row_data, gain_row, shift_row):
    centered = row_data - lax.optimization_barrier(jnp.mean(row_data, axis=-1, keepdims=True))
    variance = lax.optimization_barrier(jnp.mean(centered * centered, axis=-1, keepdims=True))
    return centered * lax.rsqrt(variance + 1e-06) * gain_row + shift_row

def attend(pieces):
    query_rows, key_rows, value_rows, labels = pieces
    length = labels.shape[0]
    query_heads = query_rows.reshape(length, H, HD)
    key_heads = key_rows.reshape(length, H, HD)
    value_heads = value_rows.reshape(length, H, HD)
    scores = jnp.einsum('qhd,khd->hqk', query_heads, key_heads, precision=lax.Precision.HIGHEST) * (1.0 / math.sqrt(HD))
    scores = low_back(scores)
    places = jnp.arange(length)
    allowed = (labels[:, None] == labels[None, :]) & (labels[None, :] != 0) | (places[:, None] == places[None, :])
    scores = jnp.where(allowed[None], scores, -1e+30)
    top = lax.optimization_barrier(jnp.max(scores, axis=-1, keepdims=True))
    expo = jnp.exp(scores - top)
    probs = low(expo / lax.optimization_barrier(jnp.sum(expo, axis=-1, keepdims=True)))
    mixed = jnp.einsum('hqk,khd->qhd', probs, value_heads, precision=lax.Precision.HIGHEST)
    return mixed.reshape(length, H * HD)

def one_layer(params, inputs, labels):
    w_query, w_key, w_value, w_output, w_inner, w_outer, b_query, b_value, b_output, b_inner, b_outer, norm1_gain, norm1_bias, norm2_gain, norm2_bias = params
    queries = low(low_back(matmul(inputs, w_query) + b_query))
    keys_all = low(low_back(matmul(inputs, w_key)))
    values_all = low(low_back(matmul(inputs, w_value) + b_value))
    context = lax.map(jax.checkpoint(attend), (queries, keys_all, values_all, labels))
    context = low(low_back(context))
    attention = low_back(matmul(context, w_output) + b_output)
    first = normalize(inputs + attention, norm1_gain, norm1_bias)
    inner = low_back(matmul(low(first), w_inner) + b_inner)
    hidden = low(jax.nn.gelu(inner, approximate=False))
    outer = low_back(matmul(hidden, w_outer) + b_outer)
    return normalize(first + outer, norm2_gain, norm2_bias)

def reference(tokens, segment_ids, w_query, w_key, w_value, w_output, w_inner, w_outer, b_query, b_value, b_output, b_inner, b_outer, norm1_gain, norm1_bias, norm2_gain, norm2_bias, cotangent):
    params = tuple((weight_in.astype(jnp.float32) for weight_in in (w_query, w_key, w_value, w_output, w_inner, w_outer, b_query, b_value, b_output, b_inner, b_outer, norm1_gain, norm1_bias, norm2_gain, norm2_bias)))
    rows_block = math.gcd(SEQS, 8)
    block_count = SEQS // rows_block
    inputs = tokens.astype(jnp.float32).reshape(block_count, rows_block, LEN, D)
    labels = segment_ids.reshape(block_count, rows_block, LEN)
    seeds = cotangent.astype(jnp.float32).reshape(block_count, rows_block, LEN, D)

    def block_step(totals, pieces):
        block_in, block_labels, block_seed = pieces

        def apply_layer(weights_in, rows_in):
            return one_layer(weights_in, rows_in, block_labels)
        block_out, pull_back = jax.vjp(apply_layer, params, block_in)
        grad_params, grad_rows = pull_back(block_seed)
        return (jax.tree.map(jnp.add, totals, grad_params), (block_out, grad_rows))
    zeros_init = jax.tree.map(jnp.zeros_like, params)
    totals, (outputs, grad_inputs) = lax.scan(block_step, zeros_init, (inputs, labels, seeds))
    layer_out = outputs.reshape(SEQS, LEN, D).astype(jnp.bfloat16)
    grad_tokens = grad_inputs.reshape(SEQS, LEN, D).astype(jnp.bfloat16)
    return (layer_out, grad_tokens, totals[0], totals[1], totals[2], totals[3], totals[4], totals[5], totals[6], totals[7], totals[8], totals[9], totals[10], totals[11], totals[12], totals[13], totals[14])
```

```python
import functools
import math

import jax
import jax.numpy as jnp
from jax import lax
from jax.experimental import pallas as pl
from jax.experimental.pallas import tpu as pltpu
from jax.sharding import PartitionSpec as P

H = 16
HD = 64
LINE = 4
RING = 8
UNITS = 12
MESH = pl.DeviceIdType.MESH
BF = jnp.bfloat16
F32 = jnp.float32
ANY = pl.BlockSpec(memory_space=pl.ANY)


class Place:
    def __init__(self):
        self.g = lax.axis_index("grp")
        self.s = lax.axis_index("seq")
        self.lo = lax.rem(self.g, RING)
        self.c = lax.rem(self.lo, 2)
        xb = lax.rem(self.lo // 2, 2)
        yb = self.lo // 4
        self.dc, self.dx, self.dy = 1 - 2 * self.c, 2 - 4 * xb, 4 - 8 * yb
        self.at_c = (self.g + self.dc, self.s)
        self.at_x = (self.g + self.dx, self.s)
        self.at_y = (self.g + self.dy, self.s)
        self.chip = self.lo // 2
        self.chip_x = self.chip + 1 - 2 * xb
        self.chip_y = self.chip + 2 - 4 * yb
        self.chip_d = self.chip_x + 2 - 4 * yb

    def along(self, t):
        return (self.g, t)


def send(src, dst, send_sem, recv_sem, to):
    return pltpu.make_async_remote_copy(
        src_ref=src, dst_ref=dst, send_sem=send_sem, recv_sem=recv_sem, device_id=to, device_id_type=MESH
    )


def greet(me):
    barrier = pltpu.get_barrier_semaphore()

    def signal(to):
        pl.semaphore_signal(barrier, inc=1, device_id=to, device_id_type=MESH)

    for to in (me.at_c, me.at_x, me.at_y):
        signal(to)
    for t in range(LINE):
        pl.when(me.s != t)(lambda t=t: signal(me.along(t)))
    pl.semaphore_wait(barrier, 3 + LINE - 1)


def exchange_sequences(me, whole, split, sems, index):
    send_sem, recv_sem, local_sem = sems
    block = split.shape[1]

    def copy(t):
        return send(
            split.at[t], whole.at[pl.ds(me.s * block, block)], send_sem.at[index, t], recv_sem.at[index, me.s], me.along(t)
        )

    def landed(t):
        return send(
            split.at[t], whole.at[pl.ds(t * block, block)], send_sem.at[index, t], recv_sem.at[index, t], me.along(t)
        )

    own = pltpu.make_async_copy(split.at[me.s], whole.at[pl.ds(me.s * block, block)], local_sem.at[index])

    def start():
        own.start()
        for t in range(LINE):
            pl.when(me.s != t)(lambda t=t: copy(t).start())

    def wait():
        own.wait()
        for t in range(LINE):
            pl.when(me.s != t)(lambda t=t: landed(t).wait_recv())

    def sent():
        for t in range(LINE):
            pl.when(me.s != t)(lambda t=t: copy(t).wait_send())

    return start, wait, sent


def return_sequences(me, whole, split, sems, index):
    send_sem, recv_sem, local_sem = sems
    block = split.shape[1]

    def copy(t):
        return send(
            whole.at[pl.ds(t * block, block)], split.at[me.s], send_sem.at[index, t], recv_sem.at[index, me.s], me.along(t)
        )

    def landed(t):
        return send(
            whole.at[pl.ds(t * block, block)], split.at[t], send_sem.at[index, t], recv_sem.at[index, t], me.along(t)
        )

    own = pltpu.make_async_copy(whole.at[pl.ds(me.s * block, block)], split.at[me.s], local_sem.at[index])

    def start():
        own.start()
        for t in range(LINE):
            pl.when(me.s != t)(lambda t=t: copy(t).start())

    def wait():
        own.wait()
        for t in range(LINE):
            pl.when(me.s != t)(lambda t=t: landed(t).wait_recv())

    def sent():
        for t in range(LINE):
            pl.when(me.s != t)(lambda t=t: copy(t).wait_send())

    return start, wait, sent


class Gather:
    def __init__(self, me, src, dst, rows, sems, u):
        self.me, self.src, self.dst, self.rows, self.u = me, src, dst, rows, u
        self.local, self.zs, self.zr, self.xs, self.xr, self.cs, self.cr = sems

    def own(self):
        me = self.me
        return pltpu.make_async_copy(self.src, self.dst((me.lo * LINE + me.s) * self.rows, self.rows), self.local.at[self.u])

    def z_copy(self, source, to, slot):
        me = self.me
        there = self.dst((me.lo * LINE + source) * self.rows, self.rows)
        return there, self.zs.at[self.u, slot], self.zr.at[self.u, source], me.along(to)

    def z_direct(self, to):
        me = self.me
        there, ss, rs, dev = self.z_copy(me.s, to, to)
        return send(self.src, there, ss, rs, dev)

    def z_pass(self, source, to):
        there, ss, rs, dev = self.z_copy(source, to, LINE - 1 - source if False else self.pass_slot(to))
        return send(there, there, ss, rs, dev)

    @staticmethod
    def pass_slot(to):
        return 1 if to == 0 else 2

    def start(self):
        me = self.me
        self.own().start()
        for t in range(LINE):
            near = (me.s != t) & (me.s - t <= 2) & (t - me.s <= 2)
            pl.when(near)(lambda t=t: self.z_direct(t).start())

    def z_recv(self, source):
        there, ss, rs, dev = self.z_copy(source, source, source)
        send(there, there, ss, rs, dev).wait_recv()

    def relay(self):
        me = self.me

        @pl.when(me.s == 1)
        def _():
            self.z_recv(3)
            self.z_pass(3, 0).start()

        @pl.when(me.s == 2)
        def _():
            self.z_recv(0)
            self.z_pass(0, 3).start()

    def line_done(self):
        me = self.me
        self.own().wait()
        for t in range(LINE):
            done = (me.s == 1) if t == 3 else ((me.s == 2) if t == 0 else (me.s == LINE))
            pl.when((me.s != t) & jnp.logical_not(done))(lambda t=t: self.z_recv(t))

    def block(self, lo, half=None):
        rows = self.rows * LINE
        if half is None:
            return self.dst(lo * rows, rows)
        return self.dst(lo * rows + half * (rows // 2), rows // 2)

    def x1(self, lo):
        return send(self.block(lo), self.block(lo), self.xs.at[self.u, 0], self.xr.at[self.u, 0], self.me.at_x)

    def y1(self, lo):
        return send(self.block(lo), self.block(lo), self.xs.at[self.u, 1], self.xr.at[self.u, 1], self.me.at_y)

    def x2(self, lo):
        return send(self.block(lo, 1), self.block(lo, 1), self.xs.at[self.u, 2], self.xr.at[self.u, 2], self.me.at_x)

    def y2(self, lo):
        return send(self.block(lo, 0), self.block(lo, 0), self.xs.at[self.u, 3], self.xr.at[self.u, 3], self.me.at_y)

    def core(self, lo, k):
        return send(self.block(lo), self.block(lo), self.cs.at[self.u, k], self.cr.at[self.u, k], self.me.at_c)

    def spread(self):
        me = self.me
        self.x1(me.lo).start()
        self.y1(me.lo).start()
        self.core(me.lo, 0).start()

    def cross(self):
        me = self.me
        lo_x, lo_y = me.lo + me.dx, me.lo + me.dy
        self.x1(lo_x).wait_recv()
        self.y2(lo_x).start()
        self.core(lo_x, 1).start()
        self.y1(lo_y).wait_recv()
        self.x2(lo_y).start()
        self.core(lo_y, 2).start()

    def corner(self):
        me = self.me
        lo_d = me.lo + me.dx + me.dy
        self.x2(lo_d).wait_recv()
        self.y2(lo_d).wait_recv()
        self.core(lo_d, 3).start()

    def whole(self):
        me = self.me
        for k, lo in enumerate((me.lo, me.lo + me.dx, me.lo + me.dy, me.lo + me.dx + me.dy)):
            self.core(lo + me.dc, k).wait_recv()

    def sent(self):
        me = self.me
        for t in range(LINE):
            near = (me.s != t) & (me.s - t <= 2) & (t - me.s <= 2)
            pl.when(near)(lambda t=t: self.z_direct(t).wait_send())
        pl.when(me.s == 1)(lambda: self.z_pass(3, 0).wait_send())
        pl.when(me.s == 2)(lambda: self.z_pass(0, 3).wait_send())
        self.x1(me.lo).wait_send()
        self.y1(me.lo).wait_send()
        self.x2(me.lo + me.dy).wait_send()
        self.y2(me.lo + me.dx).wait_send()
        for k, lo in enumerate((me.lo, me.lo + me.dx, me.lo + me.dy, me.lo + me.dx + me.dy)):
            self.core(lo, k).wait_send()


def rows_of(ref, columns=None):
    if columns is None:
        return lambda row, n: ref.at[pl.ds(row, n)]
    return lambda row, n: ref.at[pl.ds(row, n), columns]


def gather_kernel(
    tok, cot, vec, wq, wk, wv, wo, wi, wu,
    tok_all, cot_all, vec_all, wq_all, wk_all, wv_all, wo_all, wi_all, wu_all,
    local, zs, zr, xs, xr, cs, cr, a_send, a_recv, a_local,
):
    me = Place()
    sems = (local, zs, zr, xs, xr, cs, cr)
    a_sems = (a_send, a_recv, a_local)
    units = [Gather(me, vec, rows_of(vec_all), vec.shape[0], sems, 0)]

    def add(src, ref, columns=None):
        units.append(Gather(me, src, rows_of(ref, columns), src.shape[0], sems, len(units)))

    for src, ref in ((wq, wq_all), (wk, wk_all), (wv, wv_all), (wo, wo_all)):
        add(src, ref)
    width = wi.shape[1] // 4
    for j in range(4):
        add(wi.at[:, pl.ds(j * width, width)], wi_all, pl.ds(j * width, width))
    width = wu.shape[1] // 4
    for j in range(4):
        add(wu.at[:, pl.ds(j * width, width)], wu_all, pl.ds(j * width, width))
    n = len(units)
    greet(me)
    tokens = exchange_sequences(me, tok_all, tok, a_sems, 0)
    seed = exchange_sequences(me, cot_all, cot, a_sems, 1)
    units[0].start()
    units[1].start()
    units[2].start()
    tokens[0]()
    for k in range(n + 3):
        if k < n:
            units[k].relay()
            units[k].line_done()
            units[k].spread()
        if 0 <= k - 1 < n:
            units[k - 1].cross()
        if 0 <= k - 2 < n:
            units[k - 2].corner()
        if 0 <= k - 3 < n:
            units[k - 3].whole()
        if k + 3 < n:
            units[k + 3].start()
        if k == 6:
            seed[0]()
    tokens[1]()
    seed[1]()
    for unit in units:
        unit.sent()
    tokens[2]()
    seed[2]()


def gather_all(tok, cot, vec, weights):
    block = tok.shape[1] * LINE
    outs = [
        jax.ShapeDtypeStruct((block, tok.shape[2]), BF),
        jax.ShapeDtypeStruct((block, tok.shape[2]), BF),
        jax.ShapeDtypeStruct((vec.shape[0] * RING * LINE, vec.shape[1]), BF),
    ] + [jax.ShapeDtypeStruct((w.shape[0] * RING * LINE, w.shape[1]), BF) for w in weights]
    n = UNITS + 1
    dma = pltpu.SemaphoreType.DMA
    return pl.pallas_call(
        gather_kernel,
        out_shape=outs,
        in_specs=[ANY] * 9,
        out_specs=[ANY] * 9,
        scratch_shapes=[
            dma((n,)), dma((n, 4)), dma((n, 4)), dma((n, 4)), dma((n, 4)), dma((n, 4)), dma((n, 4)),
            dma((2, 4)), dma((2, 4)), dma((2,)),
        ],
        compiler_params=pltpu.CompilerParams(collective_id=0, has_side_effects=True, vmem_limit_bytes=56 << 20),
        name="gather_weights",
    )(tok, cot, vec, *weights)


def reduce_kernel(
    gq, gk, gv, go, gi, gu, vec, lay, gtok,
    lay_out, gtok_out, oq, ok, ov, oo, oi, ou, vec_out,
    from_core, half, plane, line, own, acc, zsum, ztot, vbuf, vrecv,
    cs, cr, hs, hr, ps, pr, zs, zr, own_sem, out_sem, vs, vr, vl, a_send, a_recv, a_local,
):
    me = Place()
    a_sems = (a_send, a_recv, a_local)
    rows = oq.shape[0]
    width = oq.shape[1]

    def square(ref, out):
        return (lambda lo: ref.at[pl.ds(lo * rows, rows)], out)

    units = []
    for j in range(4):
        units.append(
            (
                lambda lo, j=j: gu.at[pl.ds(lo * (4 * rows) + j * rows, rows)],
                ou.at[pl.ds(j * rows, rows)],
            )
        )
    for j in range(4):
        columns = pl.ds(j * width, width)
        units.append((lambda lo, columns=columns: gi.at[pl.ds(lo * rows, rows), columns], oi.at[:, columns]))
    units += [square(go, oo), square(gv, ov), square(gk, ok), square(gq, oq)]
    n = len(units)
    slots = acc.shape[0]

    def to_core(u, j):
        return send(units[u][0](2 * j + 1 - me.c), from_core.at[u, j], cs.at[u], cr.at[u], me.at_c)

    def own_load(u, j):
        return pltpu.make_async_copy(units[u][0](2 * j + me.c), own.at[u % slots, j], own_sem.at[u % slots, j])

    def half_x(u):
        a = acc.at[u % slots, me.chip_d, pl.ds(0, rows // 2)]
        return send(a, half.at[u, 0], hs.at[u, 0], hr.at[u, 0], me.at_x)

    def half_y(u):
        a = acc.at[u % slots, me.chip_d, pl.ds(rows // 2, rows // 2)]
        return send(a, half.at[u, 1], hs.at[u, 1], hr.at[u, 1], me.at_y)

    def plane_x(u):
        return send(acc.at[u % slots, me.chip_x], plane.at[u, 0], ps.at[u, 0], pr.at[u, 0], me.at_x)

    def plane_y(u):
        return send(acc.at[u % slots, me.chip_y], plane.at[u, 1], ps.at[u, 1], pr.at[u, 1], me.at_y)

    end = (me.s == 0) | (me.s == 3)
    mid = (me.s == 1) | (me.s == 2)
    partner = me.along(me.s + 1 - 2 * lax.rem(me.s, 2))
    other = me.along(3 - me.s)

    def line_in(u):
        return send(zsum.at[u], line.at[u, 0], zs.at[u, 0], zr.at[u, 0], partner)

    def line_swap(u):
        return send(zsum.at[u], line.at[u, 1], zs.at[u, 0], zr.at[u, 1], other)

    def line_out(u):
        return send(ztot.at[u], line.at[u, 0], zs.at[u, 1], zr.at[u, 0], partner)

    def out_mid(u):
        return pltpu.make_async_copy(ztot.at[u], units[u][1], out_sem.at[u])

    def out_end(u):
        return pltpu.make_async_copy(line.at[u, 0], units[u][1], out_sem.at[u])

    def wide(x):
        return x.astype(F32)

    def s0(u):
        for j in range(4):
            to_core(u, j).start()
        for j in range(4):
            own_load(u, j).start()

    def s1(u):
        if u >= slots:
            sent_acc(u - slots)
        for j in range(4):
            own_load(u, j).wait()
        send(from_core.at[u], from_core.at[u], cs.at[u], cr.at[u], me.at_c).wait_recv()
        slot = u % slots
        acc[slot] = (wide(own[slot]) + wide(from_core[u])).astype(BF)
        half_x(u).start()
        half_y(u).start()

    def s2(u):
        slot = u % slots
        low, high = pl.ds(0, rows // 2), pl.ds(rows // 2, rows // 2)
        half_x(u).wait_recv()
        acc[slot, me.chip_y, low] = (wide(acc[slot, me.chip_y, low]) + wide(half[u, 0])).astype(BF)
        plane_y(u).start()
        half_y(u).wait_recv()
        acc[slot, me.chip_x, high] = (wide(acc[slot, me.chip_x, high]) + wide(half[u, 1])).astype(BF)
        plane_x(u).start()

    def s3(u):
        slot = u % slots
        plane_x(u).wait_recv()
        plane_y(u).wait_recv()
        zsum[u] = (wide(acc[slot, me.chip]) + wide(plane[u, 0]) + wide(plane[u, 1])).astype(BF)
        pl.when(end)(lambda: line_in(u).start())

    def z1(u):
        @pl.when(mid)
        def _():
            line_in(u).wait_recv()
            zsum[u] = (wide(zsum[u]) + wide(line[u, 0])).astype(BF)
            line_swap(u).start()

    def z2(u):
        @pl.when(mid)
        def _():
            line_swap(u).wait_recv()
            ztot[u] = (wide(zsum[u]) + wide(line[u, 1])).astype(BF)
            line_out(u).start()
            out_mid(u).start()

    def z3(u):
        @pl.when(end)
        def _():
            line_out(u).wait_recv()
            out_end(u).start()

    def sent_acc(u):
        half_x(u).wait_send()
        half_y(u).wait_send()
        plane_x(u).wait_send()
        plane_y(u).wait_send()

    def finish(u):
        send(from_core.at[u], from_core.at[u], cs.at[u], cr.at[u], me.at_c).wait_send()
        pl.when(end)(lambda: line_in(u).wait_send())
        pl.when(end)(lambda: out_end(u).wait())

        @pl.when(mid)
        def _():
            line_swap(u).wait_send()
            line_out(u).wait_send()
            out_mid(u).wait()

    def v_swap(k, to):
        return send(vbuf.at[k], vrecv.at[k], vs.at[k], vr.at[k], to)

    v_to = (me.at_c, me.at_x, me.at_y)

    def v_step(k):
        if k == 0:
            pltpu.make_async_copy(vec, vbuf.at[0], vl).start()
            pltpu.make_async_copy(vec, vbuf.at[0], vl).wait()
            v_swap(0, v_to[0]).start()
        elif k < 4:
            v_swap(k - 1, v_to[k - 1]).wait_recv()
            vbuf[k] = vbuf[k - 1] + vrecv[k - 1]
            if k < 3:
                v_swap(k, v_to[k]).start()
            else:
                pl.when(end)(lambda: v_swap(3, partner).start())
        elif k == 4:

            @pl.when(mid)
            def _():
                v_swap(3, partner).wait_recv()
                vbuf[4] = vbuf[3] + vrecv[3]
                v_swap(4, other).start()

        elif k == 5:

            @pl.when(mid)
            def _():
                v_swap(4, other).wait_recv()
                vbuf[5] = vbuf[4] + vrecv[4]
                v_swap(5, partner).start()
                vec_out[...] = vbuf[5]

        elif k == 6:

            @pl.when(end)
            def _():
                v_swap(5, partner).wait_recv()
                vec_out[...] = vrecv[5]

    def v_finish():
        for k in range(3):
            v_swap(k, v_to[k]).wait_send()
        pl.when(end)(lambda: v_swap(3, partner).wait_send())

        @pl.when(mid)
        def _():
            v_swap(4, other).wait_send()
            v_swap(5, partner).wait_send()

    greet(me)
    back = return_sequences(me, lay, lay_out, a_sems, 0)
    back2 = return_sequences(me, gtok, gtok_out, a_sems, 1)
    stages = (s0, s1, s2, s3, z1, z2, z3)
    for k in range(n + len(stages) - 1):
        for d, stage in enumerate(stages):
            if 0 <= k - d < n:
                stage(k - d)
        if k < 7:
            v_step(k)
        if k == 1:
            back[0]()
        if k == 5:
            back2[0]()
    for u in range(n - slots, n):
        sent_acc(u)
    for u in range(n):
        finish(u)
    v_finish()
    back[1]()
    back2[1]()
    back[2]()
    back2[2]()


def reduce_all(grads, vec, lay, gtok, line_block):
    d = grads[0].shape[0]
    rows = d // RING
    n = UNITS
    slots = 4
    dma = pltpu.SemaphoreType.DMA
    vm = pltpu.VMEM
    sq = jax.ShapeDtypeStruct((rows, d), BF)
    outs = [jax.ShapeDtypeStruct((LINE, line_block, d), BF)] * 2 + [
        sq, sq, sq, sq,
        jax.ShapeDtypeStruct((rows, 4 * d), BF),
        jax.ShapeDtypeStruct((4 * rows, d), BF),
        jax.ShapeDtypeStruct(vec.shape, F32),
    ]
    return pl.pallas_call(
        reduce_kernel,
        out_shape=outs,
        in_specs=[ANY] * 9,
        out_specs=[ANY] * 8 + [pl.BlockSpec(memory_space=pltpu.VMEM)],
        scratch_shapes=[
            vm((n, 4, rows, d), BF), vm((n, 2, rows // 2, d), BF), vm((n, 2, rows, d), BF), vm((n, 2, rows, d), BF),
            vm((slots, 4, rows, d), BF), vm((slots, 4, rows, d), BF), vm((n, rows, d), BF), vm((n, rows, d), BF),
            vm((6,) + vec.shape, F32), vm((6,) + vec.shape, F32),
            dma((n,)), dma((n,)), dma((n, 2)), dma((n, 2)), dma((n, 2)), dma((n, 2)), dma((n, 2)), dma((n, 2)),
            dma((slots, 4)), dma((n,)), dma((6,)), dma((6,)), dma,
            dma((2, 4)), dma((2, 4)), dma((2,)),
        ],
        compiler_params=pltpu.CompilerParams(collective_id=1, has_side_effects=True, vmem_limit_bytes=58 << 20),
        name="reduce_grads",
    )(*grads, vec, lay, gtok)


def normalize(row_data, gain_row, shift_row):
    centered = row_data - jnp.mean(row_data, axis=-1, keepdims=True)
    variance = jnp.mean(centered * centered, axis=-1, keepdims=True)
    return centered * lax.rsqrt(variance + 1e-06) * gain_row + shift_row


def exact_gelu(values_in):
    return jax.nn.gelu(values_in, approximate=False)


def dot(a, b):
    return jnp.einsum("ab,bc->ac", a, b, preferred_element_type=F32)


def dot_t(a, b):
    return jnp.einsum("ab,cb->ac", a, b, preferred_element_type=F32)


def t_dot(a, b):
    return jnp.einsum("ab,ac->bc", a, b, preferred_element_type=F32)


def total(x):
    return jnp.sum(x.astype(F32), axis=0)


def heads(x):
    return x.reshape(x.shape[0], H, HD)


def layer(tokens, labels, weights, vectors, seed):
    wq, wk, wv, wo, wi, wu = weights
    bq, bv, bo, bi, bu, g1, s1, g2, s2 = vectors
    queries = (dot(tokens, wq) + bq).astype(BF)
    keys = dot(tokens, wk).astype(BF)
    values = (dot(tokens, wv) + bv).astype(BF)
    places = jnp.arange(labels.shape[0])
    marks = jnp.where(labels != 0, labels, -1 - places)
    allowed = marks[:, None] == marks[None, :]
    scale = 1.0 / math.sqrt(HD)
    raw = jnp.einsum("qhd,khd->hqk", heads(queries), heads(keys), preferred_element_type=F32) * scale
    scores = jnp.where(allowed[None], raw, -1e30)
    probs = jax.nn.softmax(scores, axis=-1)
    low = probs.astype(BF)
    context = jnp.einsum("hqk,khd->qhd", low, heads(values), preferred_element_type=F32)
    context = context.reshape(tokens.shape).astype(BF)
    attention = dot(context, wo) + bo
    first, first_pull = jax.vjp(normalize, tokens.astype(F32) + attention, g1, s1)
    first_low = first.astype(BF)
    inner = dot(first_low, wi) + bi
    hidden, gelu_pull = jax.vjp(exact_gelu, inner)
    hidden = hidden.astype(BF)
    second, second_pull = jax.vjp(normalize, first + dot(hidden, wu) + bu, g2, s2)
    layer_out = second.astype(BF)
    grad_second, grad_g2, grad_s2 = second_pull(seed.astype(F32))
    grad_outer = grad_second.astype(BF)
    (grad_inner,) = gelu_pull(dot_t(grad_outer, wu))
    grad_inner = grad_inner.astype(BF)
    grad_first = grad_second + dot_t(grad_inner, wi)
    grad_resid, grad_g1, grad_s1 = first_pull(grad_first)
    grad_attention = grad_resid.astype(BF)
    grad_context = dot_t(grad_attention, wo).astype(BF)
    grad_probs = jnp.einsum("qhd,khd->hqk", heads(grad_context), heads(values), preferred_element_type=F32)
    grad_scores = (probs * (grad_probs - jnp.sum(probs * grad_probs, axis=-1, keepdims=True))).astype(BF)
    gq = jnp.einsum("hqk,khd->qhd", grad_scores, heads(keys), preferred_element_type=F32) * scale
    gk = jnp.einsum("hqk,qhd->khd", grad_scores, heads(queries), preferred_element_type=F32) * scale
    gv = jnp.einsum("hqk,qhd->khd", low, heads(grad_context), preferred_element_type=F32)
    gq, gk, gv = (x.reshape(tokens.shape).astype(BF) for x in (gq, gk, gv))
    grad_tokens = (grad_resid + dot_t(gq, wq) + dot_t(gk, wk) + dot_t(gv, wv)).astype(BF)
    grads = (
        t_dot(tokens, gq), t_dot(tokens, gk), t_dot(tokens, gv), t_dot(context, grad_attention),
        t_dot(first_low, grad_inner), t_dot(hidden, grad_outer),
    )
    sums = (total(gq), total(gv), total(grad_attention), total(grad_inner), total(grad_outer), grad_g1, grad_s1, grad_g2, grad_s2)
    return layer_out, grad_tokens, tuple(g.astype(BF) for g in grads), sums


def local(tokens, labels, *rest):
    weights, vectors, cotangent = rest[:6], rest[6:15], rest[15]
    groups = lax.axis_size("grp") // RING
    g, s = lax.axis_index("grp"), lax.axis_index("seq")
    lo = lax.rem(g, RING)
    if groups > 1:
        def regroup(w):
            full = lax.all_gather(w, ("grp", "seq"), axis=0, tiled=True)
            n = full.shape[0] // (RING * LINE)
            return lax.dynamic_slice_in_dim(full, (lo * LINE + s) * n, n, 0)

        weights = tuple(regroup(w) for w in weights)
        vectors = tuple(regroup(v) for v in vectors)
    piece = vectors[0].shape[0]
    lanes = 128
    packed = [jnp.pad(v, (0, lanes - v.shape[0]))[None] for v in vectors]
    packed = jnp.concatenate(packed + [jnp.zeros((16 - len(vectors), lanes), BF)], axis=0)
    got = gather_all(tokens, cotangent, packed, weights)
    full_tokens, full_seed, full_vec = got[:3]
    full_weights = got[3:]
    full_vec = full_vec.reshape(RING * LINE, 16, lanes)
    full_vectors = [full_vec[:, i, : v.shape[0]].reshape(-1).astype(F32) for i, v in enumerate(vectors)]
    own_labels = lax.dynamic_index_in_dim(labels, s, 0, keepdims=False)
    lay, gtok, grads, sums = layer(full_tokens, own_labels, full_weights, full_vectors, full_seed)
    d = sums[0].shape[0]
    order = [0, 1, 2, 4, 5, 6, 7, 8, 3]
    stacked = jnp.concatenate([sums[i].reshape(-1, d) for i in order] + [jnp.zeros((4, d), F32)], axis=0)
    out = reduce_all(grads, stacked, lay, gtok, tokens.shape[1])
    layer_out, grad_tokens = out[:2]
    mats = [m.astype(F32) for m in out[2:8]]
    vec = out[8]
    flat = [vec[i] for i in range(8)] + [vec[8:12].reshape(-1)]
    back = dict(zip(order, flat))
    flat = [back[i] for i in range(9)]
    if groups > 1:
        same = [[l + RING * h for h in range(groups)] for l in range(RING)]
        eight = [[l + RING * h for l in range(RING)] for h in range(groups)]

        def rejoin(m):
            m = lax.psum(m, "grp", axis_index_groups=same)
            m = lax.all_gather(m, "grp", axis=0, tiled=True, axis_index_groups=eight)
            n = m.shape[0] // (RING * groups)
            return lax.dynamic_slice_in_dim(m, g * n, n, 0)

        mats = [rejoin(m) for m in mats]
        flat = [lax.psum(v, "grp", axis_index_groups=same) for v in flat]
    flat = [lax.dynamic_slice_in_dim(v, g * (v.shape[0] // (RING * groups)), v.shape[0] // (RING * groups), 0) for v in flat]
    return (layer_out, grad_tokens, *mats, *flat)


def solution(mesh):
    both = ("grp", "seq")
    rows = P("grp", "seq", None)
    return jax.shard_map(
        local,
        mesh=mesh,
        in_specs=(rows, P("grp", None)) + (P(both, None),) * 6 + (P(both),) * 9 + (rows,),
        out_specs=(rows, rows) + (P("grp", None),) * 6 + (P("grp"),) * 9,
        check_vma=False,
    )
```

```python
import functools
import math

import jax
import jax.numpy as jnp
from jax import lax
from jax.experimental import pallas as pl
from jax.experimental.pallas import tpu as pltpu
from jax.sharding import PartitionSpec as P

H = 16
HD = 64
LINE = 4
RING = 8
UNITS = 12
QUARTERS = 4
LANES = 128
MESH = pl.DeviceIdType.MESH
BF = jnp.bfloat16
F32 = jnp.float32
ANY = pl.BlockSpec(memory_space=pl.ANY)


class Place:
    def __init__(self):
        self.g = lax.axis_index("grp")
        self.s = lax.axis_index("seq")
        self.lo = lax.rem(self.g, RING)
        self.c = lax.rem(self.lo, 2)
        xb = lax.rem(self.lo // 2, 2)
        yb = self.lo // 4
        self.dc, self.dx, self.dy = 1 - 2 * self.c, 2 - 4 * xb, 4 - 8 * yb
        self.at_c = (self.g + self.dc, self.s)
        self.at_x = (self.g + self.dx, self.s)
        self.at_y = (self.g + self.dy, self.s)
        self.chip = self.lo // 2
        self.chip_x = self.chip + 1 - 2 * xb
        self.chip_y = self.chip + 2 - 4 * yb
        self.chip_d = self.chip_x + 2 - 4 * yb

    def along(self, t):
        return (self.g, t)


def send(src, dst, send_sem, recv_sem, to):
    return pltpu.make_async_remote_copy(
        src_ref=src, dst_ref=dst, send_sem=send_sem, recv_sem=recv_sem, device_id=to, device_id_type=MESH
    )


def greet(me):
    barrier = pltpu.get_barrier_semaphore()

    def signal(to):
        pl.semaphore_signal(barrier, inc=1, device_id=to, device_id_type=MESH)

    for to in (me.at_c, me.at_x, me.at_y):
        signal(to)
    for t in range(LINE):
        pl.when(me.s != t)(lambda t=t: signal(me.along(t)))
    pl.semaphore_wait(barrier, 3 + LINE - 1)


class Exchange:
    def __init__(self, me, whole, split, sems, index, back):
        self.me, self.whole, self.split, self.index, self.back = me, whole, split, index, back
        self.send_sem, self.recv_sem, self.local_sem = sems

    def rows(self, t):
        n = self.split.shape[1]
        return self.whole.at[pl.ds(t * n, n)]

    def ends(self, t):
        return (self.rows(t), self.split.at[self.me.s]) if self.back else (self.split.at[t], self.rows(self.me.s))

    def copy(self, t):
        src, dst = self.ends(t)
        return send(src, dst, self.send_sem.at[self.index, t], self.recv_sem.at[self.index, self.me.s], self.me.along(t))

    def landed(self, t):
        dst = self.split.at[t] if self.back else self.rows(t)
        return send(dst, dst, self.send_sem.at[self.index, t], self.recv_sem.at[self.index, t], self.me.along(t))

    def own(self):
        src, dst = self.ends(self.me.s)
        return pltpu.make_async_copy(src, dst, self.local_sem.at[self.index])

    def start(self, distance):
        s = self.me.s
        if distance == 1:
            self.own().start()
        for t in range(LINE):
            pl.when((s - t == distance) | (t - s == distance))(lambda t=t: self.copy(t).start())

    def wait(self):
        self.own().wait()
        for t in range(LINE):
            pl.when(self.me.s != t)(lambda t=t: self.landed(t).wait_recv())

    def sent(self):
        for t in range(LINE):
            pl.when(self.me.s != t)(lambda t=t: self.copy(t).wait_send())


class Gather:
    def __init__(self, me, src, dst, rows, sems, u):
        self.me, self.src, self.dst, self.rows, self.u = me, src, dst, rows, u
        self.local, self.zs, self.zr, self.xs, self.xr, self.cs, self.cr = sems

    def own(self):
        me = self.me
        return pltpu.make_async_copy(self.src, self.dst((me.lo * LINE + me.s) * self.rows, self.rows), self.local.at[self.u])

    def z_copy(self, source, to, slot):
        me = self.me
        there = self.dst((me.lo * LINE + source) * self.rows, self.rows)
        return there, self.zs.at[self.u, slot], self.zr.at[self.u, source], me.along(to)

    def z_direct(self, to):
        me = self.me
        there, ss, rs, dev = self.z_copy(me.s, to, to)
        return send(self.src, there, ss, rs, dev)

    def z_pass(self, source, to):
        there, ss, rs, dev = self.z_copy(source, to, self.pass_slot(to))
        return send(there, there, ss, rs, dev)

    @staticmethod
    def pass_slot(to):
        return 1 if to == 0 else 2

    def start(self):
        me = self.me
        self.own().start()
        for t in range(LINE):
            near = (me.s != t) & (me.s - t <= 2) & (t - me.s <= 2)
            pl.when(near)(lambda t=t: self.z_direct(t).start())

    def z_recv(self, source):
        there, ss, rs, dev = self.z_copy(source, source, source)
        send(there, there, ss, rs, dev).wait_recv()

    def relay(self):
        me = self.me

        @pl.when(me.s == 1)
        def _():
            self.z_recv(3)
            self.z_pass(3, 0).start()

        @pl.when(me.s == 2)
        def _():
            self.z_recv(0)
            self.z_pass(0, 3).start()

    def line_done(self):
        me = self.me
        self.own().wait()
        for t in range(LINE):
            done = (me.s == 1) if t == 3 else ((me.s == 2) if t == 0 else (me.s == LINE))
            pl.when((me.s != t) & jnp.logical_not(done))(lambda t=t: self.z_recv(t))

    def block(self, lo, half=None):
        rows = self.rows * LINE
        if half is None:
            return self.dst(lo * rows, rows)
        return self.dst(lo * rows + half * (rows // 2), rows // 2)

    def x1(self, lo):
        return send(self.block(lo), self.block(lo), self.xs.at[self.u, 0], self.xr.at[self.u, 0], self.me.at_x)

    def y1(self, lo):
        return send(self.block(lo), self.block(lo), self.xs.at[self.u, 1], self.xr.at[self.u, 1], self.me.at_y)

    def x2(self, lo):
        return send(self.block(lo, 1), self.block(lo, 1), self.xs.at[self.u, 2], self.xr.at[self.u, 2], self.me.at_x)

    def y2(self, lo):
        return send(self.block(lo, 0), self.block(lo, 0), self.xs.at[self.u, 3], self.xr.at[self.u, 3], self.me.at_y)

    def core(self, lo, k):
        return send(self.block(lo), self.block(lo), self.cs.at[self.u, k], self.cr.at[self.u, k], self.me.at_c)

    def spread(self):
        me = self.me
        self.x1(me.lo).start()
        self.y1(me.lo).start()
        self.core(me.lo, 0).start()

    def cross(self):
        me = self.me
        lo_x, lo_y = me.lo + me.dx, me.lo + me.dy
        self.x1(lo_x).wait_recv()
        self.y2(lo_x).start()
        self.core(lo_x, 1).start()
        self.y1(lo_y).wait_recv()
        self.x2(lo_y).start()
        self.core(lo_y, 2).start()

    def corner(self):
        me = self.me
        lo_d = me.lo + me.dx + me.dy
        self.x2(lo_d).wait_recv()
        self.y2(lo_d).wait_recv()
        self.core(lo_d, 3).start()

    def whole(self):
        me = self.me
        for k, lo in enumerate((me.lo, me.lo + me.dx, me.lo + me.dy, me.lo + me.dx + me.dy)):
            self.core(lo + me.dc, k).wait_recv()

    def sent(self):
        me = self.me
        for t in range(LINE):
            near = (me.s != t) & (me.s - t <= 2) & (t - me.s <= 2)
            pl.when(near)(lambda t=t: self.z_direct(t).wait_send())
        pl.when(me.s == 1)(lambda: self.z_pass(3, 0).wait_send())
        pl.when(me.s == 2)(lambda: self.z_pass(0, 3).wait_send())
        self.x1(me.lo).wait_send()
        self.y1(me.lo).wait_send()
        self.x2(me.lo + me.dy).wait_send()
        self.y2(me.lo + me.dx).wait_send()
        for k, lo in enumerate((me.lo, me.lo + me.dx, me.lo + me.dy, me.lo + me.dx + me.dy)):
            self.core(lo, k).wait_send()


def rows_of(ref, columns=None):
    if columns is None:
        return lambda row, n: ref.at[pl.ds(row, n)]
    return lambda row, n: ref.at[pl.ds(row, n), columns]


def rows_of(ref, columns=None):
    if columns is None:
        return lambda row, n: ref.at[pl.ds(row, n)]
    return lambda row, n: ref.at[pl.ds(row, n), columns]


def mm(a, b, ca=1, cb=0):
    return lax.dot_general(a, b, (((ca,), (cb,)), ((), ())), preferred_element_type=F32)


def at_tile(j, tile):
    return pl.ds(pl.multiple_of(j * tile, tile), tile)


def iota(shape, dim):
    return lax.broadcasted_iota(jnp.int32, shape, dim)


def half_masks():
    low = (iota((1, LANES), 1) < HD).astype(F32)
    return low, 1.0 - low


def gelu_parts(u):
    t = 1.0 / (1.0 + (0.3275911 * 0.7071067811865476) * jnp.abs(u))
    poly = t * (0.254829592 + t * (-0.284496736 + t * (1.421413741 + t * (-1.453152027 + t * 1.061405429))))
    bell = jnp.exp(-0.5 * u * u)
    tail = 0.5 * poly * bell
    cdf = jnp.where(u >= 0.0, 1.0 - tail, tail)
    return u * cdf, cdf + u * (bell * 0.3989422804014327)


def stats(r):
    centered = r - jnp.mean(r, axis=-1, keepdims=True)
    scale = lax.rsqrt(jnp.mean(centered * centered, axis=-1, keepdims=True) + 1e-06)
    return centered * scale, scale


def norm_back(u, n, scale):
    return (u - jnp.mean(u, axis=-1, keepdims=True) - n * jnp.mean(u * n, axis=-1, keepdims=True)) * scale


def eighths(x):
    return jnp.sum(x.reshape(x.shape[0] // 8, 8, x.shape[1]), axis=0)


ROW = 64
TILE = 256
BQ, BV, BO, BI, BU, G1, S1, G2, S2 = range(9)
INNER = 16


def forward_kernel(
    tok, cot, mark_row, mark_col, vec, wq, wk, wv, wo, wi, wu,
    x_out, wq_all, wk_all, wv_all, wo_all, wi_all, wu_all, q_out, k_out, v_out, p_out, ctx_out, low_out,
    n1_out, scale_out, hid_out, slope_out, gsec_out, gout_out, lay_out, vec_out, part_out,
    x, seed, packed, vecs, part, w_in, wu_in, q, k, v, bias, probs, ctx, n1, scale1, low, hidden, slope, res, gsec, gout, lay,
    local, zs, zr, xs, xr, cs, cr, a_send, a_recv, a_local, w_sem, p_sem, o_sem,
):
    me = Place()
    sems = (local, zs, zr, xs, xr, cs, cr)
    a_sems = (a_send, a_recv, a_local)
    d = x.shape[1]
    length = x.shape[0]
    units, pieces = [], []

    def add(src, ref, columns=None):
        units.append(Gather(me, src, rows_of(ref, columns), src.shape[0], sems, len(units)))
        pieces.append(ref if columns is None else ref.at[:, columns])

    add(wq, wq_all)
    add(vec, packed)
    for src, ref in ((wk, wk_all), (wv, wv_all), (wo, wo_all)):
        add(src, ref)
    for src, ref in ((wi, wi_all), (wu, wu_all)):
        width = src.shape[1] // QUARTERS
        for j in range(QUARTERS):
            columns = pl.ds(j * width, width)
            add(src.at[:, columns], ref, columns)
    n = len(units)
    saves = []

    def save(src, dst):
        copy = pltpu.make_async_copy(src, dst, o_sem.at[len(saves)])
        copy.start()
        saves.append(copy)

    def load(u):
        if u < n - QUARTERS:
            slot = (u if u == 0 else u - 1) % 3
            return pltpu.make_async_copy(pieces[u], w_in.at[slot], w_sem.at[slot])
        slot = (u - (n - QUARTERS)) % 2
        return pltpu.make_async_copy(pieces[u], wu_in.at[slot], w_sem.at[3 + slot])

    def row(i):
        return vecs[pl.ds(i, 1), :]

    def unpack():
        p = packed[...]
        piece = d // (RING * LINE)
        spread = (iota((LANES, d), 1) % piece == iota((LANES, d), 0)).astype(BF)
        wide = mm(p, spread).reshape(RING * LINE, 16, d)
        here = iota((RING * LINE, 1, d), 0) == iota((RING * LINE, 1, d), 2) // piece
        vecs[pl.ds(0, 16), :] = jnp.sum(jnp.where(here, wide, 0.0), axis=0)
        p = p.astype(F32).reshape(RING * LINE, 16, LANES)
        p = jnp.sum(jnp.where(iota(p.shape, 1) == BI, p, 0.0), axis=1).astype(BF)
        spread = (iota((LANES, d), 1) % LANES == iota((LANES, d), 0)).astype(BF)
        per = RING * LINE // QUARTERS
        wide = mm(p, spread).reshape(QUARTERS, per, d)
        here = iota((1, per, d), 1) == iota((1, per, d), 2) // LANES
        inner = jnp.sum(jnp.where(here, wide, 0.0), axis=1)
        vecs[pl.ds(INNER, 8), :] = jnp.concatenate([inner, jnp.zeros_like(inner)], axis=0)

    def project():
        bias[...] = jnp.where(mark_col[...] == mark_row[...], 0.0, -1e30)
        for slot, out, b, factor in ((0, q, BQ, 1.0 / math.sqrt(HD)), (1, k, None, None), (2, v, BV, None)):

            def step(j, _):
                tile = at_tile(j, TILE)
                y = mm(x[...], w_in[slot, :, tile])
                if b is not None:
                    y = y + vecs[pl.ds(b, 1), tile]
                y = y.astype(BF)
                if factor is not None:
                    y = (y.astype(F32) * factor).astype(BF)
                out[2 * j] = y[:, :LANES]
                out[2 * j + 1] = y[:, LANES:]
                return 0

            lax.fori_loop(0, d // TILE, step, 0)

    def p_save(h, slot):
        return pltpu.make_async_copy(probs.at[slot], p_out.at[h], p_sem.at[slot])

    def attend(first, last):
        def step(pair, _):
            masks = half_masks()
            kp, vp = k[pair], v[pair]
            qp = q[pair]
            out = None
            for h in range(2):
                slot = 2 * lax.rem(pair, 2) + h
                pl.when(pair >= 2)(lambda: p_save(2 * pair + h, slot).wait())
                scores = mm(qp * masks[h].astype(BF), kp, 1, 1) + bias[...]
                e = jnp.exp(scores - jnp.max(scores, axis=1, keepdims=True))
                p = (e * (1.0 / jnp.sum(e, axis=1, keepdims=True))).astype(BF)
                probs[slot] = p
                p_save(2 * pair + h, slot).start()
                part_out_h = mm(p, vp) * masks[h]
                out = part_out_h if out is None else out + part_out_h
            ctx[:, at_tile(pair, LANES)] = out.astype(BF)
            return 0

        lax.fori_loop(first, last, step, 0)

    def first_norm():
        def step(j, _):
            tile = at_tile(j, TILE)
            y = mm(ctx[...], w_in[0, :, tile]) + vecs[pl.ds(BO, 1), tile]
            n1[:, tile] = y + x[:, tile].astype(F32)
            return 0

        lax.fori_loop(0, d // TILE, step, 0)

        def norm(j, _):
            rows = at_tile(j, ROW)
            centred, scale = stats(n1[rows, :])
            n1[rows, :] = centred
            scale1[rows, :] = jnp.broadcast_to(scale, (ROW, LANES))
            first = centred * row(G1) + row(S1)
            low[rows, :] = first.astype(BF)
            res[rows, :] = first + row(BU)
            return 0

        lax.fori_loop(0, length // ROW, norm, 0)

    def inner(quarter, slot):
        def step(j, _):
            tile = at_tile(j, TILE)
            u = mm(low[...], w_in[slot, :, tile]) + vecs[pl.ds(INNER + quarter, 1), tile]
            act, grad = gelu_parts(u)
            hidden[quarter, :, tile] = act.astype(BF)
            slope[quarter, :, tile] = grad.astype(BF)
            return 0

        lax.fori_loop(0, d // TILE, step, 0)

    def outer(piece, slot):
        tile = pl.ds(piece * TILE, TILE)
        y = res[:, tile]
        for quarter in range(QUARTERS):
            y = y + mm(hidden[quarter], wu_in[slot, pl.ds(quarter * d, d), :])
        res[:, tile] = y

    def second_norm():
        def step(j, sums):
            rows = at_tile(j, ROW)
            centred, scale = stats(res[rows, :])
            lay[rows, :] = (centred * row(G2) + row(S2)).astype(BF)
            g = seed[rows, :].astype(F32)
            grad = norm_back(g * row(G2), centred, scale)
            gsec[rows, :] = grad
            rounded = grad.astype(BF)
            gout[rows, :] = rounded
            return sums[0] + eighths(g * centred), sums[1] + eighths(g), sums[2] + eighths(rounded.astype(F32))

        zero = jnp.zeros((8, d), F32)
        sums = lax.fori_loop(0, length // ROW, step, (zero, zero, zero))
        for i, s in enumerate(sums):
            part[pl.ds(i, 1), :] = jnp.sum(s, axis=0, keepdims=True)

    greet(me)
    tokens = Exchange(me, x, tok, a_sems, 0, False)
    seeds = Exchange(me, seed, cot, a_sems, 1, False)
    part[...] = jnp.zeros_like(part)
    units[0].start()
    units[1].start()
    units[2].start()
    for tick in range(n + 3):
        if tick < n:
            units[tick].relay()
            units[tick].line_done()
            units[tick].spread()
        if tick + 3 < n:
            units[tick + 3].start()
        if tick < 3:
            tokens.start((2, 3, 1)[tick])
        if 6 <= tick < 9:
            seeds.start((2, 3, 1)[tick - 6])
        if 0 <= tick - 1 < n:
            units[tick - 1].cross()
        if 0 <= tick - 2 < n:
            units[tick - 2].corner()
        done = tick - 3
        if done >= 0:
            units[done].whole()
            if done != 1:
                load(done).start()
        if tick == 4:
            unpack()
            save(vecs, vec_out)
        if tick == 6:
            tokens.wait()
            save(x, x_out)
            for u in (0, 2, 3):
                load(u).wait()
            project()
            for src, dst in ((q, q_out), (k, k_out), (v, v_out)):
                save(src, dst)
        if tick == 7:
            attend(0, 4)
        if tick == 8:
            attend(4, 8)
            save(ctx, ctx_out)
        if tick == 9:
            load(4).wait()
            first_norm()
            for src, dst in ((n1, n1_out), (scale1, scale_out), (low, low_out)):
                save(src, dst)
            load(5).wait()
            inner(0, 1)
        if 10 <= tick < 13:
            load(tick - 4).wait()
            inner(tick - 9, (tick - 8) % 3)
        if tick == 12:
            save(hidden, hid_out)
            save(slope, slope_out)
        if 13 <= tick < 16:
            load(tick - 4).wait()
            outer(tick - 13, (tick - 13) % 2)
    load(n - 1).wait()
    outer(3, 1)
    seeds.wait()
    second_norm()
    for src, dst in ((gsec, gsec_out), (gout, gout_out), (lay, lay_out), (part, part_out)):
        save(src, dst)
    for unit in units:
        unit.sent()
    tokens.sent()
    seeds.sent()
    for slot in range(4):
        p_save(12 + slot, slot).wait()
    for copy in saves:
        copy.wait()


def forward_all(tok, cot, mark_row, mark_col, vec, weights):
    d = tok.shape[2]
    length = tok.shape[1] * LINE
    pairs = d // LANES
    quarter = weights[4].shape[1] // QUARTERS
    shape = jax.ShapeDtypeStruct
    bf, wide = shape((length, d), BF), shape((length, d), F32)
    heads = shape((pairs, length, LANES), BF)
    mlp = shape((QUARTERS, length, quarter), BF)
    outs = (
        [bf]
        + [shape((w.shape[0] * RING * LINE, w.shape[1]), BF) for w in weights]
        + [heads, heads, heads, shape((2 * pairs, length, length), BF), bf, bf]
        + [wide, shape((length, LANES), F32), mlp, mlp, wide, bf, bf, shape((24, d), F32), shape((8, d), F32)]
    )
    n = UNITS + 1
    dma = pltpu.SemaphoreType.DMA

    def vm(s):
        return pltpu.VMEM(s.shape, s.dtype)

    vmem = pl.BlockSpec(memory_space=pltpu.VMEM)
    return pl.pallas_call(
        forward_kernel,
        out_shape=outs,
        in_specs=[ANY, ANY, vmem, vmem] + [ANY] * 7,
        out_specs=[ANY] * len(outs),
        scratch_shapes=[
            vm(bf), vm(bf), pltpu.VMEM((vec.shape[0] * RING * LINE, LANES), BF), pltpu.VMEM((24, d), F32), pltpu.VMEM((8, d), F32),
            pltpu.VMEM((3, d, d), BF), pltpu.VMEM((2, QUARTERS * quarter, d // QUARTERS), BF),
            vm(heads), vm(heads), vm(heads), pltpu.VMEM((length, length), F32), pltpu.VMEM((4, length, length), BF),
            vm(bf), vm(wide), pltpu.VMEM((length, LANES), F32), vm(bf), vm(mlp), vm(mlp), vm(wide), vm(wide), vm(bf), vm(bf),
            dma((n,)), dma((n, 4)), dma((n, 4)), dma((n, 4)), dma((n, 4)), dma((n, 4)), dma((n, 4)),
            dma((2, 4)), dma((2, 4)), dma((2,)), dma((5,)), dma((4,)), dma((16,)),
        ],
        compiler_params=pltpu.CompilerParams(collective_id=0, has_side_effects=True, vmem_limit_bytes=58 << 20),
        name="forward",
    )(tok, cot, mark_row, mark_col, vec, *weights)


def backward_kernel(
    x_in, wq, wk, wv, wo, wi, wu, q_in, k_in, v_in, p_in, ctx_in, low_in,
    n1_in, scale_in, hid_in, slope_in, gsec_in, gout_in, lay_in, vec_in, part_in,
    lay_out, gtok_out, oq, ok, ov, oo, oi, ou, vec_out,
    from_core, half, plane, line, own, to_send, acc, zsum, ztot, vbuf, vrecv,
    hidden, gout, slope, ginner, gfirst, n1, scale1, low, dk, dv, probs, w_in, vecs, part, sums,
    credit, cs, cr, hs, hr, ps, pr, zs, zr, out_sem, vs, vr, a_send, a_recv, a_local, i_sem, w_sem, p_sem,
):
    me = Place()
    a_sems = (a_send, a_recv, a_local)
    length, d = gout.shape
    rows = d // RING
    q, k, v, x = hidden.at[0], hidden.at[1], hidden.at[2], hidden.at[3]
    gattn, gctx, ctx, gtok = slope.at[0], slope.at[1], slope.at[2], slope.at[3]
    dq = gout

    units = []

    def whole(ref):
        return lambda lo: ref[:, at_tile(lo, rows)]

    def tall(j):
        return lambda lo: hidden[lo // 2, :, pl.ds(pl.multiple_of(lax.rem(lo, 2) * (QUARTERS * rows) + j * rows, rows), rows)]

    for j in range(QUARTERS):
        units.append((tall(j), gout, ou.at[pl.ds(j * rows, rows)]))
    for j in range(QUARTERS):
        units.append((whole(low), ginner.at[j], oi.at[:, pl.ds(j * d, d)]))
    units += [(whole(ctx), gattn, oo), (whole(x), dv, ov), (whole(x), dk, ok), (whole(x), dq, oq)]
    n = len(units)
    core_slots, acc_slots, z_slots = from_core.shape[0], acc.shape[0], zsum.shape[0]

    def load(src, dst, i):
        return pltpu.make_async_copy(src, dst, i_sem.at[i])

    pieces = []
    for j in range(QUARTERS):
        pieces += [wu.at[pl.ds(j * d, d)], wi.at[:, pl.ds(j * d, d)]]
    pieces += [wo, wq, wk, wv]

    def w_load(i):
        return pltpu.make_async_copy(pieces[i], w_in.at[i % 3], w_sem.at[i % 3])

    def core_all(u):
        return send(from_core.at[u % core_slots], from_core.at[u % core_slots], cs.at[u], cr.at[u], me.at_c)

    def half_x(u):
        a = acc.at[u % acc_slots, me.chip_d, pl.ds(0, rows // 2)]
        return send(a, half.at[u, 0], hs.at[u, 0], hr.at[u, 0], me.at_x)

    def half_y(u):
        a = acc.at[u % acc_slots, me.chip_d, pl.ds(rows // 2, rows // 2)]
        return send(a, half.at[u, 1], hs.at[u, 1], hr.at[u, 1], me.at_y)

    def plane_x(u):
        return send(acc.at[u % acc_slots, me.chip_x], plane.at[u, 0], ps.at[u, 0], pr.at[u, 0], me.at_x)

    def plane_y(u):
        return send(acc.at[u % acc_slots, me.chip_y], plane.at[u, 1], ps.at[u, 1], pr.at[u, 1], me.at_y)

    end = (me.s == 0) | (me.s == 3)
    mid = (me.s == 1) | (me.s == 2)
    partner = me.along(me.s + 1 - 2 * lax.rem(me.s, 2))
    other = me.along(3 - me.s)

    def line_in(u):
        return send(zsum.at[u % z_slots], line.at[u, 0], zs.at[u, 0], zr.at[u, 0], partner)

    def line_swap(u):
        return send(zsum.at[u % z_slots], line.at[u, 1], zs.at[u, 0], zr.at[u, 1], other)

    def line_back(u):
        return send(ztot.at[u % z_slots], line.at[u, 0], zs.at[u, 1], zr.at[u, 0], partner)

    def out_mid(u):
        return pltpu.make_async_copy(ztot.at[u % z_slots], units[u][2], out_sem.at[u])

    def out_end(u):
        return pltpu.make_async_copy(line.at[u, 0], units[u][2], out_sem.at[u])

    def wide(a):
        return a.astype(F32)

    def produce(u):
        left, right, _ = units[u]
        slot = u % 2
        if u >= 2:
            core_all(u - 2).wait_send()
        if u >= core_slots:
            pl.semaphore_wait(credit, 1)

        def step(j, _):
            to_send[slot, j] = mm(left(2 * j + 1 - me.c), right[...], 0, 0).astype(BF)
            send(to_send.at[slot, j], from_core.at[u % core_slots, j], cs.at[u], cr.at[u], me.at_c).start()
            return 0

        lax.fori_loop(0, 4, step, 0)

        def keep(j, _):
            own[slot, j] = mm(left(2 * j + me.c), right[...], 0, 0).astype(BF)
            return 0

        lax.fori_loop(0, 4, keep, 0)

    def s1(u):
        if u >= acc_slots:
            sent_acc(u - acc_slots)
        core_all(u).wait_recv()
        slot = u % acc_slots

        def step(j, _):
            acc[slot, j] = (wide(own[u % 2, j]) + wide(from_core[u % core_slots, j])).astype(BF)
            return 0

        lax.fori_loop(0, 4, step, 0)
        half_x(u).start()
        half_y(u).start()
        if u + core_slots < n:
            pl.semaphore_signal(credit, inc=1, device_id=me.at_c, device_id_type=MESH)

    def s2(u):
        slot = u % acc_slots
        low_rows, high_rows = pl.ds(0, rows // 2), pl.ds(rows // 2, rows // 2)
        half_x(u).wait_recv()
        acc[slot, me.chip_y, low_rows] = (wide(acc[slot, me.chip_y, low_rows]) + wide(half[u, 0])).astype(BF)
        plane_y(u).start()
        half_y(u).wait_recv()
        acc[slot, me.chip_x, high_rows] = (wide(acc[slot, me.chip_x, high_rows]) + wide(half[u, 1])).astype(BF)
        plane_x(u).start()

    def s3(u):
        if u >= z_slots:
            pl.when(end)(lambda: line_in(u - z_slots).wait_send())
            pl.when(mid)(lambda: line_swap(u - z_slots).wait_send())
        plane_x(u).wait_recv()
        plane_y(u).wait_recv()
        zsum[u % z_slots] = (wide(acc[u % acc_slots, me.chip]) + wide(plane[u, 0]) + wide(plane[u, 1])).astype(BF)
        pl.when(end)(lambda: line_in(u).start())

    def z1(u):
        @pl.when(mid)
        def _():
            line_in(u).wait_recv()
            zsum[u % z_slots] = (wide(zsum[u % z_slots]) + wide(line[u, 0])).astype(BF)
            line_swap(u).start()

    def z2(u):
        @pl.when(mid)
        def _():
            if u >= z_slots:
                line_back(u - z_slots).wait_send()
                out_mid(u - z_slots).wait()
            line_swap(u).wait_recv()
            ztot[u % z_slots] = (wide(zsum[u % z_slots]) + wide(line[u, 1])).astype(BF)
            line_back(u).start()
            out_mid(u).start()

    def z3(u):
        @pl.when(end)
        def _():
            line_back(u).wait_recv()
            out_end(u).start()

    def sent_acc(u):
        half_x(u).wait_send()
        half_y(u).wait_send()
        plane_x(u).wait_send()
        plane_y(u).wait_send()

    def v_swap(i, to):
        return send(vbuf.at[i], vrecv.at[i], vs.at[i], vr.at[i], to)

    v_to = (me.at_c, me.at_x, me.at_y)

    def v_step(i):
        if i == 0:
            vbuf[0] = sums[...]
            v_swap(0, v_to[0]).start()
        elif i < 4:
            v_swap(i - 1, v_to[i - 1]).wait_recv()
            vbuf[i] = vbuf[i - 1] + vrecv[i - 1]
            if i < 3:
                v_swap(i, v_to[i]).start()
            else:
                pl.when(end)(lambda: v_swap(3, partner).start())
        elif i == 4:

            @pl.when(mid)
            def _():
                v_swap(3, partner).wait_recv()
                vbuf[4] = vbuf[3] + vrecv[3]
                v_swap(4, other).start()

        elif i == 5:

            @pl.when(mid)
            def _():
                v_swap(4, other).wait_recv()
                vbuf[5] = vbuf[4] + vrecv[4]
                v_swap(5, partner).start()
                vec_out[...] = vbuf[5]

        elif i == 6:

            @pl.when(end)
            def _():
                v_swap(5, partner).wait_recv()
                vec_out[...] = vrecv[5]

    def put(i, value, tile=slice(None)):
        sums[pl.ds(i, 1), tile] = jnp.sum(value, axis=0, keepdims=True)

    def inner_grad(quarter, slot):
        def step(j, _):
            tile = at_tile(j, TILE)
            y = mm(gout[...], w_in[slot, tile, :], 1, 1) * wide(slope[quarter, :, tile])
            y = y.astype(BF)
            ginner[quarter, :, tile] = y
            put(8 + quarter, wide(y), tile)
            return 0

        lax.fori_loop(0, d // TILE, step, 0)

    def first_grad(quarter, slot):
        def step(j, _):
            tile = at_tile(j, TILE)
            gfirst[:, tile] = gfirst[:, tile] + mm(ginner[quarter], w_in[slot, tile, :], 1, 1)
            return 0

        lax.fori_loop(0, d // TILE, step, 0)

    def first_norm_back():
        gain = vecs[pl.ds(G1, 1), :]

        def step(j, carry):
            at = at_tile(j, ROW)
            g, centred = gfirst[at, :], n1[at, :]
            grad = norm_back(g * gain, centred, scale1[at, :1])
            gfirst[at, :] = grad
            rounded = grad.astype(BF)
            gattn[at, :] = rounded
            return carry[0] + eighths(g * centred), carry[1] + eighths(g), carry[2] + eighths(wide(rounded))

        zero = jnp.zeros((8, d), F32)
        gains, shifts, biases = lax.fori_loop(0, length // ROW, step, (zero, zero, zero))
        put(4, gains)
        put(5, shifts)
        put(2, biases)

    def context_grad(slot):
        def step(j, _):
            tile = at_tile(j, TILE)
            gctx[:, tile] = mm(gattn[...], w_in[slot, tile, :], 1, 1).astype(BF)
            return 0

        lax.fori_loop(0, d // TILE, step, 0)

    def p_load(pair, h, slot):
        return pltpu.make_async_copy(p_in.at[2 * pair + h], probs.at[slot, h], p_sem.at[slot, h])

    def attend_back(first, last):
        pairs = d // LANES

        def step(pair, _):
            slot = lax.rem(pair, 2)

            @pl.when(pair + 1 < pairs)
            def _():
                for h in range(2):
                    p_load(pair + 1, h, 1 - slot).start()

            masks = half_masks()
            at = at_tile(pair, LANES)
            qp, kp, vp, gp = q[:, at], k[:, at], v[:, at], gctx[:, at]
            outs = None
            for h in range(2):
                p_load(pair, h, slot).wait()
                p = wide(probs[slot, h])
                g = mm(gp * masks[h].astype(BF), vp, 1, 1)
                w = p * g
                s = (w - p * jnp.sum(w, axis=1, keepdims=True)).astype(BF)
                got = (
                    mm(s, kp) * (masks[h] * (1.0 / math.sqrt(HD))),
                    mm(s, qp, 0, 0) * masks[h],
                    mm(probs[slot, h], gp, 0, 0) * masks[h],
                )
                outs = got if outs is None else tuple(a + b for a, b in zip(outs, got))
            for ref, y, i in ((dq, outs[0], 0), (dk, outs[1], None), (dv, outs[2], 1)):
                y = y.astype(BF)
                ref[:, at] = y
                if i is not None:
                    put(i, wide(y), at)
            return 0

        lax.fori_loop(first, last, step, 0)

    def token_grad():
        def step(j, _):
            tile = at_tile(j, TILE)
            y = gfirst[:, tile]
            for ref, i in ((dq, 9), (dk, 10), (dv, 11)):
                y = y + mm(ref[...], w_in[i % 3, tile, :], 1, 1)
            gtok[:, tile] = y.astype(BF)
            return 0

        lax.fori_loop(0, d // TILE, step, 0)

    for quarter in range(QUARTERS):
        load(hid_in.at[quarter], hidden.at[quarter], quarter).start()
    load(gout_in, gout, 4).start()
    w_load(0).start()
    load(slope_in, slope, 5).start()
    w_load(1).start()
    load(gsec_in, gfirst, 6).start()
    later = ((low_in, low, 7), (n1_in, n1, 8), (scale_in, scale1, 9), (vec_in, vecs, 10), (part_in, part, 11))
    for src, dst, i in later:
        load(src, dst, i).start()
    greet(me)
    lay_back = Exchange(me, lay_in, lay_out, a_sems, 0, True)
    tok_back = Exchange(me, gtok, gtok_out, a_sems, 1, True)
    for quarter in range(QUARTERS):
        load(hid_in.at[quarter], hidden.at[quarter], quarter).wait()
    load(gout_in, gout, 4).wait()
    produce(0)
    sums[...] = jnp.zeros_like(sums)

    def work(tick):
        if tick < QUARTERS:
            if tick == 0:
                load(slope_in, slope, 5).wait()
                load(gsec_in, gfirst, 6).wait()
                load(low_in, low, 7).wait()
            w_load(2 * tick + 2).start()
            w_load(2 * tick).wait()
            inner_grad(tick, (2 * tick) % 3)
            w_load(2 * tick + 3).start()
            w_load(2 * tick + 1).wait()
            first_grad(tick, (2 * tick + 1) % 3)
        if tick == 3:
            for src, dst, i in ((q_in, q, 0), (k_in, k, 1), (v_in, v, 2)):
                for pair in range(d // LANES):
                    load(src.at[pair], dst.at[:, pl.ds(pair * LANES, LANES)], i).start()
            load(x_in, x, 3).start()
            load(ctx_in, ctx, 5).start()
            for h in range(2):
                p_load(0, h, 0).start()
        if tick == 4:
            for src, dst, i in later[1:]:
                load(src, dst, i).wait()
            first_norm_back()
            w_load(8).wait()
            context_grad(8 % 3)
            w_load(10).start()
            w_load(11).start()
            for i in range(3):
                load(x_in, dst_whole(i), i).wait()
            load(x_in, x, 3).wait()
            load(ctx_in, ctx, 5).wait()
            attend_back(0, 1)
        if tick == 5:
            attend_back(1, 4)
        if tick == 6:
            attend_back(4, 6)
        if tick == 7:
            attend_back(6, 8)
            for row, i in ((0, 6), (1, 7), (2, 3)):
                sums[pl.ds(i, 1), :] = part[pl.ds(row, 1), :]
        if tick == 8:
            for i in (9, 10, 11):
                w_load(i).wait()
            token_grad()

    def dst_whole(i):
        return (q, k, v)[i]

    stages = (s1, s2, s3, z1, z2, z3)
    for tick in range(n + len(stages) - 1):
        if tick + 1 < n:
            produce(tick + 1)
        for back, stage in enumerate(stages):
            if 0 <= tick - back < n:
                stage(tick - back)
        if tick < 3:
            lay_back.start((2, 3, 1)[tick])
        work(tick)
        if 8 <= tick < 11:
            tok_back.start((2, 3, 1)[tick - 8])
        if 8 <= tick < 15:
            v_step(tick - 8)
    for u in range(n - 2, n):
        core_all(u).wait_send()
    for u in range(n - acc_slots, n):
        sent_acc(u)
    for u in range(n):
        pl.when(end)(lambda: out_end(u).wait())
    for u in range(n - z_slots, n):
        pl.when(end)(lambda: line_in(u).wait_send())

        @pl.when(mid)
        def _():
            line_swap(u).wait_send()
            line_back(u).wait_send()
            out_mid(u).wait()

    for i in range(3):
        v_swap(i, v_to[i]).wait_send()
    pl.when(end)(lambda: v_swap(3, partner).wait_send())

    @pl.when(mid)
    def _():
        v_swap(4, other).wait_send()
        v_swap(5, partner).wait_send()

    for exchange in (lay_back, tok_back):
        exchange.wait()
        exchange.sent()


def backward_all(saved, block):
    length, d = saved[0].shape
    rows = d // RING
    n = UNITS
    core_slots, acc_slots, z_slots = 3, 3, 3
    dma = pltpu.SemaphoreType.DMA
    shape = jax.ShapeDtypeStruct

    def vm(*s, dtype=BF):
        return pltpu.VMEM(s, dtype)

    split = shape((LINE, block, d), BF)
    sq = shape((rows, d), BF)
    sums = (16, d)
    outs = [split, split, sq, sq, sq, sq, shape((rows, QUARTERS * d), BF), shape((QUARTERS * rows, d), BF), shape(sums, F32)]
    mat = (length, d)
    mlp = (QUARTERS, length, d)
    return pl.pallas_call(
        backward_kernel,
        out_shape=outs,
        in_specs=[ANY] * len(saved),
        out_specs=[ANY] * 8 + [pl.BlockSpec(memory_space=pltpu.VMEM)],
        scratch_shapes=[
            vm(core_slots, 4, rows, d), vm(n, 2, rows // 2, d), vm(n, 2, rows, d), vm(n, 2, rows, d),
            vm(2, 4, rows, d), vm(2, 4, rows, d), vm(acc_slots, 4, rows, d), vm(z_slots, rows, d), vm(z_slots, rows, d),
            vm(6, *sums, dtype=F32), vm(6, *sums, dtype=F32),
            vm(*mlp), vm(*mat), vm(*mlp), vm(*mlp), vm(*mat, dtype=F32), vm(*mat, dtype=F32), vm(length, LANES, dtype=F32), vm(*mat),
            vm(*mat), vm(*mat), vm(2, 2, length, length), vm(3, d, d), vm(24, d, dtype=F32), vm(8, d, dtype=F32), vm(*sums, dtype=F32),
            pltpu.SemaphoreType.REGULAR,
            dma((n,)), dma((n,)), dma((n, 2)), dma((n, 2)), dma((n, 2)), dma((n, 2)), dma((n, 2)), dma((n, 2)),
            dma((n,)), dma((6,)), dma((6,)), dma((2, 4)), dma((2, 4)), dma((2,)), dma((12,)), dma((3,)), dma((2, 2)),
        ],
        compiler_params=pltpu.CompilerParams(collective_id=1, has_side_effects=True, vmem_limit_bytes=62 << 20),
        name="backward",
    )(*saved)


def local(tokens, labels, *rest):
    weights, vectors, cotangent = rest[:6], rest[6:15], rest[15]
    groups = lax.axis_size("grp") // RING
    g, s = lax.axis_index("grp"), lax.axis_index("seq")
    lo = lax.rem(g, RING)
    if groups > 1:
        def regroup(w):
            full = lax.all_gather(w, ("grp", "seq"), axis=0, tiled=True)
            n = full.shape[0] // (RING * LINE)
            return lax.dynamic_slice_in_dim(full, (lo * LINE + s) * n, n, 0)

        weights = tuple(regroup(w) for w in weights)
        vectors = tuple(regroup(v) for v in vectors)
    packed = [jnp.pad(v, (0, LANES - v.shape[0]))[None] for v in vectors]
    packed = jnp.concatenate(packed + [jnp.zeros((16 - len(vectors), LANES), BF)], axis=0)
    own_labels = lax.dynamic_index_in_dim(labels, s, 0, keepdims=False)
    marks = jnp.where(own_labels != 0, own_labels, -1 - jnp.arange(own_labels.shape[0])).astype(F32)
    saved = forward_all(tokens, cotangent, marks[None, :], marks[:, None], packed, weights)
    out = backward_all(saved, tokens.shape[1])
    layer_out, grad_tokens = out[:2]
    mats = [m.astype(F32) for m in out[2:8]]
    vec = out[8]
    flat = [vec[i] for i in range(8)]
    flat.insert(3, vec[8 : 8 + QUARTERS].reshape(-1))
    if groups > 1:
        same = [[l + RING * h for h in range(groups)] for l in range(RING)]
        eight = [[l + RING * h for l in range(RING)] for h in range(groups)]

        def rejoin(m):
            m = lax.psum(m, "grp", axis_index_groups=same)
            m = lax.all_gather(m, "grp", axis=0, tiled=True, axis_index_groups=eight)
            n = m.shape[0] // (RING * groups)
            return lax.dynamic_slice_in_dim(m, g * n, n, 0)

        mats = [rejoin(m) for m in mats]
        flat = [lax.psum(v, "grp", axis_index_groups=same) for v in flat]
    flat = [lax.dynamic_slice_in_dim(v, g * (v.shape[0] // (RING * groups)), v.shape[0] // (RING * groups), 0) for v in flat]
    return (layer_out, grad_tokens, *mats, *flat)


def solution(mesh):
    both = ("grp", "seq")
    rows = P("grp", "seq", None)
    return jax.shard_map(
        local,
        mesh=mesh,
        in_specs=(rows, P("grp", None)) + (P(both, None),) * 6 + (P(both),) * 9 + (rows,),
        out_specs=(rows, rows) + (P("grp", None),) * 6 + (P("grp"),) * 9,
        check_vma=False,
    )
```

```python
import functools
import math

import jax
import jax.numpy as jnp
from jax import lax
from jax.experimental import pallas as pl
from jax.experimental.pallas import tpu as pltpu
from jax.sharding import PartitionSpec as P

H = 16
HD = 64
LINE = 4
RING = 8
UNITS = 12
QUARTERS = 4
LANES = 128
MESH = pl.DeviceIdType.MESH
BF = jnp.bfloat16
F32 = jnp.float32
ANY = pl.BlockSpec(memory_space=pl.ANY)


class Place:
    def __init__(self):
        self.g = lax.axis_index("grp")
        self.s = lax.axis_index("seq")
        self.lo = lax.rem(self.g, RING)
        self.c = lax.rem(self.lo, 2)
        xb = lax.rem(self.lo // 2, 2)
        yb = self.lo // 4
        self.dc, self.dx, self.dy = 1 - 2 * self.c, 2 - 4 * xb, 4 - 8 * yb
        self.at_c = (self.g + self.dc, self.s)
        self.at_x = (self.g + self.dx, self.s)
        self.at_y = (self.g + self.dy, self.s)
        self.chip = self.lo // 2
        self.chip_x = self.chip + 1 - 2 * xb
        self.chip_y = self.chip + 2 - 4 * yb
        self.chip_d = self.chip_x + 2 - 4 * yb

    def along(self, t):
        return (self.g, t)


def send(src, dst, send_sem, recv_sem, to):
    return pltpu.make_async_remote_copy(
        src_ref=src, dst_ref=dst, send_sem=send_sem, recv_sem=recv_sem, device_id=to, device_id_type=MESH
    )


def greet(me):
    barrier = pltpu.get_barrier_semaphore()

    def signal(to):
        pl.semaphore_signal(barrier, inc=1, device_id=to, device_id_type=MESH)

    for to in (me.at_c, me.at_x, me.at_y):
        signal(to)
    for t in range(LINE):
        pl.when(me.s != t)(lambda t=t: signal(me.along(t)))
    pl.semaphore_wait(barrier, 3 + LINE - 1)


class Exchange:
    def __init__(self, me, whole, split, sems, index, back):
        self.me, self.whole, self.split, self.index, self.back = me, whole, split, index, back
        self.send_sem, self.recv_sem, self.local_sem = sems

    def rows(self, t, part=0, parts=1):
        n = self.split.shape[1]
        return self.whole.at[pl.ds(t * n + part * (n // parts), n // parts)]

    def ends(self, t, part=0, parts=1):
        n = self.split.shape[1] // parts
        here = pl.ds(part * n, n)
        if self.back:
            return self.rows(t, part, parts), self.split.at[self.me.s, here]
        return self.split.at[t, here], self.rows(self.me.s, part, parts)

    def copy(self, t, part=0, parts=1):
        src, dst = self.ends(t, part, parts)
        return send(src, dst, self.send_sem.at[self.index, t], self.recv_sem.at[self.index, self.me.s], self.me.along(t))

    def landed(self, t):
        dst = self.split.at[t] if self.back else self.rows(t)
        return send(dst, dst, self.send_sem.at[self.index, t], self.recv_sem.at[self.index, t], self.me.along(t))

    def own(self):
        src, dst = self.ends(self.me.s)
        return pltpu.make_async_copy(src, dst, self.local_sem.at[self.index])

    def start(self, distance, part=0, parts=1):
        s = self.me.s
        if distance == 1 and part == 0:
            self.own().start()
        for t in range(LINE):
            pl.when((s - t == distance) | (t - s == distance))(lambda t=t: self.copy(t, part, parts).start())

    def wait(self):
        self.own().wait()
        for t in range(LINE):
            pl.when(self.me.s != t)(lambda t=t: self.landed(t).wait_recv())

    def sent(self):
        for t in range(LINE):
            pl.when(self.me.s != t)(lambda t=t: self.copy(t).wait_send())


class Gather:
    def __init__(self, me, src, dst, rows, sems, u, fine):
        self.me, self.src, self.dst, self.rows, self.u, self.fine = me, src, dst, rows, u, fine
        self.local, self.zs, self.zr, self.xs, self.xr, self.cs, self.cr = sems

    def own(self):
        me = self.me
        return pltpu.make_async_copy(self.src, self.dst((me.lo * LINE + me.s) * self.rows, self.rows), self.local.at[self.u])

    def shard(self, source):
        return self.dst((self.me.lo * LINE + source) * self.rows, self.rows)

    def z_send(self, source, step, slot):
        there = self.shard(source)
        src = self.src if slot < 2 else there
        return send(src, there, self.zs.at[self.u, slot], self.zr.at[self.u, source], self.me.along(self.me.s + step))

    def z_recv(self, source):
        there = self.shard(source)
        send(there, there, self.zs.at[self.u, 0], self.zr.at[self.u, source], self.me.at_c).wait_recv()

    def xy_shard(self, source, own):
        there = self.shard(source)
        for k, to in ((0, self.me.at_x), (1, self.me.at_y)):
            send(self.src if own else there, there, self.xs.at[self.u, k], self.xr.at[self.u, k], to).start()

    def start(self):
        me = self.me
        self.own().start()
        pl.when(me.s < LINE - 1)(lambda: self.z_send(me.s, 1, 0).start())
        pl.when(me.s > 0)(lambda: self.z_send(me.s, -1, 1).start())
        if self.fine:
            self.xy_shard(me.s, True)

    def hop(self, h):
        me = self.me

        @pl.when(me.s >= h)
        def _():
            self.z_recv(me.s - h)
            if h < LINE - 1:
                pl.when(me.s < LINE - 1)(lambda: self.z_send(me.s - h, 1, 2 * h).start())
            if self.fine:
                self.xy_shard(me.s - h, False)

        @pl.when(me.s < LINE - h)
        def _():
            self.z_recv(me.s + h)
            if h < LINE - 1:
                pl.when(me.s > 0)(lambda: self.z_send(me.s + h, -1, 2 * h + 1).start())
            if self.fine:
                self.xy_shard(me.s + h, False)

    def block(self, lo, half=None):
        rows = self.rows * LINE
        if half is None:
            return self.dst(lo * rows, rows)
        return self.dst(lo * rows + half * (rows // 2), rows // 2)

    def x1(self, lo):
        return send(self.block(lo), self.block(lo), self.xs.at[self.u, 0], self.xr.at[self.u, 0], self.me.at_x)

    def y1(self, lo):
        return send(self.block(lo), self.block(lo), self.xs.at[self.u, 1], self.xr.at[self.u, 1], self.me.at_y)

    def x2(self, lo):
        return send(self.block(lo, 1), self.block(lo, 1), self.xs.at[self.u, 2], self.xr.at[self.u, 2], self.me.at_x)

    def y2(self, lo):
        return send(self.block(lo, 0), self.block(lo, 0), self.xs.at[self.u, 3], self.xr.at[self.u, 3], self.me.at_y)

    def core(self, lo, k):
        return send(self.block(lo), self.block(lo), self.cs.at[self.u, k], self.cr.at[self.u, k], self.me.at_c)

    def spread(self):
        me = self.me
        self.own().wait()
        if not self.fine:
            self.x1(me.lo).start()
            self.y1(me.lo).start()
        self.core(me.lo, 0).start()

    def cross(self):
        me = self.me
        lo_x, lo_y = me.lo + me.dx, me.lo + me.dy
        self.x1(lo_x).wait_recv()
        self.y2(lo_x).start()
        self.core(lo_x, 1).start()
        self.y1(lo_y).wait_recv()
        self.x2(lo_y).start()
        self.core(lo_y, 2).start()

    def corner(self):
        me = self.me
        lo_d = me.lo + me.dx + me.dy
        self.x2(lo_d).wait_recv()
        self.y2(lo_d).wait_recv()
        self.core(lo_d, 3).start()

    def whole(self):
        me = self.me
        for k, lo in enumerate((me.lo, me.lo + me.dx, me.lo + me.dy, me.lo + me.dx + me.dy)):
            self.core(lo + me.dc, k).wait_recv()

    def sent(self):
        me = self.me
        for h in range(LINE - 1):
            right = (me.s >= h) & (me.s < LINE - 1)
            left = (me.s < LINE - h) & (me.s > 0)
            pl.when(right)(lambda h=h: self.z_send(me.s - h, 1, 2 * h).wait_send())
            pl.when(left)(lambda h=h: self.z_send(me.s + h, -1, 2 * h + 1).wait_send())
        self.x1(me.lo).wait_send()
        self.y1(me.lo).wait_send()
        self.x2(me.lo + me.dy).wait_send()
        self.y2(me.lo + me.dx).wait_send()
        for k, lo in enumerate((me.lo, me.lo + me.dx, me.lo + me.dy, me.lo + me.dx + me.dy)):
            self.core(lo, k).wait_send()


def rows_of(ref, columns=None):
    if columns is None:
        return lambda row, n: ref.at[pl.ds(row, n)]
    return lambda row, n: ref.at[pl.ds(row, n), columns]


def rows_of(ref, columns=None):
    if columns is None:
        return lambda row, n: ref.at[pl.ds(row, n)]
    return lambda row, n: ref.at[pl.ds(row, n), columns]


def mm(a, b, ca=1, cb=0):
    return lax.dot_general(a, b, (((ca,), (cb,)), ((), ())), preferred_element_type=F32)


def at_tile(j, tile):
    if isinstance(j, int):
        return pl.ds(j * tile, tile)
    return pl.ds(pl.multiple_of(j * tile, tile), tile)


def steps(first, last, step, carry=0):
    for j in range(first, last):
        carry = step(j, carry)
    return carry


def iota(shape, dim):
    return lax.broadcasted_iota(jnp.int32, shape, dim)


def half_masks():
    low = (iota((1, LANES), 1) < HD).astype(F32)
    return low, 1.0 - low


def gelu_parts(u):
    t = 1.0 / (1.0 + (0.3275911 * 0.7071067811865476) * jnp.abs(u))
    poly = t * (0.254829592 + t * (-0.284496736 + t * (1.421413741 + t * (-1.453152027 + t * 1.061405429))))
    bell = jnp.exp(-0.5 * u * u)
    tail = 0.5 * poly * bell
    cdf = jnp.where(u >= 0.0, 1.0 - tail, tail)
    return u * cdf, cdf + u * (bell * 0.3989422804014327)


def stats(r):
    centered = r - jnp.mean(r, axis=-1, keepdims=True)
    scale = lax.rsqrt(jnp.mean(centered * centered, axis=-1, keepdims=True) + 1e-06)
    return centered * scale, scale


def norm_back(u, n, scale):
    return (u - jnp.mean(u, axis=-1, keepdims=True) - n * jnp.mean(u * n, axis=-1, keepdims=True)) * scale


def eighths(x):
    return jnp.sum(x.reshape(x.shape[0] // 8, 8, x.shape[1]), axis=0)


FINE = (0, 2, 3)
OUTER_PARTS = (1, 1, 1, 2)
FORWARD_ORDER = (
    ("ST", 0), ("ST", 1), ("ST", 2), ("ST", 3), ("ST", 4), ("R", 0, 1), ("R", 1, 1), ("R", 2, 1), ("R", 3, 1), ("R", 4, 1), ("R", 0, 2),
    ("R", 1, 2), ("R", 2, 2), ("R", 3, 2), ("R", 4, 2), ("R", 0, 3), ("SP", 0), ("R", 1, 3), ("SP", 1), ("R", 2, 3), ("SP", 2),
    ("R", 3, 3), ("CX", 0), ("SP", 3), ("CX", 1), ("ST", 5), ("ST", 6), ("CX", 2), ("R", 4, 3), ("SP", 4), ("ST", 7), ("CX", 3),
    ("ST", 8), ("R", 5, 1), ("CO", 0), ("CO", 1), ("R", 6, 1), ("WH", 0), ("CO", 2), ("WH", 1), ("R", 7, 1), ("WH", 2), ("UN",),
    ("R", 8, 1), ("R", 5, 2), ("R", 6, 2), ("TK", 2, 0, 4), ("CX", 4), ("R", 7, 2), ("TK", 3, 0, 4), ("R", 8, 2), ("CO", 3),
    ("R", 5, 3), ("SP", 5), ("TK", 1, 0, 4), ("WH", 3), ("R", 6, 3), ("SP", 6), ("TK", 2, 1, 4), ("CO", 4), ("TK", 3, 1, 4), ("WH", 4),
    ("TK", 1, 1, 4), ("R", 7, 3), ("SP", 7), ("TK", 2, 2, 4), ("CX", 5), ("TK", 3, 2, 4), ("R", 8, 3), ("SP", 8), ("TK", 1, 2, 4),
    ("TK", 2, 3, 4), ("CX", 6), ("TK", 3, 3, 4), ("TK", 1, 3, 4), ("CX", 7), ("ST", 9), ("CO", 5), ("ST", 10), ("ST", 11), ("WH", 5),
    ("ST", 12), ("QP", 0), ("R", 9, 1), ("QP", 1), ("CX", 8), ("R", 10, 1), ("R", 11, 1), ("QP", 2), ("R", 12, 1), ("CO", 6), ("AT", 0),
    ("R", 9, 2), ("R", 10, 2), ("WH", 6), ("AT", 1), ("R", 11, 2), ("CO", 7), ("AT", 2), ("R", 12, 2), ("CO", 8), ("R", 9, 3),
    ("SP", 9), ("WH", 7), ("AT", 3), ("R", 10, 3), ("SP", 10), ("WH", 8), ("ST", 13), ("AT", 4), ("R", 11, 3), ("SP", 11), ("R", 12, 3),
    ("SP", 12), ("AT", 5), ("R", 13, 1), ("AT", 6), ("CX", 9), ("ST", 14), ("SD", 2, 0, 4), ("AT", 7), ("R", 13, 2), ("SD", 3, 0, 4),
    ("F0",), ("R", 14, 1), ("FN",), ("CX", 10), ("SD", 1, 0, 4), ("SD", 2, 1, 4), ("IN", 0, 0), ("SD", 3, 1, 4), ("IN", 0, 1),
    ("R", 13, 3), ("SP", 13), ("SD", 1, 1, 4), ("CX", 11), ("SD", 2, 2, 4), ("IN", 1, 0), ("R", 14, 2), ("IN", 1, 1), ("SD", 3, 2, 4),
    ("IN", 2, 0), ("CX", 12), ("SD", 1, 2, 4), ("SD", 2, 3, 4), ("IN", 2, 1), ("CO", 9), ("SD", 3, 3, 4), ("SD", 1, 3, 4), ("WH", 9),
    ("R", 14, 3), ("SP", 14), ("CO", 10), ("IN", 3, 0), ("WH", 10), ("IN", 3, 1), ("CX", 13), ("OU", 0), ("CO", 11), ("WH", 11),
    ("CO", 12), ("OU", 1), ("CX", 14), ("WH", 12), ("CO", 13), ("OU", 2), ("CO", 14), ("WH", 13), ("WH", 14), ("OU", 3), ("OU", 4),
    ("N2",),
)
BACK_PARTS = (1, 1, 1, 1, 1, 1, 1, 1, 1, 1, 1, 1)
BACK_ORDER = (
    ("LO", 2, 0, 4), ("LO", 2, 1, 4), ("LO", 2, 2, 4), ("P", 0), ("P", 1), ("IG", 0), ("S1", 0), ("FG", 0), ("S1", 1), ("LO", 2, 3, 4),
    ("IG", 1), ("LO", 3, 0, 4), ("P", 2), ("S2", 0), ("LO", 3, 1, 4), ("FG", 1), ("LO", 3, 2, 4), ("IG", 2), ("S2", 1), ("S1", 2),
    ("LO", 3, 3, 4), ("LO", 1, 0, 4), ("FG", 2), ("LO", 1, 1, 4), ("IG", 3), ("LO", 1, 2, 4), ("S3", 0), ("FG", 3), ("P", 3),
    ("LO", 1, 3, 4), ("LD",), ("NB",), ("P", 4), ("S1", 3), ("S3", 1), ("CG",), ("S2", 2), ("LW",), ("AB", 0), ("S1", 4), ("S2", 3),
    ("Z1", 0), ("AB", 1), ("AB", 2), ("AB", 3), ("S3", 2), ("Z1", 1), ("AB", 4), ("Z2", 0), ("S2", 4), ("AB", 5), ("AB", 6), ("AB", 7),
    ("S3", 3), ("Z1", 2), ("Z2", 1), ("V", 0), ("TW",), ("TG", 0), ("Z3", 0), ("P", 5), ("P", 6), ("S3", 4), ("V", 1), ("TG", 1),
    ("S1", 5), ("Z1", 3), ("Z2", 2), ("Z3", 1), ("TG", 2), ("S1", 6), ("V", 2), ("TG", 3), ("GT", 2, 0, 4), ("GT", 3, 0, 4),
    ("GT", 1, 0, 4), ("P", 7), ("S2", 5), ("Z1", 4), ("V", 3), ("P", 8), ("S2", 6), ("Z2", 3), ("S1", 7), ("Z3", 2), ("P", 9), ("V", 4),
    ("GT", 2, 1, 4), ("GT", 3, 1, 4), ("S3", 5), ("S1", 8), ("P", 10), ("V", 5), ("GT", 1, 1, 4), ("GT", 2, 2, 4), ("GT", 3, 2, 4),
    ("Z2", 4), ("S3", 6), ("S1", 9), ("V", 6), ("P", 11), ("S2", 7), ("Z1", 5), ("Z3", 3), ("S2", 8), ("GT", 1, 2, 4), ("GT", 2, 3, 4),
    ("S2", 9), ("GT", 3, 3, 4), ("GT", 1, 3, 4), ("Z1", 6), ("S3", 7), ("S1", 10), ("Z2", 5), ("Z3", 4), ("S3", 8), ("S1", 11),
    ("Z1", 7), ("S2", 10), ("Z2", 6), ("S3", 9), ("Z1", 8), ("Z3", 5), ("S2", 11), ("Z2", 7), ("Z3", 6), ("Z1", 9), ("S3", 10),
    ("Z2", 8), ("Z3", 7), ("S3", 11), ("Z1", 10), ("Z2", 9), ("Z3", 8), ("Z1", 11), ("Z2", 10), ("Z3", 9), ("Z2", 11), ("Z3", 10),
    ("Z3", 11),
)
ROW = 64
TILE = 256
BQ, BV, BO, BI, BU, G1, S1, G2, S2 = range(9)
INNER = 16


def forward_kernel(
    tok, cot, labels, vec, wq, wk, wv, wo, wi, wu,
    x_out, wq_all, wk_all, wv_all, wo_all, wi_all, wu_all, q_out, k_out, v_out, p_out, ctx_out, low_out,
    n1_out, scale_out, hid_out, slope_out, gsec_out, gout_out, lay_out, vec_out, part_out,
    x, seed, packed, vecs, part, w_in, wu_in, q, k, v, bias, probs, ctx, n1, scale1, low, hidden, slope, res, gsec, gout, lay,
    local, zs, zr, xs, xr, cs, cr, a_send, a_recv, a_local, w_sem, p_sem, o_sem,
):
    me = Place()
    sems = (local, zs, zr, xs, xr, cs, cr)
    a_sems = (a_send, a_recv, a_local)
    d = x.shape[1]
    length = x.shape[0]
    units, pieces = [], []

    def add(src, ref, columns, to=None):
        src = src if columns is None else src.at[:, columns]
        u = len(units)
        units.append(Gather(me, src, rows_of(ref, columns), src.shape[0], sems, u, u in FINE))
        pieces.append(None if to is None else pltpu.make_async_copy(ref if columns is None else ref.at[:, columns], to, w_sem.at[u]))

    add(wq, wq_all, pl.ds(0, d // 2), w_in.at[0, :, pl.ds(0, d // 2)])
    add(vec, packed, None)
    add(wq, wq_all, pl.ds(d // 2, d // 2), w_in.at[0, :, pl.ds(d // 2, d // 2)])
    for i, (src, ref) in enumerate(((wk, wk_all), (wv, wv_all), (wo, wo_all))):
        add(src, ref, None, w_in.at[1 + i])
    width = wi.shape[1] // QUARTERS
    for j in range(QUARTERS):
        add(wi, wi_all, pl.ds(j * width, width), w_in.at[4 + j])
    outer_at = []
    for j, parts in enumerate(OUTER_PARTS):
        width = d // QUARTERS // parts
        for i in range(parts):
            add(wu, wu_all, pl.ds(j * TILE + i * width, width), wu_in.at[j, :, pl.ds(i * width, width)])
            outer_at.append((j, i * width, width))
    n = len(units)
    saves = []

    def save(src, dst):
        copy = pltpu.make_async_copy(src, dst, o_sem.at[len(saves)])
        copy.start()
        saves.append(copy)

    def row(i):
        return vecs[pl.ds(i, 1), :]

    def unpack():
        p = packed[...]
        piece = d // (RING * LINE)
        spread = (iota((LANES, d), 1) % piece == iota((LANES, d), 0)).astype(BF)
        wide = mm(p, spread).reshape(RING * LINE, 16, d)
        here = iota((RING * LINE, 1, d), 0) == iota((RING * LINE, 1, d), 2) // piece
        vecs[pl.ds(0, 16), :] = jnp.sum(jnp.where(here, wide, 0.0), axis=0)
        p = p.astype(F32).reshape(RING * LINE, 16, LANES)
        p = jnp.sum(jnp.where(iota(p.shape, 1) == BI, p, 0.0), axis=1).astype(BF)
        spread = (iota((LANES, d), 1) % LANES == iota((LANES, d), 0)).astype(BF)
        per = RING * LINE // QUARTERS
        wide = mm(p, spread).reshape(QUARTERS, per, d)
        here = iota((1, per, d), 1) == iota((1, per, d), 2) // LANES
        inner = jnp.sum(jnp.where(here, wide, 0.0), axis=1)
        vecs[pl.ds(INNER, 8), :] = jnp.concatenate([inner, jnp.zeros_like(inner)], axis=0)

    def mask():
        own = labels[pl.ds(me.s, 1), :]
        marks = jnp.where(own != 0, own, -1 - iota(own.shape, 1)).astype(F32)
        down = jnp.broadcast_to(marks, (LANES, length)).T[:, :1]
        bias[...] = jnp.where(down == marks, 0.0, -1e30)

    def project(slot):
        out, b, factor = ((q, BQ, 1.0 / math.sqrt(HD)), (k, None, None), (v, BV, None))[slot]

        def step(j, _):
            tile = at_tile(j, TILE)
            y = mm(x[...], w_in[slot, :, tile])
            if b is not None:
                y = y + vecs[pl.ds(b, 1), tile]
            y = y.astype(BF)
            if factor is not None:
                y = (y.astype(F32) * factor).astype(BF)
            out[2 * j] = y[:, :LANES]
            out[2 * j + 1] = y[:, LANES:]
            return 0

        steps(0, d // TILE, step, 0)

    def p_save(h, slot):
        return pltpu.make_async_copy(probs.at[slot], p_out.at[h], p_sem.at[slot])

    def attend(pair):
        masks = half_masks()
        kp, vp, qp = k[pair], v[pair], q[pair]
        out = None
        for h in range(2):
            slot = (2 * pair + h) % 4
            if pair >= 2:
                p_save(2 * pair + h, slot).wait()
            scores = mm(qp * masks[h].astype(BF), kp, 1, 1) + bias[...]
            e = jnp.exp(scores - jnp.max(scores, axis=1, keepdims=True))
            p = (e * (1.0 / jnp.sum(e, axis=1, keepdims=True))).astype(BF)
            probs[slot] = p
            p_save(2 * pair + h, slot).start()
            term = mm(p, vp) * masks[h]
            out = term if out is None else out + term
        ctx[:, pl.ds(pair * LANES, LANES)] = out.astype(BF)

    def project_context():
        def step(j, _):
            tile = at_tile(j, TILE)
            y = mm(ctx[...], w_in[3, :, tile]) + vecs[pl.ds(BO, 1), tile]
            n1[:, tile] = y + x[:, tile].astype(F32)
            return 0

        steps(0, d // TILE, step, 0)

    def first_norm():
        def norm(j, _):
            rows = at_tile(j, ROW)
            centred, scale = stats(n1[rows, :])
            n1[rows, :] = centred
            scale1[rows, :] = jnp.broadcast_to(scale, (ROW, LANES))
            first = centred * row(G1) + row(S1)
            low[rows, :] = first.astype(BF)
            res[rows, :] = first + row(BU)
            return 0

        steps(0, length // ROW, norm, 0)

    def inner(quarter, part):
        half = d // TILE // 2

        def step(j, _):
            tile = at_tile(j, TILE)
            u = mm(low[...], w_in[4 + quarter, :, tile]) + vecs[pl.ds(INNER + quarter, 1), tile]
            act, grad = gelu_parts(u)
            hidden[quarter, :, tile] = act.astype(BF)
            slope[quarter, :, tile] = grad.astype(BF)
            return 0

        steps(part * half, (part + 1) * half, step, 0)

    def outer(i):
        j, offset, width = outer_at[i]
        tile = pl.ds(j * TILE + offset, width)
        y = res[:, tile]
        for quarter in range(QUARTERS):
            y = y + mm(hidden[quarter], wu_in[j, pl.ds(quarter * d, d), pl.ds(offset, width)])
        res[:, tile] = y

    def second_norm():
        def step(j, sums):
            rows = at_tile(j, ROW)
            centred, scale = stats(res[rows, :])
            lay[rows, :] = (centred * row(G2) + row(S2)).astype(BF)
            g = seed[rows, :].astype(F32)
            grad = norm_back(g * row(G2), centred, scale)
            gsec[rows, :] = grad
            rounded = grad.astype(BF)
            gout[rows, :] = rounded
            return sums[0] + eighths(g * centred), sums[1] + eighths(g), sums[2] + eighths(rounded.astype(F32))

        zero = jnp.zeros((8, d), F32)
        sums = steps(0, length // ROW, step, (zero, zero, zero))
        for i, s in enumerate(sums):
            part[pl.ds(i, 1), :] = jnp.sum(s, axis=0, keepdims=True)

    greet(me)
    tokens = Exchange(me, x, tok, a_sems, 0, False)
    seeds = Exchange(me, seed, cot, a_sems, 1, False)
    part[...] = jnp.zeros_like(part)
    mask()
    seen = set()

    def need(*us):
        for u in us:
            if u not in seen:
                seen.add(u)
                pieces[u].wait()

    for op, *at in FORWARD_ORDER:
        i = at[0] if at else 0
        if op == "ST":
            units[i].start()
        elif op == "R":
            units[i].hop(at[1])
        elif op == "SP":
            units[i].spread()
        elif op == "CX":
            units[i].cross()
        elif op == "CO":
            units[i].corner()
        elif op == "WH":
            units[i].whole()
            if pieces[i] is not None:
                pieces[i].start()
        elif op in ("TK", "SD"):
            (tokens if op == "TK" else seeds).start(*at)
        elif op == "UN":
            unpack()
            save(vecs, vec_out)
        elif op == "QP":
            if i == 0:
                tokens.wait()
                save(x, x_out)
                need(0, 2)
            else:
                need(2 + i)
            project(i)
            save((q, k, v)[i], (q_out, k_out, v_out)[i])
        elif op == "AT":
            attend(i)
            if i == 7:
                save(ctx, ctx_out)
        elif op == "F0":
            need(5)
            project_context()
        elif op == "FN":
            first_norm()
            for src, dst in ((n1, n1_out), (scale1, scale_out), (low, low_out)):
                save(src, dst)
        elif op == "IN":
            need(6 + i)
            inner(*at)
            if at == [QUARTERS - 1, 1]:
                save(hidden, hid_out)
                save(slope, slope_out)
        elif op == "OU":
            need(10 + i)
            outer(i)
        elif op == "N2":
            seeds.wait()
            second_norm()
            for src, dst in ((gsec, gsec_out), (gout, gout_out), (lay, lay_out), (part, part_out)):
                save(src, dst)
    for unit in units:
        unit.sent()
    tokens.sent()
    seeds.sent()
    for slot in range(4):
        p_save(12 + slot, slot).wait()
    for copy in saves:
        copy.wait()


def forward_all(tok, cot, labels, vec, weights):
    d = tok.shape[2]
    length = tok.shape[1] * LINE
    pairs = d // LANES
    quarter = weights[4].shape[1] // QUARTERS
    shape = jax.ShapeDtypeStruct
    bf, wide = shape((length, d), BF), shape((length, d), F32)
    heads = shape((pairs, length, LANES), BF)
    mlp = shape((QUARTERS, length, quarter), BF)
    outs = (
        [bf]
        + [shape((w.shape[0] * RING * LINE, w.shape[1]), BF) for w in weights]
        + [heads, heads, heads, shape((2 * pairs, length, length), BF), bf, bf]
        + [wide, shape((length, LANES), F32), mlp, mlp, wide, bf, bf, shape((24, d), F32), shape((8, d), F32)]
    )
    n = UNITS + 1 + 2
    dma = pltpu.SemaphoreType.DMA

    def vm(s):
        return pltpu.VMEM(s.shape, s.dtype)

    vmem = pl.BlockSpec(memory_space=pltpu.VMEM)
    return pl.pallas_call(
        forward_kernel,
        out_shape=outs,
        in_specs=[ANY, ANY, vmem] + [ANY] * 7,
        out_specs=[ANY] * len(outs),
        scratch_shapes=[
            vm(bf), vm(bf), pltpu.VMEM((vec.shape[0] * RING * LINE, LANES), BF), pltpu.VMEM((24, d), F32), pltpu.VMEM((8, d), F32),
            pltpu.VMEM((8, d, d), BF), pltpu.VMEM((QUARTERS, QUARTERS * quarter, d // QUARTERS), BF),
            vm(heads), vm(heads), vm(heads), pltpu.VMEM((length, length), F32), pltpu.VMEM((4, length, length), BF),
            vm(bf), vm(wide), pltpu.VMEM((length, LANES), F32), vm(bf), vm(mlp), vm(mlp), vm(wide), vm(wide), vm(bf), vm(bf),
            dma((n,)), dma((n, 6)), dma((n, 4)), dma((n, 4)), dma((n, 4)), dma((n, 4)), dma((n, 4)),
            dma((2, 4)), dma((2, 4)), dma((2,)), dma((n,)), dma((4,)), dma((16,)),
        ],
        compiler_params=pltpu.CompilerParams(collective_id=0, has_side_effects=True, vmem_limit_bytes=58 << 20),
        name="forward",
    )(tok, cot, labels, vec, *weights)


def backward_kernel(
    x_in, wq, wk, wv, wo, wi, wu, q_in, k_in, v_in, p_in, ctx_in, low_in,
    n1_in, scale_in, hid_in, slope_in, gsec_in, gout_in, lay_in, vec_in, part_in,
    lay_out, gtok_out, oq, ok, ov, oo, oi, ou, vec_out,
    from_core, half, plane, line, own, to_send, acc, zsum, ztot, vbuf, vrecv,
    hidden, gout, slope, ginner, gfirst, n1, scale1, low, dk, dv, probs, w_in, vecs, part, sums,
    credit, cs, cr, hs, hr, ps, pr, zs, zr, out_sem, vs, vr, a_send, a_recv, a_local, i_sem, w_sem, p_sem,
):
    me = Place()
    a_sems = (a_send, a_recv, a_local)
    length, d = gout.shape
    rows = d // RING
    q, k, v, x = hidden.at[0], hidden.at[1], hidden.at[2], hidden.at[3]
    gattn, gctx, ctx, gtok = slope.at[0], slope.at[1], slope.at[2], slope.at[3]
    dq = gout

    units = []

    def whole(ref):
        return lambda lo: ref[:, at_tile(lo, rows)]

    def tall(j):
        return lambda lo: hidden[lo // 2, :, pl.ds(pl.multiple_of(lax.rem(lo, 2) * (QUARTERS * rows) + j * rows, rows), rows)]

    for j in range(QUARTERS):
        units.append((tall(j), lambda at: gout[:, at], lambda o, w, j=j: ou.at[pl.ds(j * rows, rows), pl.ds(o, w)]))
    for j in range(QUARTERS):
        units.append((whole(low), lambda at, j=j: ginner[j, :, at], lambda o, w, j=j: oi.at[:, pl.ds(j * d + o, w)]))
    for left, right, out in ((ctx, gattn, oo), (x, dv, ov), (x, dk, ok), (x, dq, oq)):
        units.append((whole(left), lambda at, right=right: right[:, at], lambda o, w, out=out: out.at[:, pl.ds(o, w)]))
    parts, members = [], []
    for unit, count in enumerate(BACK_PARTS):
        members.append([])
        for i in range(count):
            members[unit].append(len(parts))
            parts.append((unit, i * (d // count), d // count))
    n = len(parts)

    def at_of(i):
        return pl.ds(parts[i][1], parts[i][2])

    def leads(i, slots):
        unit = parts[i][0]
        return members[unit - slots] if i == members[unit][0] and unit >= slots else ()

    core_slots, acc_slots, z_slots = from_core.shape[0], acc.shape[0], zsum.shape[0]

    def load(src, dst, i):
        return pltpu.make_async_copy(src, dst, i_sem.at[i])

    pieces = []
    for j in range(QUARTERS):
        pieces += [wu.at[pl.ds(j * d, d)], wi.at[:, pl.ds(j * d, d)]]
    pieces += [wo, wq, wk, wv]

    def w_load(i):
        return pltpu.make_async_copy(pieces[i], w_in.at[i % 3], w_sem.at[i % 3])

    def core_all(i):
        here = from_core.at[parts[i][0] % core_slots, :, :, at_of(i)]
        return send(here, here, cs.at[i], cr.at[i], me.at_c)

    def part_of(ref, i, *index):
        return ref.at[(parts[i][0] % ref.shape[0], *index, at_of(i))]

    low_rows, high_rows, all_rows = pl.ds(0, rows // 2), pl.ds(rows // 2, rows // 2), pl.ds(0, rows)

    def half_x(i):
        return send(part_of(acc, i, me.chip_d, low_rows), part_of(half, i, 0, low_rows), hs.at[i, 0], hr.at[i, 0], me.at_x)

    def half_y(i):
        return send(part_of(acc, i, me.chip_d, high_rows), part_of(half, i, 1, low_rows), hs.at[i, 1], hr.at[i, 1], me.at_y)

    def plane_x(i):
        return send(part_of(acc, i, me.chip_x, all_rows), part_of(plane, i, 0, all_rows), ps.at[i, 0], pr.at[i, 0], me.at_x)

    def plane_y(i):
        return send(part_of(acc, i, me.chip_y, all_rows), part_of(plane, i, 1, all_rows), ps.at[i, 1], pr.at[i, 1], me.at_y)

    end = (me.s == 0) | (me.s == 3)
    mid = (me.s == 1) | (me.s == 2)
    partner = me.along(me.s + 1 - 2 * lax.rem(me.s, 2))
    other = me.along(3 - me.s)

    def line_in(i):
        return send(part_of(zsum, i, all_rows), part_of(line, i, 0, all_rows), zs.at[i, 0], zr.at[i, 0], partner)

    def line_swap(i):
        return send(part_of(zsum, i, all_rows), part_of(line, i, 1, all_rows), zs.at[i, 0], zr.at[i, 1], other)

    def line_back(i):
        return send(part_of(ztot, i, all_rows), part_of(line, i, 0, all_rows), zs.at[i, 1], zr.at[i, 0], partner)

    def out_of(i):
        unit, offset, width = parts[i]
        return units[unit][2](offset, width)

    def out_mid(i):
        return pltpu.make_async_copy(part_of(ztot, i, all_rows), out_of(i), out_sem.at[i])

    def out_end(i):
        return pltpu.make_async_copy(part_of(line, i, 0, all_rows), out_of(i), out_sem.at[i])

    def wide(a):
        return a.astype(F32)

    def add(dst, a, b):
        dst[...] = (wide(a[...]) + wide(b[...])).astype(BF)

    def produce(i):
        unit = parts[i][0]
        left, right, _ = units[unit]
        at, slot = at_of(i), unit % 2
        for m in leads(i, 2):
            core_all(m).wait_send()
        if leads(i, core_slots):
            pl.semaphore_wait(credit, 1)

        def step(j, _):
            to_send[slot, j, :, at] = mm(left(2 * j + 1 - me.c), right(at), 0, 0).astype(BF)
            there = from_core.at[unit % core_slots, j, :, at]
            send(to_send.at[slot, j, :, at], there, cs.at[i], cr.at[i], me.at_c).start()
            return 0

        steps(0, 4, step, 0)

        def keep(j, _):
            own[slot, j, :, at] = mm(left(2 * j + me.c), right(at), 0, 0).astype(BF)
            return 0

        steps(0, 4, keep, 0)

    def s1(i):
        unit = parts[i][0]
        for m in leads(i, acc_slots):
            sent_acc(m)
        core_all(i).wait_recv()

        def step(j, _):
            here = (j, all_rows)
            add(part_of(acc, i, *here), part_of(own, i, *here), part_of(from_core, i, *here))
            return 0

        steps(0, 4, step, 0)
        half_x(i).start()
        half_y(i).start()
        if i == members[unit][-1] and unit + core_slots < len(units):
            pl.semaphore_signal(credit, inc=1, device_id=me.at_c, device_id_type=MESH)

    def s2(i):
        half_x(i).wait_recv()
        here = part_of(acc, i, me.chip_y, low_rows)
        add(here, here, part_of(half, i, 0, low_rows))
        plane_y(i).start()
        half_y(i).wait_recv()
        here = part_of(acc, i, me.chip_x, high_rows)
        add(here, here, part_of(half, i, 1, low_rows))
        plane_x(i).start()

    def s3(i):
        for m in leads(i, z_slots):
            pl.when(end)(lambda m=m: line_in(m).wait_send())
            pl.when(mid)(lambda m=m: line_swap(m).wait_send())
        plane_x(i).wait_recv()
        plane_y(i).wait_recv()
        got = wide(part_of(plane, i, 0, all_rows)[...]) + wide(part_of(plane, i, 1, all_rows)[...])
        part_of(zsum, i, all_rows)[...] = (wide(part_of(acc, i, me.chip, all_rows)[...]) + got).astype(BF)
        pl.when(end)(lambda: line_in(i).start())

    def z1(i):
        @pl.when(mid)
        def _():
            line_in(i).wait_recv()
            here = part_of(zsum, i, all_rows)
            add(here, here, part_of(line, i, 0, all_rows))
            line_swap(i).start()

    def z2(i):
        @pl.when(mid)
        def _():
            for m in leads(i, z_slots):
                line_back(m).wait_send()
                out_mid(m).wait()
            line_swap(i).wait_recv()
            add(part_of(ztot, i, all_rows), part_of(zsum, i, all_rows), part_of(line, i, 1, all_rows))
            line_back(i).start()
            out_mid(i).start()

    def z3(i):
        @pl.when(end)
        def _():
            line_back(i).wait_recv()
            out_end(i).start()

    def sent_acc(i):
        half_x(i).wait_send()
        half_y(i).wait_send()
        plane_x(i).wait_send()
        plane_y(i).wait_send()

    def v_swap(i, to):
        return send(vbuf.at[i], vrecv.at[i], vs.at[i], vr.at[i], to)

    v_to = (me.at_c, me.at_x, me.at_y)

    def v_step(i):
        if i == 0:
            vbuf[0] = sums[...]
            v_swap(0, v_to[0]).start()
        elif i < 4:
            v_swap(i - 1, v_to[i - 1]).wait_recv()
            vbuf[i] = vbuf[i - 1] + vrecv[i - 1]
            if i < 3:
                v_swap(i, v_to[i]).start()
            else:
                pl.when(end)(lambda: v_swap(3, partner).start())
        elif i == 4:

            @pl.when(mid)
            def _():
                v_swap(3, partner).wait_recv()
                vbuf[4] = vbuf[3] + vrecv[3]
                v_swap(4, other).start()

        elif i == 5:

            @pl.when(mid)
            def _():
                v_swap(4, other).wait_recv()
                vbuf[5] = vbuf[4] + vrecv[4]
                v_swap(5, partner).start()
                vec_out[...] = vbuf[5]

        elif i == 6:

            @pl.when(end)
            def _():
                v_swap(5, partner).wait_recv()
                vec_out[...] = vrecv[5]

    def put(i, value, tile=slice(None)):
        sums[pl.ds(i, 1), tile] = jnp.sum(value, axis=0, keepdims=True)

    def inner_grad(quarter, slot):
        def step(j, _):
            tile = at_tile(j, TILE)
            y = mm(gout[...], w_in[slot, tile, :], 1, 1) * wide(slope[quarter, :, tile])
            y = y.astype(BF)
            ginner[quarter, :, tile] = y
            put(8 + quarter, wide(y), tile)
            return 0

        steps(0, d // TILE, step, 0)

    def first_grad(quarter, slot):
        def step(j, _):
            tile = at_tile(j, TILE)
            gfirst[:, tile] = gfirst[:, tile] + mm(ginner[quarter], w_in[slot, tile, :], 1, 1)
            return 0

        steps(0, d // TILE, step, 0)

    def first_norm_back():
        gain = vecs[pl.ds(G1, 1), :]

        def step(j, carry):
            at = at_tile(j, ROW)
            g, centred = gfirst[at, :], n1[at, :]
            grad = norm_back(g * gain, centred, scale1[at, :1])
            gfirst[at, :] = grad
            rounded = grad.astype(BF)
            gattn[at, :] = rounded
            return carry[0] + eighths(g * centred), carry[1] + eighths(g), carry[2] + eighths(wide(rounded))

        zero = jnp.zeros((8, d), F32)
        gains, shifts, biases = steps(0, length // ROW, step, (zero, zero, zero))
        put(4, gains)
        put(5, shifts)
        put(2, biases)

    def context_grad(slot):
        def step(j, _):
            tile = at_tile(j, TILE)
            gctx[:, tile] = mm(gattn[...], w_in[slot, tile, :], 1, 1).astype(BF)
            return 0

        steps(0, d // TILE, step, 0)

    def p_load(pair, h, slot):
        return pltpu.make_async_copy(p_in.at[2 * pair + h], probs.at[slot, h], p_sem.at[slot, h])

    def attend_back(pair):
        slot = pair % 2
        if pair + 1 < d // LANES:
            for h in range(2):
                p_load(pair + 1, h, 1 - slot).start()
        masks = half_masks()
        at = pl.ds(pair * LANES, LANES)
        qp, kp, vp, gp = q[:, at], k[:, at], v[:, at], gctx[:, at]
        outs = None
        for h in range(2):
            p_load(pair, h, slot).wait()
            p = wide(probs[slot, h])
            g = mm(gp * masks[h].astype(BF), vp, 1, 1)
            w = p * g
            s = (w - p * jnp.sum(w, axis=1, keepdims=True)).astype(BF)
            got = (
                mm(s, kp) * (masks[h] * (1.0 / math.sqrt(HD))),
                mm(s, qp, 0, 0) * masks[h],
                mm(probs[slot, h], gp, 0, 0) * masks[h],
            )
            outs = got if outs is None else tuple(a + b for a, b in zip(outs, got))
        for ref, y, i in ((dq, outs[0], 0), (dk, outs[1], None), (dv, outs[2], 1)):
            y = y.astype(BF)
            ref[:, at] = y
            if i is not None:
                put(i, wide(y), at)

    def token_grad(j):
        tile = pl.ds(j * TILE, TILE)
        y = gfirst[:, tile]
        for ref, i in ((dq, 9), (dk, 10), (dv, 11)):
            y = y + mm(ref[...], w_in[i % 3, tile, :], 1, 1)
        gtok[:, tile] = y.astype(BF)

    for quarter in range(QUARTERS):
        load(hid_in.at[quarter], hidden.at[quarter], quarter).start()
    load(gout_in, gout, 4).start()
    w_load(0).start()
    load(slope_in, slope, 5).start()
    w_load(1).start()
    load(gsec_in, gfirst, 6).start()
    later = ((low_in, low, 7), (n1_in, n1, 8), (scale_in, scale1, 9), (vec_in, vecs, 10), (part_in, part, 11))
    for src, dst, i in later:
        load(src, dst, i).start()
    greet(me)
    lay_back = Exchange(me, lay_in, lay_out, a_sems, 0, True)
    tok_back = Exchange(me, gtok, gtok_out, a_sems, 1, True)
    for quarter in range(QUARTERS):
        load(hid_in.at[quarter], hidden.at[quarter], quarter).wait()
    load(gout_in, gout, 4).wait()
    sums[...] = jnp.zeros_like(sums)
    stages = {"P": produce, "S1": s1, "S2": s2, "S3": s3, "Z1": z1, "Z2": z2, "Z3": z3, "V": v_step, "AB": attend_back, "TG": token_grad}
    for op, *at in BACK_ORDER:
        i = at[0] if at else 0
        if op == "V" and i == 0:
            for row, j in ((0, 6), (1, 7), (2, 3)):
                sums[pl.ds(j, 1), :] = part[pl.ds(row, 1), :]
        if op in stages:
            stages[op](i)
        elif op in ("LO", "GT"):
            (lay_back if op == "LO" else tok_back).start(*at)
        elif op == "IG":
            if i == 0:
                load(slope_in, slope, 5).wait()
                load(gsec_in, gfirst, 6).wait()
                load(low_in, low, 7).wait()
            w_load(2 * i + 2).start()
            w_load(2 * i).wait()
            inner_grad(i, (2 * i) % 3)
        elif op == "FG":
            w_load(2 * i + 3).start()
            w_load(2 * i + 1).wait()
            first_grad(i, (2 * i + 1) % 3)
        elif op == "LD":
            for src, dst, j in ((q_in, q, 0), (k_in, k, 1), (v_in, v, 2)):
                for pair in range(d // LANES):
                    load(src.at[pair], dst.at[:, pl.ds(pair * LANES, LANES)], j).start()
            load(x_in, x, 3).start()
            load(ctx_in, ctx, 5).start()
            for h in range(2):
                p_load(0, h, 0).start()
        elif op == "LW":
            for dst, j in ((q, 0), (k, 1), (v, 2)):
                load(x_in, dst, j).wait()
            load(x_in, x, 3).wait()
            load(ctx_in, ctx, 5).wait()
        elif op == "NB":
            for src, dst, j in later[1:]:
                load(src, dst, j).wait()
            first_norm_back()
        elif op == "CG":
            w_load(10).start()
            w_load(8).wait()
            context_grad(8 % 3)
            w_load(11).start()
        elif op == "TW":
            for j in (9, 10, 11):
                w_load(j).wait()
    for unit in members[-2:]:
        for i in unit:
            core_all(i).wait_send()
    for unit in members[-acc_slots:]:
        for i in unit:
            sent_acc(i)
    for i in range(n):
        pl.when(end)(lambda i=i: out_end(i).wait())
    for unit in members[-z_slots:]:
        for i in unit:
            pl.when(end)(lambda i=i: line_in(i).wait_send())

            @pl.when(mid)
            def _(i=i):
                line_swap(i).wait_send()
                line_back(i).wait_send()
                out_mid(i).wait()

    for i in range(3):
        v_swap(i, v_to[i]).wait_send()
    pl.when(end)(lambda: v_swap(3, partner).wait_send())

    @pl.when(mid)
    def _():
        v_swap(4, other).wait_send()
        v_swap(5, partner).wait_send()

    for exchange in (lay_back, tok_back):
        exchange.wait()
        exchange.sent()


def backward_all(saved, block):
    length, d = saved[0].shape
    rows = d // RING
    units, n = len(BACK_PARTS), sum(BACK_PARTS)
    core_slots, acc_slots, z_slots = 3, 3, 3
    dma = pltpu.SemaphoreType.DMA
    shape = jax.ShapeDtypeStruct

    def vm(*s, dtype=BF):
        return pltpu.VMEM(s, dtype)

    split = shape((LINE, block, d), BF)
    sq = shape((rows, d), BF)
    sums = (16, d)
    outs = [split, split, sq, sq, sq, sq, shape((rows, QUARTERS * d), BF), shape((QUARTERS * rows, d), BF), shape(sums, F32)]
    mat = (length, d)
    mlp = (QUARTERS, length, d)
    return pl.pallas_call(
        backward_kernel,
        out_shape=outs,
        in_specs=[ANY] * len(saved),
        out_specs=[ANY] * 8 + [pl.BlockSpec(memory_space=pltpu.VMEM)],
        scratch_shapes=[
            vm(core_slots, 4, rows, d), vm(units, 2, rows // 2, d), vm(units, 2, rows, d), vm(units, 2, rows, d),
            vm(2, 4, rows, d), vm(2, 4, rows, d), vm(acc_slots, 4, rows, d), vm(z_slots, rows, d), vm(z_slots, rows, d),
            vm(6, *sums, dtype=F32), vm(6, *sums, dtype=F32),
            vm(*mlp), vm(*mat), vm(*mlp), vm(*mlp), vm(*mat, dtype=F32), vm(*mat, dtype=F32), vm(length, LANES, dtype=F32), vm(*mat),
            vm(*mat), vm(*mat), vm(2, 2, length, length), vm(3, d, d), vm(24, d, dtype=F32), vm(8, d, dtype=F32), vm(*sums, dtype=F32),
            pltpu.SemaphoreType.REGULAR,
            dma((n,)), dma((n,)), dma((n, 2)), dma((n, 2)), dma((n, 2)), dma((n, 2)), dma((n, 2)), dma((n, 2)),
            dma((n,)), dma((6,)), dma((6,)), dma((2, 4)), dma((2, 4)), dma((2,)), dma((12,)), dma((3,)), dma((2, 2)),
        ],
        compiler_params=pltpu.CompilerParams(collective_id=1, has_side_effects=True, vmem_limit_bytes=62 << 20),
        name="backward",
    )(*saved)


def finish_kernel(lay, gtok, *rest):
    mats, sums, outs = rest[:6], rest[6], rest[7:]
    outs[0][...] = lay[...]
    outs[1][...] = gtok[...]
    for src, dst in zip(mats, outs[2:8]):
        dst[...] = src[...].astype(F32)
    lo = lax.axis_index("grp")
    for i, dst in zip((0, 1, 2, 8, 3, 4, 5, 6, 7), outs[8:]):
        n = dst.shape[0]
        if i < 8:
            row, column = i, lo * n
        else:
            per = sums.shape[1] // n
            row, column = 8 + lo // per, lax.rem(lo, per) * n
        dst[...] = sums[pl.ds(row, 1), pl.ds(pl.multiple_of(column, LANES), n)].reshape(n)


def finish(out):
    count = out[0].shape[0]
    shape = jax.ShapeDtypeStruct

    def rows(a, dtype):
        block = (a.shape[0] // count,) + a.shape[1:]
        return pl.BlockSpec(block, lambda i: (i,) + (0,) * (len(block) - 1)), shape(a.shape, dtype)

    d = out[8].shape[1]
    ins = [rows(a, a.dtype)[0] for a in out[:8]] + [pl.BlockSpec(out[8].shape, lambda i: (0, 0))]
    big = [rows(a, a.dtype if k < 2 else F32) for k, a in enumerate(out[:8])]
    sizes = [d // RING] * 3 + [QUARTERS * d // RING] + [d // RING] * 5
    small = [(pl.BlockSpec((n,), lambda i: (0,)), shape((n,), F32)) for n in sizes]
    specs, shapes = zip(*(big + small))
    return tuple(
        pl.pallas_call(
            finish_kernel,
            grid=(count,),
            in_specs=ins,
            out_specs=list(specs),
            out_shape=list(shapes),
            compiler_params=pltpu.CompilerParams(vmem_limit_bytes=40 << 20),
            name="finish",
        )(*out)
    )


def local(tokens, labels, *rest):
    weights, vectors, cotangent = rest[:6], rest[6:15], rest[15]
    groups = lax.axis_size("grp") // RING
    g, s = lax.axis_index("grp"), lax.axis_index("seq")
    lo = lax.rem(g, RING)
    if groups > 1:
        def regroup(w):
            full = lax.all_gather(w, ("grp", "seq"), axis=0, tiled=True)
            n = full.shape[0] // (RING * LINE)
            return lax.dynamic_slice_in_dim(full, (lo * LINE + s) * n, n, 0)

        weights = tuple(regroup(w) for w in weights)
        vectors = tuple(regroup(v) for v in vectors)
    gaps = [jnp.zeros((LANES - v.shape[0],), BF) for v in vectors]
    packed = [p for v, gap in zip(vectors, gaps) for p in (v, gap)] + [jnp.zeros(((16 - len(vectors)) * LANES,), BF)]
    packed = jnp.concatenate(packed).reshape(16, LANES)
    saved = forward_all(tokens, cotangent, labels, packed, weights)
    out = backward_all(saved, tokens.shape[1])
    if groups == 1:
        return finish(out)
    layer_out, grad_tokens = out[:2]
    mats = [m.astype(F32) for m in out[2:8]]
    vec = out[8]
    flat = [vec[i] for i in range(8)]
    flat.insert(3, vec[8 : 8 + QUARTERS].reshape(-1))
    same = [[l + RING * h for h in range(groups)] for l in range(RING)]
    eight = [[l + RING * h for l in range(RING)] for h in range(groups)]

    def rejoin(m):
        m = lax.psum(m, "grp", axis_index_groups=same)
        m = lax.all_gather(m, "grp", axis=0, tiled=True, axis_index_groups=eight)
        n = m.shape[0] // (RING * groups)
        return lax.dynamic_slice_in_dim(m, g * n, n, 0)

    mats = [rejoin(m) for m in mats]
    flat = [lax.psum(v, "grp", axis_index_groups=same) for v in flat]
    flat = [lax.dynamic_slice_in_dim(v, g * (v.shape[0] // (RING * groups)), v.shape[0] // (RING * groups), 0) for v in flat]
    return (layer_out, grad_tokens, *mats, *flat)


def solution(mesh):
    both = ("grp", "seq")
    rows = P("grp", "seq", None)
    return jax.shard_map(
        local,
        mesh=mesh,
        in_specs=(rows, P("grp", None)) + (P(both, None),) * 6 + (P(both),) * 9 + (rows,),
        out_specs=(rows, rows) + (P("grp", None),) * 6 + (P("grp"),) * 9,
        check_vma=False,
    )
```

```python
import functools
import math

import jax
import jax.numpy as jnp
from jax import lax
from jax.experimental import pallas as pl
from jax.experimental.pallas import tpu as pltpu
from jax.sharding import PartitionSpec as P

H = 16
HD = 64
LINE = 4
RING = 8
UNITS = 12
QUARTERS = 4
LANES = 128
MESH = pl.DeviceIdType.MESH
BF = jnp.bfloat16
F32 = jnp.float32
ANY = pl.BlockSpec(memory_space=pl.ANY)


class Place:
    def __init__(self):
        self.g = lax.axis_index("grp")
        self.s = lax.axis_index("seq")
        self.lo = lax.rem(self.g, RING)
        self.c = lax.rem(self.lo, 2)
        xb = lax.rem(self.lo // 2, 2)
        yb = self.lo // 4
        self.dc, self.dx, self.dy = 1 - 2 * self.c, 2 - 4 * xb, 4 - 8 * yb
        self.at_c = (self.g + self.dc, self.s)
        self.at_x = (self.g + self.dx, self.s)
        self.at_y = (self.g + self.dy, self.s)
        self.chip = self.lo // 2
        self.chip_x = self.chip + 1 - 2 * xb
        self.chip_y = self.chip + 2 - 4 * yb
        self.chip_d = self.chip_x + 2 - 4 * yb

    def along(self, t):
        return (self.g, t)


def send(src, dst, send_sem, recv_sem, to):
    return pltpu.make_async_remote_copy(
        src_ref=src, dst_ref=dst, send_sem=send_sem, recv_sem=recv_sem, device_id=to, device_id_type=MESH
    )


def greet(me):
    barrier = pltpu.get_barrier_semaphore()

    def signal(to):
        pl.semaphore_signal(barrier, inc=1, device_id=to, device_id_type=MESH)

    for to in (me.at_c, me.at_x, me.at_y):
        signal(to)
    for t in range(LINE):
        pl.when(me.s != t)(lambda t=t: signal(me.along(t)))
    pl.semaphore_wait(barrier, 3 + LINE - 1)


class Exchange:
    def __init__(self, me, whole, split, sems, index, back):
        self.me, self.whole, self.split, self.index, self.back = me, whole, split, index, back
        self.send_sem, self.recv_sem, self.local_sem = sems

    def rows(self, t, part=0, parts=1):
        n = self.split.shape[1]
        return self.whole.at[pl.ds(t * n + part * (n // parts), n // parts)]

    def ends(self, t, part=0, parts=1):
        n = self.split.shape[1] // parts
        here = pl.ds(part * n, n)
        if self.back:
            return self.rows(t, part, parts), self.split.at[self.me.s, here]
        return self.split.at[t, here], self.rows(self.me.s, part, parts)

    def copy(self, t, part=0, parts=1):
        src, dst = self.ends(t, part, parts)
        return send(src, dst, self.send_sem.at[self.index, t], self.recv_sem.at[self.index, self.me.s], self.me.along(t))

    def landed(self, t):
        dst = self.split.at[t] if self.back else self.rows(t)
        return send(dst, dst, self.send_sem.at[self.index, t], self.recv_sem.at[self.index, t], self.me.along(t))

    def own(self):
        src, dst = self.ends(self.me.s)
        return pltpu.make_async_copy(src, dst, self.local_sem.at[self.index])

    def start(self, distance, part=0, parts=1):
        s = self.me.s
        if distance == 1 and part == 0:
            self.own().start()
        for t in range(LINE):
            pl.when((s - t == distance) | (t - s == distance))(lambda t=t: self.copy(t, part, parts).start())

    def wait(self):
        self.own().wait()
        for t in range(LINE):
            pl.when(self.me.s != t)(lambda t=t: self.landed(t).wait_recv())

    def sent(self):
        for t in range(LINE):
            pl.when(self.me.s != t)(lambda t=t: self.copy(t).wait_send())


class Gather:
    def __init__(self, me, src, dst, rows, sems, u, fine):
        self.me, self.src, self.dst, self.rows, self.u, self.fine = me, src, dst, rows, u, fine
        self.local, self.zs, self.zr, self.xs, self.xr, self.cs, self.cr = sems

    def own(self):
        me = self.me
        return pltpu.make_async_copy(self.src, self.dst((me.lo * LINE + me.s) * self.rows, self.rows), self.local.at[self.u])

    def shard(self, source):
        return self.dst((self.me.lo * LINE + source) * self.rows, self.rows)

    def z_send(self, source, step, slot):
        there = self.shard(source)
        src = self.src if slot < 2 else there
        return send(src, there, self.zs.at[self.u, slot], self.zr.at[self.u, source], self.me.along(self.me.s + step))

    def z_recv(self, source):
        there = self.shard(source)
        send(there, there, self.zs.at[self.u, 0], self.zr.at[self.u, source], self.me.at_c).wait_recv()

    def xy_shard(self, source, own):
        there = self.shard(source)
        for k, to in ((0, self.me.at_x), (1, self.me.at_y)):
            send(self.src if own else there, there, self.xs.at[self.u, k], self.xr.at[self.u, k], to).start()

    def start(self):
        me = self.me
        self.own().start()
        pl.when(me.s < LINE - 1)(lambda: self.z_send(me.s, 1, 0).start())
        pl.when(me.s > 0)(lambda: self.z_send(me.s, -1, 1).start())
        if self.fine:
            self.xy_shard(me.s, True)

    def hop(self, h):
        me = self.me

        @pl.when(me.s >= h)
        def _():
            self.z_recv(me.s - h)
            if h < LINE - 1:
                pl.when(me.s < LINE - 1)(lambda: self.z_send(me.s - h, 1, 2 * h).start())
            if self.fine:
                self.xy_shard(me.s - h, False)

        @pl.when(me.s < LINE - h)
        def _():
            self.z_recv(me.s + h)
            if h < LINE - 1:
                pl.when(me.s > 0)(lambda: self.z_send(me.s + h, -1, 2 * h + 1).start())
            if self.fine:
                self.xy_shard(me.s + h, False)

    def block(self, lo, half=None):
        rows = self.rows * LINE
        if half is None:
            return self.dst(lo * rows, rows)
        return self.dst(lo * rows + half * (rows // 2), rows // 2)

    def x1(self, lo):
        return send(self.block(lo), self.block(lo), self.xs.at[self.u, 0], self.xr.at[self.u, 0], self.me.at_x)

    def y1(self, lo):
        return send(self.block(lo), self.block(lo), self.xs.at[self.u, 1], self.xr.at[self.u, 1], self.me.at_y)

    def x2(self, lo):
        return send(self.block(lo, 1), self.block(lo, 1), self.xs.at[self.u, 2], self.xr.at[self.u, 2], self.me.at_x)

    def y2(self, lo):
        return send(self.block(lo, 0), self.block(lo, 0), self.xs.at[self.u, 3], self.xr.at[self.u, 3], self.me.at_y)

    def core(self, lo, k):
        return send(self.block(lo), self.block(lo), self.cs.at[self.u, k], self.cr.at[self.u, k], self.me.at_c)

    def spread(self):
        me = self.me
        self.own().wait()
        if not self.fine:
            self.x1(me.lo).start()
            self.y1(me.lo).start()
        self.core(me.lo, 0).start()

    def cross(self):
        me = self.me
        lo_x, lo_y = me.lo + me.dx, me.lo + me.dy
        self.x1(lo_x).wait_recv()
        self.y2(lo_x).start()
        self.core(lo_x, 1).start()
        self.y1(lo_y).wait_recv()
        self.x2(lo_y).start()
        self.core(lo_y, 2).start()

    def corner(self):
        me = self.me
        lo_d = me.lo + me.dx + me.dy
        self.x2(lo_d).wait_recv()
        self.y2(lo_d).wait_recv()
        self.core(lo_d, 3).start()

    def whole(self):
        me = self.me
        for k, lo in enumerate((me.lo, me.lo + me.dx, me.lo + me.dy, me.lo + me.dx + me.dy)):
            self.core(lo + me.dc, k).wait_recv()

    def sent(self):
        me = self.me
        for h in range(LINE - 1):
            right = (me.s >= h) & (me.s < LINE - 1)
            left = (me.s < LINE - h) & (me.s > 0)
            pl.when(right)(lambda h=h: self.z_send(me.s - h, 1, 2 * h).wait_send())
            pl.when(left)(lambda h=h: self.z_send(me.s + h, -1, 2 * h + 1).wait_send())
        self.x1(me.lo).wait_send()
        self.y1(me.lo).wait_send()
        self.x2(me.lo + me.dy).wait_send()
        self.y2(me.lo + me.dx).wait_send()
        for k, lo in enumerate((me.lo, me.lo + me.dx, me.lo + me.dy, me.lo + me.dx + me.dy)):
            self.core(lo, k).wait_send()


def rows_of(ref, columns=None):
    if columns is None:
        return lambda row, n: ref.at[pl.ds(row, n)]
    return lambda row, n: ref.at[pl.ds(row, n), columns]


def rows_of(ref, columns=None):
    if columns is None:
        return lambda row, n: ref.at[pl.ds(row, n)]
    return lambda row, n: ref.at[pl.ds(row, n), columns]


def mm(a, b, ca=1, cb=0):
    return lax.dot_general(a, b, (((ca,), (cb,)), ((), ())), preferred_element_type=F32)


def at_tile(j, tile):
    if isinstance(j, int):
        return pl.ds(j * tile, tile)
    return pl.ds(pl.multiple_of(j * tile, tile), tile)


def steps(first, last, step, carry=0):
    for j in range(first, last):
        carry = step(j, carry)
    return carry


def iota(shape, dim):
    return lax.broadcasted_iota(jnp.int32, shape, dim)


def half_masks():
    low = (iota((1, LANES), 1) < HD).astype(F32)
    return low, 1.0 - low


def gelu_parts(u):
    t = 1.0 / (1.0 + (0.3275911 * 0.7071067811865476) * jnp.abs(u))
    poly = t * (0.254829592 + t * (-0.284496736 + t * (1.421413741 + t * (-1.453152027 + t * 1.061405429))))
    bell = jnp.exp(-0.5 * u * u)
    tail = 0.5 * poly * bell
    cdf = jnp.where(u >= 0.0, 1.0 - tail, tail)
    return u * cdf, cdf + u * (bell * 0.3989422804014327)


def stats(r):
    centered = r - jnp.mean(r, axis=-1, keepdims=True)
    scale = lax.rsqrt(jnp.mean(centered * centered, axis=-1, keepdims=True) + 1e-06)
    return centered * scale, scale


def norm_back(u, n, scale):
    return (u - jnp.mean(u, axis=-1, keepdims=True) - n * jnp.mean(u * n, axis=-1, keepdims=True)) * scale


def eighths(x):
    return jnp.sum(x.reshape(x.shape[0] // 8, 8, x.shape[1]), axis=0)


FINE = (0, 2, 3)
OUTER_PARTS = (1, 1, 1, 2)
FORWARD_ORDER = (
    ("ST", 0), ("ST", 1), ("ST", 2), ("ST", 3), ("ST", 4), ("R", 0, 1), ("R", 1, 1), ("R", 2, 1), ("R", 3, 1), ("R", 4, 1), ("R", 0, 2),
    ("R", 1, 2), ("R", 2, 2), ("R", 3, 2), ("R", 4, 2), ("R", 0, 3), ("SP", 0), ("R", 1, 3), ("SP", 1), ("R", 2, 3), ("SP", 2),
    ("R", 3, 3), ("CX", 0), ("SP", 3), ("CX", 1), ("ST", 5), ("ST", 6), ("CX", 2), ("R", 4, 3), ("SP", 4), ("ST", 7), ("CX", 3),
    ("ST", 8), ("R", 5, 1), ("CO", 0), ("CO", 1), ("R", 6, 1), ("WH", 0), ("CO", 2), ("WH", 1), ("R", 7, 1), ("WH", 2), ("UN",),
    ("R", 8, 1), ("R", 5, 2), ("R", 6, 2), ("TK", 2, 0, 4), ("CX", 4), ("R", 7, 2), ("TK", 3, 0, 4), ("R", 8, 2), ("CO", 3),
    ("R", 5, 3), ("SP", 5), ("TK", 1, 0, 4), ("WH", 3), ("R", 6, 3), ("SP", 6), ("TK", 2, 1, 4), ("CO", 4), ("TK", 3, 1, 4), ("WH", 4),
    ("TK", 1, 1, 4), ("R", 7, 3), ("SP", 7), ("TK", 2, 2, 4), ("CX", 5), ("TK", 3, 2, 4), ("R", 8, 3), ("SP", 8), ("TK", 1, 2, 4),
    ("TK", 2, 3, 4), ("CX", 6), ("TK", 3, 3, 4), ("TK", 1, 3, 4), ("CX", 7), ("ST", 9), ("CO", 5), ("ST", 10), ("ST", 11), ("WH", 5),
    ("ST", 12), ("QP", 0), ("R", 9, 1), ("QP", 1), ("CX", 8), ("R", 10, 1), ("R", 11, 1), ("QP", 2), ("R", 12, 1), ("CO", 6), ("AT", 0),
    ("R", 9, 2), ("R", 10, 2), ("WH", 6), ("AT", 1), ("R", 11, 2), ("CO", 7), ("AT", 2), ("R", 12, 2), ("CO", 8), ("R", 9, 3),
    ("SP", 9), ("WH", 7), ("AT", 3), ("R", 10, 3), ("SP", 10), ("WH", 8), ("ST", 13), ("AT", 4), ("R", 11, 3), ("SP", 11), ("R", 12, 3),
    ("SP", 12), ("AT", 5), ("R", 13, 1), ("AT", 6), ("CX", 9), ("ST", 14), ("SD", 2, 0, 4), ("AT", 7), ("R", 13, 2), ("SD", 3, 0, 4),
    ("F0",), ("R", 14, 1), ("FN",), ("CX", 10), ("SD", 1, 0, 4), ("SD", 2, 1, 4), ("IN", 0, 0), ("SD", 3, 1, 4), ("IN", 0, 1),
    ("R", 13, 3), ("SP", 13), ("SD", 1, 1, 4), ("CX", 11), ("SD", 2, 2, 4), ("IN", 1, 0), ("R", 14, 2), ("IN", 1, 1), ("SD", 3, 2, 4),
    ("IN", 2, 0), ("CX", 12), ("SD", 1, 2, 4), ("SD", 2, 3, 4), ("IN", 2, 1), ("CO", 9), ("SD", 3, 3, 4), ("SD", 1, 3, 4), ("WH", 9),
    ("R", 14, 3), ("SP", 14), ("CO", 10), ("IN", 3, 0), ("WH", 10), ("IN", 3, 1), ("CX", 13), ("OU", 0), ("CO", 11), ("WH", 11),
    ("CO", 12), ("OU", 1), ("CX", 14), ("WH", 12), ("CO", 13), ("OU", 2), ("CO", 14), ("WH", 13), ("WH", 14), ("OU", 3), ("OU", 4),
    ("N2",),
)
BACK_PARTS = (1, 1, 1, 1, 1, 1, 1, 1, 1, 1, 1, 1)
BACK_ORDER = (
    ("LO", 2, 0, 4), ("LO", 2, 1, 4), ("LO", 2, 2, 4), ("P", 0), ("P", 1), ("IG", 0), ("S1", 0), ("FG", 0), ("S1", 1), ("LO", 2, 3, 4),
    ("IG", 1), ("LO", 3, 0, 4), ("P", 2), ("S2", 0), ("LO", 3, 1, 4), ("FG", 1), ("LO", 3, 2, 4), ("IG", 2), ("S2", 1), ("S1", 2),
    ("LO", 3, 3, 4), ("LO", 1, 0, 4), ("FG", 2), ("LO", 1, 1, 4), ("IG", 3), ("LO", 1, 2, 4), ("S3", 0), ("FG", 3), ("P", 3),
    ("LO", 1, 3, 4), ("LD",), ("NB",), ("P", 4), ("S1", 3), ("S3", 1), ("CG",), ("S2", 2), ("LW",), ("AB", 0), ("S1", 4), ("S2", 3),
    ("Z1", 0), ("AB", 1), ("AB", 2), ("AB", 3), ("S3", 2), ("Z1", 1), ("AB", 4), ("Z2", 0), ("S2", 4), ("AB", 5), ("AB", 6), ("AB", 7),
    ("S3", 3), ("Z1", 2), ("Z2", 1), ("V", 0), ("TW",), ("TG", 0), ("Z3", 0), ("P", 5), ("P", 6), ("S3", 4), ("V", 1), ("TG", 1),
    ("S1", 5), ("Z1", 3), ("Z2", 2), ("Z3", 1), ("TG", 2), ("S1", 6), ("V", 2), ("TG", 3), ("GT", 2, 0, 4), ("GT", 3, 0, 4),
    ("GT", 1, 0, 4), ("P", 7), ("S2", 5), ("Z1", 4), ("V", 3), ("P", 8), ("S2", 6), ("Z2", 3), ("S1", 7), ("Z3", 2), ("P", 9), ("V", 4),
    ("GT", 2, 1, 4), ("GT", 3, 1, 4), ("S3", 5), ("S1", 8), ("P", 10), ("V", 5), ("GT", 1, 1, 4), ("GT", 2, 2, 4), ("GT", 3, 2, 4),
    ("Z2", 4), ("S3", 6), ("S1", 9), ("V", 6), ("P", 11), ("S2", 7), ("Z1", 5), ("Z3", 3), ("S2", 8), ("GT", 1, 2, 4), ("GT", 2, 3, 4),
    ("S2", 9), ("GT", 3, 3, 4), ("GT", 1, 3, 4), ("Z1", 6), ("S3", 7), ("S1", 10), ("Z2", 5), ("Z3", 4), ("S3", 8), ("S1", 11),
    ("Z1", 7), ("S2", 10), ("Z2", 6), ("S3", 9), ("Z1", 8), ("Z3", 5), ("S2", 11), ("Z2", 7), ("Z3", 6), ("Z1", 9), ("S3", 10),
    ("Z2", 8), ("Z3", 7), ("S3", 11), ("Z1", 10), ("Z2", 9), ("Z3", 8), ("Z1", 11), ("Z2", 10), ("Z3", 9), ("Z2", 11), ("Z3", 10),
    ("Z3", 11),
)
ROW = 64
TILE = 256
BQ, BV, BO, BI, BU, G1, S1, G2, S2 = range(9)
INNER = 16


def forward_kernel(
    tok, cot, labels, vec, wq, wk, wv, wo, wi, wu,
    x_out, wq_all, wk_all, wv_all, wo_all, wi_all, wu_all, q_out, k_out, v_out, p_out, ctx_out, low_out,
    n1_out, scale_out, hid_out, slope_out, gsec_out, gout_out, lay_out, vec_out, part_out,
    x, seed, packed, vecs, part, w_in, wu_in, q, k, v, bias, probs, ctx, n1, scale1, low, hidden, slope, res, gsec, gout, lay,
    local, zs, zr, xs, xr, cs, cr, a_send, a_recv, a_local, w_sem, p_sem, o_sem,
):
    me = Place()
    sems = (local, zs, zr, xs, xr, cs, cr)
    a_sems = (a_send, a_recv, a_local)
    d = x.shape[1]
    length = x.shape[0]
    units, pieces = [], []

    def add(src, ref, columns, to=None):
        src = src if columns is None else src.at[:, columns]
        u = len(units)
        units.append(Gather(me, src, rows_of(ref, columns), src.shape[0], sems, u, u in FINE))
        pieces.append(None if to is None else pltpu.make_async_copy(ref if columns is None else ref.at[:, columns], to, w_sem.at[u]))

    add(wq, wq_all, pl.ds(0, d // 2), w_in.at[0, :, pl.ds(0, d // 2)])
    add(vec, packed, None)
    add(wq, wq_all, pl.ds(d // 2, d // 2), w_in.at[0, :, pl.ds(d // 2, d // 2)])
    for i, (src, ref) in enumerate(((wk, wk_all), (wv, wv_all), (wo, wo_all))):
        add(src, ref, None, w_in.at[1 + i])
    width = wi.shape[1] // QUARTERS
    for j in range(QUARTERS):
        add(wi, wi_all, pl.ds(j * width, width), w_in.at[4 + j])
    outer_at = []
    for j, parts in enumerate(OUTER_PARTS):
        width = d // QUARTERS // parts
        for i in range(parts):
            add(wu, wu_all, pl.ds(j * TILE + i * width, width), wu_in.at[j, :, pl.ds(i * width, width)])
            outer_at.append((j, i * width, width))
    n = len(units)
    saves = []

    def save(src, dst):
        copy = pltpu.make_async_copy(src, dst, o_sem.at[len(saves)])
        copy.start()
        saves.append(copy)

    def row(i):
        return vecs[pl.ds(i, 1), :]

    def unpack():
        p = packed[...]
        piece = d // (RING * LINE)
        spread = (iota((LANES, d), 1) % piece == iota((LANES, d), 0)).astype(BF)
        wide = mm(p, spread).reshape(RING * LINE, 16, d)
        here = iota((RING * LINE, 1, d), 0) == iota((RING * LINE, 1, d), 2) // piece
        vecs[pl.ds(0, 16), :] = jnp.sum(jnp.where(here, wide, 0.0), axis=0)
        p = p.astype(F32).reshape(RING * LINE, 16, LANES)
        p = jnp.sum(jnp.where(iota(p.shape, 1) == BI, p, 0.0), axis=1).astype(BF)
        spread = (iota((LANES, d), 1) % LANES == iota((LANES, d), 0)).astype(BF)
        per = RING * LINE // QUARTERS
        wide = mm(p, spread).reshape(QUARTERS, per, d)
        here = iota((1, per, d), 1) == iota((1, per, d), 2) // LANES
        inner = jnp.sum(jnp.where(here, wide, 0.0), axis=1)
        vecs[pl.ds(INNER, 8), :] = jnp.concatenate([inner, jnp.zeros_like(inner)], axis=0)

    def mask():
        own = labels[pl.ds(me.s, 1), :]
        marks = jnp.where(own != 0, own, -1 - iota(own.shape, 1)).astype(F32)
        down = jnp.broadcast_to(marks, (LANES, length)).T[:, :1]
        bias[...] = jnp.where(down == marks, 0.0, -1e30)

    def project(slot):
        out, b, factor = ((q, BQ, 1.0 / math.sqrt(HD)), (k, None, None), (v, BV, None))[slot]

        def step(j, _):
            tile = at_tile(j, TILE)
            y = mm(x[...], w_in[slot, :, tile])
            if b is not None:
                y = y + vecs[pl.ds(b, 1), tile]
            y = y.astype(BF)
            if factor is not None:
                y = (y.astype(F32) * factor).astype(BF)
            out[2 * j] = y[:, :LANES]
            out[2 * j + 1] = y[:, LANES:]
            return 0

        steps(0, d // TILE, step, 0)

    def p_save(h, slot):
        return pltpu.make_async_copy(probs.at[slot], p_out.at[h], p_sem.at[slot])

    def attend(pair):
        masks = half_masks()
        kp, vp, qp = k[pair], v[pair], q[pair]
        out = None
        for h in range(2):
            slot = (2 * pair + h) % 4
            if pair >= 2:
                p_save(2 * pair + h, slot).wait()
            scores = mm(qp * masks[h].astype(BF), kp, 1, 1) + bias[...]
            e = jnp.exp(scores - jnp.max(scores, axis=1, keepdims=True))
            p = (e * (1.0 / jnp.sum(e, axis=1, keepdims=True))).astype(BF)
            probs[slot] = p
            p_save(2 * pair + h, slot).start()
            term = mm(p, vp) * masks[h]
            out = term if out is None else out + term
        ctx[:, pl.ds(pair * LANES, LANES)] = out.astype(BF)

    def project_context():
        def step(j, _):
            tile = at_tile(j, TILE)
            y = mm(ctx[...], w_in[3, :, tile]) + vecs[pl.ds(BO, 1), tile]
            n1[:, tile] = y + x[:, tile].astype(F32)
            return 0

        steps(0, d // TILE, step, 0)

    def first_norm():
        def norm(j, _):
            rows = at_tile(j, ROW)
            centred, scale = stats(n1[rows, :])
            n1[rows, :] = centred
            scale1[rows, :] = jnp.broadcast_to(scale, (ROW, LANES))
            first = centred * row(G1) + row(S1)
            low[rows, :] = first.astype(BF)
            res[rows, :] = first + row(BU)
            return 0

        steps(0, length // ROW, norm, 0)

    def inner(quarter, part):
        half = d // TILE // 2

        def step(j, _):
            tile = at_tile(j, TILE)
            u = mm(low[...], w_in[4 + quarter, :, tile]) + vecs[pl.ds(INNER + quarter, 1), tile]
            act, grad = gelu_parts(u)
            hidden[quarter, :, tile] = act.astype(BF)
            slope[quarter, :, tile] = grad.astype(BF)
            return 0

        steps(part * half, (part + 1) * half, step, 0)

    def outer(i):
        j, offset, width = outer_at[i]
        tile = pl.ds(j * TILE + offset, width)
        y = res[:, tile]
        for quarter in range(QUARTERS):
            y = y + mm(hidden[quarter], wu_in[j, pl.ds(quarter * d, d), pl.ds(offset, width)])
        res[:, tile] = y

    def second_norm():
        def step(j, sums):
            rows = at_tile(j, ROW)
            centred, scale = stats(res[rows, :])
            lay[rows, :] = (centred * row(G2) + row(S2)).astype(BF)
            g = seed[rows, :].astype(F32)
            grad = norm_back(g * row(G2), centred, scale)
            gsec[rows, :] = grad
            rounded = grad.astype(BF)
            gout[rows, :] = rounded
            return sums[0] + eighths(g * centred), sums[1] + eighths(g), sums[2] + eighths(rounded.astype(F32))

        zero = jnp.zeros((8, d), F32)
        sums = steps(0, length // ROW, step, (zero, zero, zero))
        for i, s in enumerate(sums):
            part[pl.ds(i, 1), :] = jnp.sum(s, axis=0, keepdims=True)

    greet(me)
    tokens = Exchange(me, x, tok, a_sems, 0, False)
    seeds = Exchange(me, seed, cot, a_sems, 1, False)
    part[...] = jnp.zeros_like(part)
    mask()
    seen = set()

    def need(*us):
        for u in us:
            if u not in seen:
                seen.add(u)
                pieces[u].wait()

    for op, *at in FORWARD_ORDER:
        i = at[0] if at else 0
        if op == "ST":
            units[i].start()
        elif op == "R":
            units[i].hop(at[1])
        elif op == "SP":
            units[i].spread()
        elif op == "CX":
            units[i].cross()
        elif op == "CO":
            units[i].corner()
        elif op == "WH":
            units[i].whole()
            if pieces[i] is not None:
                pieces[i].start()
        elif op in ("TK", "SD"):
            (tokens if op == "TK" else seeds).start(*at)
        elif op == "UN":
            unpack()
            save(vecs, vec_out)
        elif op == "QP":
            if i == 0:
                tokens.wait()
                save(x, x_out)
                need(0, 2)
            else:
                need(2 + i)
            project(i)
            save((q, k, v)[i], (q_out, k_out, v_out)[i])
        elif op == "AT":
            attend(i)
            if i == 7:
                save(ctx, ctx_out)
        elif op == "F0":
            need(5)
            project_context()
        elif op == "FN":
            first_norm()
            for src, dst in ((n1, n1_out), (scale1, scale_out), (low, low_out)):
                save(src, dst)
        elif op == "IN":
            need(6 + i)
            inner(*at)
            if at == [QUARTERS - 1, 1]:
                save(hidden, hid_out)
                save(slope, slope_out)
        elif op == "OU":
            need(10 + i)
            outer(i)
        elif op == "N2":
            seeds.wait()
            second_norm()
            for src, dst in ((gsec, gsec_out), (gout, gout_out), (lay, lay_out), (part, part_out)):
                save(src, dst)
    for unit in units:
        unit.sent()
    tokens.sent()
    seeds.sent()
    for slot in range(4):
        p_save(12 + slot, slot).wait()
    for copy in saves:
        copy.wait()


def forward_all(tok, cot, labels, vec, weights):
    d = tok.shape[2]
    length = tok.shape[1] * LINE
    pairs = d // LANES
    quarter = weights[4].shape[1] // QUARTERS
    shape = jax.ShapeDtypeStruct
    bf, wide = shape((length, d), BF), shape((length, d), F32)
    heads = shape((pairs, length, LANES), BF)
    mlp = shape((QUARTERS, length, quarter), BF)
    outs = (
        [bf]
        + [shape((w.shape[0] * RING * LINE, w.shape[1]), BF) for w in weights]
        + [heads, heads, heads, shape((2 * pairs, length, length), BF), bf, bf]
        + [wide, shape((length, LANES), F32), mlp, mlp, wide, bf, bf, shape((24, d), F32), shape((8, d), F32)]
    )
    n = UNITS + 1 + 2
    dma = pltpu.SemaphoreType.DMA

    def vm(s):
        return pltpu.VMEM(s.shape, s.dtype)

    vmem = pl.BlockSpec(memory_space=pltpu.VMEM)
    return pl.pallas_call(
        forward_kernel,
        out_shape=outs,
        in_specs=[ANY, ANY, vmem] + [ANY] * 7,
        out_specs=[ANY] * len(outs),
        scratch_shapes=[
            vm(bf), vm(bf), pltpu.VMEM((vec.shape[0] * RING * LINE, LANES), BF), pltpu.VMEM((24, d), F32), pltpu.VMEM((8, d), F32),
            pltpu.VMEM((8, d, d), BF), pltpu.VMEM((QUARTERS, QUARTERS * quarter, d // QUARTERS), BF),
            vm(heads), vm(heads), vm(heads), pltpu.VMEM((length, length), F32), pltpu.VMEM((4, length, length), BF),
            vm(bf), vm(wide), pltpu.VMEM((length, LANES), F32), vm(bf), vm(mlp), vm(mlp), vm(wide), vm(wide), vm(bf), vm(bf),
            dma((n,)), dma((n, 6)), dma((n, 4)), dma((n, 4)), dma((n, 4)), dma((n, 4)), dma((n, 4)),
            dma((2, 4)), dma((2, 4)), dma((2,)), dma((n,)), dma((4,)), dma((16,)),
        ],
        compiler_params=pltpu.CompilerParams(collective_id=0, has_side_effects=True, vmem_limit_bytes=58 << 20),
        name="forward",
    )(tok, cot, labels, vec, *weights)


def backward_kernel(
    x_in, wq, wk, wv, wo, wi, wu, q_in, k_in, v_in, p_in, ctx_in, low_in,
    n1_in, scale_in, hid_in, slope_in, gsec_in, gout_in, lay_in, vec_in, part_in,
    lay_out, gtok_out, oq, ok, ov, oo, oi, ou, vec_out,
    from_core, half, plane, line, own, to_send, acc, zsum, ztot, vbuf, vrecv,
    hidden, gout, slope, ginner, gfirst, n1, scale1, low, dk, dv, probs, w_in, vecs, part, sums,
    credit, cs, cr, hs, hr, ps, pr, zs, zr, out_sem, vs, vr, a_send, a_recv, a_local, i_sem, w_sem, p_sem,
):
    me = Place()
    a_sems = (a_send, a_recv, a_local)
    length, d = gout.shape
    rows = d // RING
    q, k, v, x = hidden.at[0], hidden.at[1], hidden.at[2], hidden.at[3]
    gattn, gctx, ctx, gtok = slope.at[0], slope.at[1], slope.at[2], slope.at[3]
    dq = gout

    units = []

    def whole(ref):
        return lambda lo: ref[:, at_tile(lo, rows)]

    def tall(j):
        return lambda lo: hidden[lo // 2, :, pl.ds(pl.multiple_of(lax.rem(lo, 2) * (QUARTERS * rows) + j * rows, rows), rows)]

    for j in range(QUARTERS):
        units.append((tall(j), lambda at: gout[:, at], lambda o, w, j=j: ou.at[pl.ds(j * rows, rows), pl.ds(o, w)]))
    for j in range(QUARTERS):
        units.append((whole(low), lambda at, j=j: ginner[j, :, at], lambda o, w, j=j: oi.at[:, pl.ds(j * d + o, w)]))
    for left, right, out in ((ctx, gattn, oo), (x, dv, ov), (x, dk, ok), (x, dq, oq)):
        units.append((whole(left), lambda at, right=right: right[:, at], lambda o, w, out=out: out.at[:, pl.ds(o, w)]))
    parts, members = [], []
    for unit, count in enumerate(BACK_PARTS):
        members.append([])
        for i in range(count):
            members[unit].append(len(parts))
            parts.append((unit, i * (d // count), d // count))
    n = len(parts)

    def at_of(i):
        return pl.ds(parts[i][1], parts[i][2])

    def leads(i, slots):
        unit = parts[i][0]
        return members[unit - slots] if i == members[unit][0] and unit >= slots else ()

    core_slots, acc_slots, z_slots = from_core.shape[0], acc.shape[0], zsum.shape[0]

    def load(src, dst, i):
        return pltpu.make_async_copy(src, dst, i_sem.at[i])

    pieces = []
    for j in range(QUARTERS):
        pieces += [wu.at[pl.ds(j * d, d)], wi.at[:, pl.ds(j * d, d)]]
    pieces += [wo, wq, wk, wv]

    def w_load(i):
        return pltpu.make_async_copy(pieces[i], w_in.at[i % 3], w_sem.at[i % 3])

    def core_all(i):
        here = from_core.at[parts[i][0] % core_slots, :, :, at_of(i)]
        return send(here, here, cs.at[i], cr.at[i], me.at_c)

    def part_of(ref, i, *index):
        return ref.at[(parts[i][0] % ref.shape[0], *index, at_of(i))]

    low_rows, high_rows, all_rows = pl.ds(0, rows // 2), pl.ds(rows // 2, rows // 2), pl.ds(0, rows)

    def half_x(i):
        return send(part_of(acc, i, me.chip_d, low_rows), part_of(half, i, 0, low_rows), hs.at[i, 0], hr.at[i, 0], me.at_x)

    def half_y(i):
        return send(part_of(acc, i, me.chip_d, high_rows), part_of(half, i, 1, low_rows), hs.at[i, 1], hr.at[i, 1], me.at_y)

    def plane_x(i):
        return send(part_of(acc, i, me.chip_x, all_rows), part_of(plane, i, 0, all_rows), ps.at[i, 0], pr.at[i, 0], me.at_x)

    def plane_y(i):
        return send(part_of(acc, i, me.chip_y, all_rows), part_of(plane, i, 1, all_rows), ps.at[i, 1], pr.at[i, 1], me.at_y)

    end = (me.s == 0) | (me.s == 3)
    mid = (me.s == 1) | (me.s == 2)
    partner = me.along(me.s + 1 - 2 * lax.rem(me.s, 2))
    other = me.along(3 - me.s)

    def line_in(i):
        return send(part_of(zsum, i, all_rows), part_of(line, i, 0, all_rows), zs.at[i, 0], zr.at[i, 0], partner)

    def line_swap(i):
        return send(part_of(zsum, i, all_rows), part_of(line, i, 1, all_rows), zs.at[i, 0], zr.at[i, 1], other)

    def line_back(i):
        return send(part_of(ztot, i, all_rows), part_of(line, i, 0, all_rows), zs.at[i, 1], zr.at[i, 0], partner)

    def out_of(i):
        unit, offset, width = parts[i]
        return units[unit][2](offset, width)

    def out_mid(i):
        return pltpu.make_async_copy(part_of(ztot, i, all_rows), out_of(i), out_sem.at[i])

    def out_end(i):
        return pltpu.make_async_copy(part_of(line, i, 0, all_rows), out_of(i), out_sem.at[i])

    def wide(a):
        return a.astype(F32)

    def add(dst, a, b):
        dst[...] = (wide(a[...]) + wide(b[...])).astype(BF)

    def produce(i):
        unit = parts[i][0]
        left, right, _ = units[unit]
        at, slot = at_of(i), unit % 2
        for m in leads(i, 2):
            core_all(m).wait_send()
        if leads(i, core_slots):
            pl.semaphore_wait(credit, 1)

        def step(j, _):
            to_send[slot, j, :, at] = mm(left(2 * j + 1 - me.c), right(at), 0, 0).astype(BF)
            there = from_core.at[unit % core_slots, j, :, at]
            send(to_send.at[slot, j, :, at], there, cs.at[i], cr.at[i], me.at_c).start()
            return 0

        steps(0, 4, step, 0)

        def keep(j, _):
            own[slot, j, :, at] = mm(left(2 * j + me.c), right(at), 0, 0).astype(BF)
            return 0

        steps(0, 4, keep, 0)

    def s1(i):
        unit = parts[i][0]
        for m in leads(i, acc_slots):
            sent_acc(m)
        core_all(i).wait_recv()

        def step(j, _):
            here = (j, all_rows)
            add(part_of(acc, i, *here), part_of(own, i, *here), part_of(from_core, i, *here))
            return 0

        steps(0, 4, step, 0)
        half_x(i).start()
        half_y(i).start()
        if i == members[unit][-1] and unit + core_slots < len(units):
            pl.semaphore_signal(credit, inc=1, device_id=me.at_c, device_id_type=MESH)

    def s2(i):
        half_x(i).wait_recv()
        here = part_of(acc, i, me.chip_y, low_rows)
        add(here, here, part_of(half, i, 0, low_rows))
        plane_y(i).start()
        half_y(i).wait_recv()
        here = part_of(acc, i, me.chip_x, high_rows)
        add(here, here, part_of(half, i, 1, low_rows))
        plane_x(i).start()

    def s3(i):
        for m in leads(i, z_slots):
            pl.when(end)(lambda m=m: line_in(m).wait_send())
            pl.when(mid)(lambda m=m: line_swap(m).wait_send())
        plane_x(i).wait_recv()
        plane_y(i).wait_recv()
        got = wide(part_of(plane, i, 0, all_rows)[...]) + wide(part_of(plane, i, 1, all_rows)[...])
        part_of(zsum, i, all_rows)[...] = (wide(part_of(acc, i, me.chip, all_rows)[...]) + got).astype(BF)
        pl.when(end)(lambda: line_in(i).start())

    def z1(i):
        @pl.when(mid)
        def _():
            line_in(i).wait_recv()
            here = part_of(zsum, i, all_rows)
            add(here, here, part_of(line, i, 0, all_rows))
            line_swap(i).start()

    def z2(i):
        @pl.when(mid)
        def _():
            for m in leads(i, z_slots):
                line_back(m).wait_send()
                out_mid(m).wait()
            line_swap(i).wait_recv()
            add(part_of(ztot, i, all_rows), part_of(zsum, i, all_rows), part_of(line, i, 1, all_rows))
            line_back(i).start()
            out_mid(i).start()

    def z3(i):
        @pl.when(end)
        def _():
            line_back(i).wait_recv()
            out_end(i).start()

    def sent_acc(i):
        half_x(i).wait_send()
        half_y(i).wait_send()
        plane_x(i).wait_send()
        plane_y(i).wait_send()

    def v_swap(i, to):
        return send(vbuf.at[i], vrecv.at[i], vs.at[i], vr.at[i], to)

    v_to = (me.at_c, me.at_x, me.at_y)

    def v_step(i):
        if i == 0:
            vbuf[0] = sums[...]
            v_swap(0, v_to[0]).start()
        elif i < 4:
            v_swap(i - 1, v_to[i - 1]).wait_recv()
            vbuf[i] = vbuf[i - 1] + vrecv[i - 1]
            if i < 3:
                v_swap(i, v_to[i]).start()
            else:
                pl.when(end)(lambda: v_swap(3, partner).start())
        elif i == 4:

            @pl.when(mid)
            def _():
                v_swap(3, partner).wait_recv()
                vbuf[4] = vbuf[3] + vrecv[3]
                v_swap(4, other).start()

        elif i == 5:

            @pl.when(mid)
            def _():
                v_swap(4, other).wait_recv()
                vbuf[5] = vbuf[4] + vrecv[4]
                v_swap(5, partner).start()
                vec_out[...] = vbuf[5]

        elif i == 6:

            @pl.when(end)
            def _():
                v_swap(5, partner).wait_recv()
                vec_out[...] = vrecv[5]

    def put(i, value, tile=slice(None)):
        sums[pl.ds(i, 1), tile] = jnp.sum(value, axis=0, keepdims=True)

    def inner_grad(quarter, slot):
        def step(j, _):
            tile = at_tile(j, TILE)
            y = mm(gout[...], w_in[slot, tile, :], 1, 1) * wide(slope[quarter, :, tile])
            y = y.astype(BF)
            ginner[quarter, :, tile] = y
            put(8 + quarter, wide(y), tile)
            return 0

        steps(0, d // TILE, step, 0)

    def first_grad(quarter, slot):
        def step(j, _):
            tile = at_tile(j, TILE)
            gfirst[:, tile] = gfirst[:, tile] + mm(ginner[quarter], w_in[slot, tile, :], 1, 1)
            return 0

        steps(0, d // TILE, step, 0)

    def first_norm_back():
        gain = vecs[pl.ds(G1, 1), :]

        def step(j, carry):
            at = at_tile(j, ROW)
            g, centred = gfirst[at, :], n1[at, :]
            grad = norm_back(g * gain, centred, scale1[at, :1])
            gfirst[at, :] = grad
            rounded = grad.astype(BF)
            gattn[at, :] = rounded
            return carry[0] + eighths(g * centred), carry[1] + eighths(g), carry[2] + eighths(wide(rounded))

        zero = jnp.zeros((8, d), F32)
        gains, shifts, biases = steps(0, length // ROW, step, (zero, zero, zero))
        put(4, gains)
        put(5, shifts)
        put(2, biases)

    def context_grad(slot):
        def step(j, _):
            tile = at_tile(j, TILE)
            gctx[:, tile] = mm(gattn[...], w_in[slot, tile, :], 1, 1).astype(BF)
            return 0

        steps(0, d // TILE, step, 0)

    def p_load(pair, h, slot):
        return pltpu.make_async_copy(p_in.at[2 * pair + h], probs.at[slot, h], p_sem.at[slot, h])

    def attend_back(pair):
        slot = pair % 2
        if pair + 1 < d // LANES:
            for h in range(2):
                p_load(pair + 1, h, 1 - slot).start()
        masks = half_masks()
        at = pl.ds(pair * LANES, LANES)
        qp, kp, vp, gp = q[:, at], k[:, at], v[:, at], gctx[:, at]
        outs = None
        for h in range(2):
            p_load(pair, h, slot).wait()
            p = wide(probs[slot, h])
            g = mm(gp * masks[h].astype(BF), vp, 1, 1)
            w = p * g
            s = (w - p * jnp.sum(w, axis=1, keepdims=True)).astype(BF)
            got = (
                mm(s, kp) * (masks[h] * (1.0 / math.sqrt(HD))),
                mm(s, qp, 0, 0) * masks[h],
                mm(probs[slot, h], gp, 0, 0) * masks[h],
            )
            outs = got if outs is None else tuple(a + b for a, b in zip(outs, got))
        for ref, y, i in ((dq, outs[0], 0), (dk, outs[1], None), (dv, outs[2], 1)):
            y = y.astype(BF)
            ref[:, at] = y
            if i is not None:
                put(i, wide(y), at)

    def token_grad(j):
        tile = pl.ds(j * TILE, TILE)
        y = gfirst[:, tile]
        for ref, i in ((dq, 9), (dk, 10), (dv, 11)):
            y = y + mm(ref[...], w_in[i % 3, tile, :], 1, 1)
        gtok[:, tile] = y.astype(BF)

    for quarter in range(QUARTERS):
        load(hid_in.at[quarter], hidden.at[quarter], quarter).start()
    load(gout_in, gout, 4).start()
    w_load(0).start()
    load(slope_in, slope, 5).start()
    w_load(1).start()
    load(gsec_in, gfirst, 6).start()
    later = ((low_in, low, 7), (n1_in, n1, 8), (scale_in, scale1, 9), (vec_in, vecs, 10), (part_in, part, 11))
    for src, dst, i in later:
        load(src, dst, i).start()
    greet(me)
    lay_back = Exchange(me, lay_in, lay_out, a_sems, 0, True)
    tok_back = Exchange(me, gtok, gtok_out, a_sems, 1, True)
    for quarter in range(QUARTERS):
        load(hid_in.at[quarter], hidden.at[quarter], quarter).wait()
    load(gout_in, gout, 4).wait()
    sums[...] = jnp.zeros_like(sums)
    stages = {"P": produce, "S1": s1, "S2": s2, "S3": s3, "Z1": z1, "Z2": z2, "Z3": z3, "V": v_step, "AB": attend_back, "TG": token_grad}
    for op, *at in BACK_ORDER:
        i = at[0] if at else 0
        if op == "V" and i == 0:
            for row, j in ((0, 6), (1, 7), (2, 3)):
                sums[pl.ds(j, 1), :] = part[pl.ds(row, 1), :]
        if op in stages:
            stages[op](i)
        elif op in ("LO", "GT"):
            (lay_back if op == "LO" else tok_back).start(*at)
        elif op == "IG":
            if i == 0:
                load(slope_in, slope, 5).wait()
                load(gsec_in, gfirst, 6).wait()
                load(low_in, low, 7).wait()
            w_load(2 * i + 2).start()
            w_load(2 * i).wait()
            inner_grad(i, (2 * i) % 3)
        elif op == "FG":
            w_load(2 * i + 3).start()
            w_load(2 * i + 1).wait()
            first_grad(i, (2 * i + 1) % 3)
        elif op == "LD":
            for src, dst, j in ((q_in, q, 0), (k_in, k, 1), (v_in, v, 2)):
                for pair in range(d // LANES):
                    load(src.at[pair], dst.at[:, pl.ds(pair * LANES, LANES)], j).start()
            load(x_in, x, 3).start()
            load(ctx_in, ctx, 5).start()
            for h in range(2):
                p_load(0, h, 0).start()
        elif op == "LW":
            for dst, j in ((q, 0), (k, 1), (v, 2)):
                load(x_in, dst, j).wait()
            load(x_in, x, 3).wait()
            load(ctx_in, ctx, 5).wait()
        elif op == "NB":
            for src, dst, j in later[1:]:
                load(src, dst, j).wait()
            first_norm_back()
        elif op == "CG":
            w_load(10).start()
            w_load(8).wait()
            context_grad(8 % 3)
            w_load(11).start()
        elif op == "TW":
            for j in (9, 10, 11):
                w_load(j).wait()
    for unit in members[-2:]:
        for i in unit:
            core_all(i).wait_send()
    for unit in members[-acc_slots:]:
        for i in unit:
            sent_acc(i)
    for i in range(n):
        pl.when(end)(lambda i=i: out_end(i).wait())
    for unit in members[-z_slots:]:
        for i in unit:
            pl.when(end)(lambda i=i: line_in(i).wait_send())

            @pl.when(mid)
            def _(i=i):
                line_swap(i).wait_send()
                line_back(i).wait_send()
                out_mid(i).wait()

    for i in range(3):
        v_swap(i, v_to[i]).wait_send()
    pl.when(end)(lambda: v_swap(3, partner).wait_send())

    @pl.when(mid)
    def _():
        v_swap(4, other).wait_send()
        v_swap(5, partner).wait_send()

    for exchange in (lay_back, tok_back):
        exchange.wait()
        exchange.sent()


def backward_all(saved, block):
    length, d = saved[0].shape
    rows = d // RING
    units, n = len(BACK_PARTS), sum(BACK_PARTS)
    core_slots, acc_slots, z_slots = 3, 3, 3
    dma = pltpu.SemaphoreType.DMA
    shape = jax.ShapeDtypeStruct

    def vm(*s, dtype=BF):
        return pltpu.VMEM(s, dtype)

    split = shape((LINE, block, d), BF)
    sq = shape((rows, d), BF)
    sums = (16, d)
    outs = [split, split, sq, sq, sq, sq, shape((rows, QUARTERS * d), BF), shape((QUARTERS * rows, d), BF), shape(sums, F32)]
    mat = (length, d)
    mlp = (QUARTERS, length, d)
    return pl.pallas_call(
        backward_kernel,
        out_shape=outs,
        in_specs=[ANY] * len(saved),
        out_specs=[ANY] * 8 + [pl.BlockSpec(memory_space=pltpu.VMEM)],
        scratch_shapes=[
            vm(core_slots, 4, rows, d), vm(units, 2, rows // 2, d), vm(units, 2, rows, d), vm(units, 2, rows, d),
            vm(2, 4, rows, d), vm(2, 4, rows, d), vm(acc_slots, 4, rows, d), vm(z_slots, rows, d), vm(z_slots, rows, d),
            vm(6, *sums, dtype=F32), vm(6, *sums, dtype=F32),
            vm(*mlp), vm(*mat), vm(*mlp), vm(*mlp), vm(*mat, dtype=F32), vm(*mat, dtype=F32), vm(length, LANES, dtype=F32), vm(*mat),
            vm(*mat), vm(*mat), vm(2, 2, length, length), vm(3, d, d), vm(24, d, dtype=F32), vm(8, d, dtype=F32), vm(*sums, dtype=F32),
            pltpu.SemaphoreType.REGULAR,
            dma((n,)), dma((n,)), dma((n, 2)), dma((n, 2)), dma((n, 2)), dma((n, 2)), dma((n, 2)), dma((n, 2)),
            dma((n,)), dma((6,)), dma((6,)), dma((2, 4)), dma((2, 4)), dma((2,)), dma((12,)), dma((3,)), dma((2, 2)),
        ],
        compiler_params=pltpu.CompilerParams(collective_id=1, has_side_effects=True, vmem_limit_bytes=62 << 20),
        name="backward",
    )(*saved)


def pack_kernel(*refs):
    out = refs[-1]
    rows = []
    for ref in refs[:-1]:
        row = ref[...].astype(F32).reshape(1, ref.shape[0])
        if ref.shape[0] < LANES:
            row = jnp.concatenate([row, jnp.zeros((1, LANES - ref.shape[0]), F32)], axis=1)
        rows.append(row)
    rows.append(jnp.zeros((out.shape[0] - len(rows), LANES), F32))
    out[...] = jnp.concatenate(rows, axis=0).astype(BF)


def pack(vectors):
    vmem = pl.BlockSpec(memory_space=pltpu.VMEM)
    return pl.pallas_call(
        pack_kernel,
        in_specs=[vmem] * len(vectors),
        out_specs=vmem,
        out_shape=jax.ShapeDtypeStruct((16, LANES), BF),
        name="pack",
    )(*vectors)


def finish_kernel(lay, gtok, *rest):
    mats, sums, outs = rest[:6], rest[6], rest[7:]
    outs[0][...] = lay[...]
    outs[1][...] = gtok[...]
    for src, dst in zip(mats, outs[2:8]):
        dst[...] = src[...].astype(F32)
    lo = lax.axis_index("grp")
    for i, dst in zip((0, 1, 2, 8, 3, 4, 5, 6, 7), outs[8:]):
        n = dst.shape[0]
        if i < 8:
            row, column = i, lo * n
        else:
            per = sums.shape[1] // n
            row, column = 8 + lo // per, lax.rem(lo, per) * n
        dst[...] = sums[pl.ds(row, 1), pl.ds(pl.multiple_of(column, LANES), n)].reshape(n)


def finish(out):
    count = out[0].shape[0]
    shape = jax.ShapeDtypeStruct

    def rows(a, dtype):
        block = (a.shape[0] // count,) + a.shape[1:]
        return pl.BlockSpec(block, lambda i: (i,) + (0,) * (len(block) - 1)), shape(a.shape, dtype)

    d = out[8].shape[1]
    ins = [rows(a, a.dtype)[0] for a in out[:8]] + [pl.BlockSpec(out[8].shape, lambda i: (0, 0))]
    big = [rows(a, a.dtype if k < 2 else F32) for k, a in enumerate(out[:8])]
    sizes = [d // RING] * 3 + [QUARTERS * d // RING] + [d // RING] * 5
    small = [(pl.BlockSpec((n,), lambda i: (0,)), shape((n,), F32)) for n in sizes]
    specs, shapes = zip(*(big + small))
    return tuple(
        pl.pallas_call(
            finish_kernel,
            grid=(count,),
            in_specs=ins,
            out_specs=list(specs),
            out_shape=list(shapes),
            compiler_params=pltpu.CompilerParams(vmem_limit_bytes=62 << 20),
            name="finish",
        )(*out)
    )


def local(tokens, labels, *rest):
    weights, vectors, cotangent = rest[:6], rest[6:15], rest[15]
    groups = lax.axis_size("grp") // RING
    g, s = lax.axis_index("grp"), lax.axis_index("seq")
    lo = lax.rem(g, RING)
    if groups > 1:
        def regroup(w):
            full = lax.all_gather(w, ("grp", "seq"), axis=0, tiled=True)
            n = full.shape[0] // (RING * LINE)
            return lax.dynamic_slice_in_dim(full, (lo * LINE + s) * n, n, 0)

        weights = tuple(regroup(w) for w in weights)
        vectors = tuple(regroup(v) for v in vectors)
    packed = pack(vectors)
    saved = forward_all(tokens, cotangent, labels, packed, weights)
    out = backward_all(saved, tokens.shape[1])
    if groups == 1:
        return finish(out)
    layer_out, grad_tokens = out[:2]
    mats = [m.astype(F32) for m in out[2:8]]
    vec = out[8]
    flat = [vec[i] for i in range(8)]
    flat.insert(3, vec[8 : 8 + QUARTERS].reshape(-1))
    same = [[l + RING * h for h in range(groups)] for l in range(RING)]
    eight = [[l + RING * h for l in range(RING)] for h in range(groups)]

    def rejoin(m):
        m = lax.psum(m, "grp", axis_index_groups=same)
        m = lax.all_gather(m, "grp", axis=0, tiled=True, axis_index_groups=eight)
        n = m.shape[0] // (RING * groups)
        return lax.dynamic_slice_in_dim(m, g * n, n, 0)

    mats = [rejoin(m) for m in mats]
    flat = [lax.psum(v, "grp", axis_index_groups=same) for v in flat]
    flat = [lax.dynamic_slice_in_dim(v, g * (v.shape[0] // (RING * groups)), v.shape[0] // (RING * groups), 0) for v in flat]
    return (layer_out, grad_tokens, *mats, *flat)


def solution(mesh):
    both = ("grp", "seq")
    rows = P("grp", "seq", None)
    return jax.shard_map(
        local,
        mesh=mesh,
        in_specs=(rows, P("grp", None)) + (P(both, None),) * 6 + (P(both),) * 9 + (rows,),
        out_specs=(rows, rows) + (P("grp", None),) * 6 + (P("grp"),) * 9,
        check_vma=False,
    )
```

```python
import functools
import math

import jax
import jax.numpy as jnp
from jax import lax
from jax.experimental import pallas as pl
from jax.experimental.pallas import tpu as pltpu
from jax.sharding import PartitionSpec as P

H = 16
HD = 64
LINE = 4
RING = 8
UNITS = 12
QUARTERS = 4
LANES = 128
MESH = pl.DeviceIdType.MESH
BF = jnp.bfloat16
F32 = jnp.float32
ANY = pl.BlockSpec(memory_space=pl.ANY)


class Place:
    def __init__(self):
        self.g = lax.axis_index("grp")
        self.s = lax.axis_index("seq")
        self.lo = lax.rem(self.g, RING)
        self.c = lax.rem(self.lo, 2)
        xb = lax.rem(self.lo // 2, 2)
        yb = self.lo // 4
        self.dc, self.dx, self.dy = 1 - 2 * self.c, 2 - 4 * xb, 4 - 8 * yb
        self.at_c = (self.g + self.dc, self.s)
        self.at_x = (self.g + self.dx, self.s)
        self.at_y = (self.g + self.dy, self.s)
        self.chip = self.lo // 2
        self.chip_x = self.chip + 1 - 2 * xb
        self.chip_y = self.chip + 2 - 4 * yb
        self.chip_d = self.chip_x + 2 - 4 * yb

    def along(self, t):
        return (self.g, t)


def send(src, dst, send_sem, recv_sem, to):
    return pltpu.make_async_remote_copy(
        src_ref=src, dst_ref=dst, send_sem=send_sem, recv_sem=recv_sem, device_id=to, device_id_type=MESH
    )


def greet(me):
    barrier = pltpu.get_barrier_semaphore()

    def signal(to):
        pl.semaphore_signal(barrier, inc=1, device_id=to, device_id_type=MESH)

    for to in (me.at_c, me.at_x, me.at_y):
        signal(to)
    for t in range(LINE):
        pl.when(me.s != t)(lambda t=t: signal(me.along(t)))
    pl.semaphore_wait(barrier, 3 + LINE - 1)


class Exchange:
    def __init__(self, me, whole, split, sems, index, back):
        self.me, self.whole, self.split, self.index, self.back = me, whole, split, index, back
        self.send_sem, self.recv_sem, self.local_sem = sems

    def rows(self, t, part=0, parts=1):
        n = self.split.shape[1]
        return self.whole.at[pl.ds(t * n + part * (n // parts), n // parts)]

    def ends(self, t, part=0, parts=1):
        n = self.split.shape[1] // parts
        here = pl.ds(part * n, n)
        if self.back:
            return self.rows(t, part, parts), self.split.at[self.me.s, here]
        return self.split.at[t, here], self.rows(self.me.s, part, parts)

    def copy(self, t, part=0, parts=1):
        src, dst = self.ends(t, part, parts)
        return send(src, dst, self.send_sem.at[self.index, t], self.recv_sem.at[self.index, self.me.s], self.me.along(t))

    def landed(self, t):
        dst = self.split.at[t] if self.back else self.rows(t)
        return send(dst, dst, self.send_sem.at[self.index, t], self.recv_sem.at[self.index, t], self.me.along(t))

    def own(self):
        src, dst = self.ends(self.me.s)
        return pltpu.make_async_copy(src, dst, self.local_sem.at[self.index])

    def start(self, distance, part=0, parts=1):
        s = self.me.s
        if distance == 1 and part == 0:
            self.own().start()
        for t in range(LINE):
            pl.when((s - t == distance) | (t - s == distance))(lambda t=t: self.copy(t, part, parts).start())

    def wait(self):
        self.own().wait()
        for t in range(LINE):
            pl.when(self.me.s != t)(lambda t=t: self.landed(t).wait_recv())

    def sent(self):
        for t in range(LINE):
            pl.when(self.me.s != t)(lambda t=t: self.copy(t).wait_send())


class Gather:
    def __init__(self, me, src, dst, rows, sems, u, fine):
        self.me, self.src, self.dst, self.rows, self.u, self.fine = me, src, dst, rows, u, fine
        self.local, self.zs, self.zr, self.xs, self.xr, self.cs, self.cr = sems

    def own(self):
        me = self.me
        return pltpu.make_async_copy(self.src, self.dst((me.lo * LINE + me.s) * self.rows, self.rows), self.local.at[self.u])

    def shard(self, source):
        return self.dst((self.me.lo * LINE + source) * self.rows, self.rows)

    def z_send(self, source, step, slot):
        there = self.shard(source)
        src = self.src if slot < 2 else there
        return send(src, there, self.zs.at[self.u, slot], self.zr.at[self.u, source], self.me.along(self.me.s + step))

    def z_recv(self, source):
        there = self.shard(source)
        send(there, there, self.zs.at[self.u, 0], self.zr.at[self.u, source], self.me.at_c).wait_recv()

    def xy_shard(self, source, own):
        there = self.shard(source)
        for k, to in ((0, self.me.at_x), (1, self.me.at_y)):
            send(self.src if own else there, there, self.xs.at[self.u, k], self.xr.at[self.u, k], to).start()

    def start(self):
        me = self.me
        self.own().start()
        pl.when(me.s < LINE - 1)(lambda: self.z_send(me.s, 1, 0).start())
        pl.when(me.s > 0)(lambda: self.z_send(me.s, -1, 1).start())
        if self.fine:
            self.xy_shard(me.s, True)

    def hop(self, h):
        me = self.me

        @pl.when(me.s >= h)
        def _():
            self.z_recv(me.s - h)
            if h < LINE - 1:
                pl.when(me.s < LINE - 1)(lambda: self.z_send(me.s - h, 1, 2 * h).start())
            if self.fine:
                self.xy_shard(me.s - h, False)

        @pl.when(me.s < LINE - h)
        def _():
            self.z_recv(me.s + h)
            if h < LINE - 1:
                pl.when(me.s > 0)(lambda: self.z_send(me.s + h, -1, 2 * h + 1).start())
            if self.fine:
                self.xy_shard(me.s + h, False)

    def block(self, lo, half=None):
        rows = self.rows * LINE
        if half is None:
            return self.dst(lo * rows, rows)
        return self.dst(lo * rows + half * (rows // 2), rows // 2)

    def x1(self, lo):
        return send(self.block(lo), self.block(lo), self.xs.at[self.u, 0], self.xr.at[self.u, 0], self.me.at_x)

    def y1(self, lo):
        return send(self.block(lo), self.block(lo), self.xs.at[self.u, 1], self.xr.at[self.u, 1], self.me.at_y)

    def x2(self, lo):
        return send(self.block(lo, 1), self.block(lo, 1), self.xs.at[self.u, 2], self.xr.at[self.u, 2], self.me.at_x)

    def y2(self, lo):
        return send(self.block(lo, 0), self.block(lo, 0), self.xs.at[self.u, 3], self.xr.at[self.u, 3], self.me.at_y)

    def core(self, lo, k):
        return send(self.block(lo), self.block(lo), self.cs.at[self.u, k], self.cr.at[self.u, k], self.me.at_c)

    def spread(self):
        me = self.me
        self.own().wait()
        if not self.fine:
            self.x1(me.lo).start()
            self.y1(me.lo).start()
        self.core(me.lo, 0).start()

    def cross(self):
        me = self.me
        lo_x, lo_y = me.lo + me.dx, me.lo + me.dy
        self.x1(lo_x).wait_recv()
        self.y2(lo_x).start()
        self.core(lo_x, 1).start()
        self.y1(lo_y).wait_recv()
        self.x2(lo_y).start()
        self.core(lo_y, 2).start()

    def corner(self):
        me = self.me
        lo_d = me.lo + me.dx + me.dy
        self.x2(lo_d).wait_recv()
        self.y2(lo_d).wait_recv()
        self.core(lo_d, 3).start()

    def whole(self):
        me = self.me
        for k, lo in enumerate((me.lo, me.lo + me.dx, me.lo + me.dy, me.lo + me.dx + me.dy)):
            self.core(lo + me.dc, k).wait_recv()

    def sent(self):
        me = self.me
        for h in range(LINE - 1):
            right = (me.s >= h) & (me.s < LINE - 1)
            left = (me.s < LINE - h) & (me.s > 0)
            pl.when(right)(lambda h=h: self.z_send(me.s - h, 1, 2 * h).wait_send())
            pl.when(left)(lambda h=h: self.z_send(me.s + h, -1, 2 * h + 1).wait_send())
        self.x1(me.lo).wait_send()
        self.y1(me.lo).wait_send()
        self.x2(me.lo + me.dy).wait_send()
        self.y2(me.lo + me.dx).wait_send()
        for k, lo in enumerate((me.lo, me.lo + me.dx, me.lo + me.dy, me.lo + me.dx + me.dy)):
            self.core(lo, k).wait_send()


def rows_of(ref, columns=None):
    if columns is None:
        return lambda row, n: ref.at[pl.ds(row, n)]
    return lambda row, n: ref.at[pl.ds(row, n), columns]


def rows_of(ref, columns=None):
    if columns is None:
        return lambda row, n: ref.at[pl.ds(row, n)]
    return lambda row, n: ref.at[pl.ds(row, n), columns]


def mm(a, b, ca=1, cb=0):
    return lax.dot_general(a, b, (((ca,), (cb,)), ((), ())), preferred_element_type=F32)


def at_tile(j, tile):
    if isinstance(j, int):
        return pl.ds(j * tile, tile)
    return pl.ds(pl.multiple_of(j * tile, tile), tile)


def steps(first, last, step, carry=0):
    for j in range(first, last):
        carry = step(j, carry)
    return carry


def iota(shape, dim):
    return lax.broadcasted_iota(jnp.int32, shape, dim)


def half_masks():
    low = (iota((1, LANES), 1) < HD).astype(F32)
    return low, 1.0 - low


def gelu_parts(u):
    t = 1.0 / (1.0 + (0.3275911 * 0.7071067811865476) * jnp.abs(u))
    poly = t * (0.254829592 + t * (-0.284496736 + t * (1.421413741 + t * (-1.453152027 + t * 1.061405429))))
    bell = jnp.exp(-0.5 * u * u)
    tail = 0.5 * poly * bell
    cdf = jnp.where(u >= 0.0, 1.0 - tail, tail)
    return u * cdf, cdf + u * (bell * 0.3989422804014327)


def stats(r):
    centered = r - jnp.mean(r, axis=-1, keepdims=True)
    scale = lax.rsqrt(jnp.mean(centered * centered, axis=-1, keepdims=True) + 1e-06)
    return centered * scale, scale


def norm_back(u, n, scale):
    return (u - jnp.mean(u, axis=-1, keepdims=True) - n * jnp.mean(u * n, axis=-1, keepdims=True)) * scale


def eighths(x):
    return jnp.sum(x.reshape(x.shape[0] // 8, 8, x.shape[1]), axis=0)


FINE = (0, 2, 3, 4)
OUTER_PARTS = (1, 1, 1, 1)
FORWARD_ORDER = (
    ("ST", 0), ("ST", 1), ("ST", 2), ("ST", 3), ("ST", 4), ("ST", 5), ("R", 0, 1), ("R", 1, 1), ("R", 2, 1), ("R", 3, 1), ("R", 4, 1),
    ("R", 5, 1), ("R", 0, 2), ("R", 1, 2), ("R", 2, 2), ("R", 3, 2), ("R", 4, 2), ("R", 5, 2), ("R", 0, 3), ("SP", 0), ("R", 1, 3),
    ("SP", 1), ("R", 2, 3), ("SP", 2), ("R", 3, 3), ("SP", 3), ("CX", 0), ("ST", 6), ("R", 4, 3), ("SP", 4), ("CX", 2), ("ST", 7),
    ("R", 5, 3), ("CX", 1), ("SP", 5), ("ST", 8), ("CX", 3), ("ST", 9), ("R", 6, 1), ("CO", 0), ("R", 7, 1), ("CX", 4), ("WH", 0),
    ("ST", 10), ("R", 8, 1), ("CO", 2), ("CO", 1), ("R", 9, 1), ("WH", 2), ("WH", 1), ("R", 6, 2), ("TK", 2, 0, 4), ("UN",),
    ("R", 7, 2), ("R", 10, 1), ("CX", 5), ("R", 8, 2), ("R", 9, 2), ("CO", 3), ("R", 6, 3), ("SP", 6), ("TK", 3, 0, 4), ("WH", 3),
    ("TK", 1, 0, 4), ("CO", 4), ("TK", 2, 1, 4), ("WH", 4), ("TK", 3, 1, 4), ("R", 7, 3), ("SP", 7), ("CO", 5), ("TK", 1, 1, 4),
    ("R", 10, 2), ("WH", 5), ("R", 8, 3), ("SP", 8), ("TK", 2, 2, 4), ("R", 9, 3), ("SP", 9), ("TK", 3, 2, 4), ("CX", 6),
    ("TK", 1, 2, 4), ("TK", 2, 3, 4), ("TK", 3, 3, 4), ("CX", 7), ("TK", 1, 3, 4), ("R", 10, 3), ("SP", 10), ("ST", 11), ("ST", 12),
    ("CX", 8), ("ST", 13), ("SD", 2, 0, 4), ("QP", 0), ("CX", 9), ("R", 11, 1), ("QP", 1), ("R", 12, 1), ("SD", 3, 0, 4), ("QP", 2),
    ("R", 13, 1), ("CO", 6), ("AT", 0), ("CO", 7), ("WH", 6), ("SD", 1, 0, 4), ("AT", 1), ("R", 11, 2), ("WH", 7), ("AT", 2),
    ("R", 12, 2), ("SD", 2, 1, 4), ("AT", 3), ("CX", 10), ("AT", 4), ("R", 13, 2), ("SD", 3, 1, 4), ("AT", 5), ("R", 11, 3), ("SP", 11),
    ("CO", 8), ("AT", 6), ("R", 12, 3), ("SP", 12), ("CO", 9), ("SD", 1, 1, 4), ("WH", 8), ("AT", 7), ("F0",), ("R", 13, 3), ("SP", 13),
    ("CO", 10), ("WH", 9), ("SD", 2, 2, 4), ("FN",), ("IN", 0, 0), ("WH", 10), ("SD", 3, 2, 4), ("IN", 0, 1), ("CX", 11), ("IN", 1, 0),
    ("SD", 1, 2, 4), ("IN", 1, 1), ("IN", 2, 0), ("CX", 12), ("SD", 2, 3, 4), ("IN", 2, 1), ("IN", 3, 0), ("SD", 3, 3, 4), ("IN", 3, 1),
    ("CX", 13), ("OU", 0), ("CO", 11), ("SD", 1, 3, 4), ("WH", 11), ("CO", 12), ("OU", 1), ("WH", 12), ("CO", 13), ("OU", 2),
    ("WH", 13), ("OU", 3), ("N2",),
)
BACK_PARTS = (1, 1, 1, 1, 1, 1, 1, 1, 1, 1, 1, 1)
BACK_ORDER = (
    ("LO", 2, 0, 4), ("LO", 2, 1, 4), ("LO", 2, 2, 4), ("P", 0), ("P", 1), ("IG", 0), ("S1", 0), ("FG", 0), ("S1", 1), ("LO", 2, 3, 4),
    ("IG", 1), ("LO", 3, 0, 4), ("P", 2), ("S2", 0), ("LO", 3, 1, 4), ("FG", 1), ("LO", 3, 2, 4), ("IG", 2), ("S2", 1), ("S1", 2),
    ("LO", 3, 3, 4), ("LO", 1, 0, 4), ("FG", 2), ("LO", 1, 1, 4), ("IG", 3), ("LO", 1, 2, 4), ("S3", 0), ("FG", 3), ("P", 3),
    ("LO", 1, 3, 4), ("LD",), ("NB",), ("P", 4), ("S1", 3), ("S3", 1), ("CG",), ("S2", 2), ("LW",), ("AB", 0), ("S1", 4), ("S2", 3),
    ("Z1", 0), ("AB", 1), ("AB", 2), ("AB", 3), ("S3", 2), ("Z1", 1), ("AB", 4), ("Z2", 0), ("S2", 4), ("AB", 5), ("AB", 6), ("AB", 7),
    ("S3", 3), ("Z1", 2), ("Z2", 1), ("V", 0), ("TW",), ("TG", 0), ("Z3", 0), ("P", 5), ("P", 6), ("S3", 4), ("V", 1), ("TG", 1),
    ("S1", 5), ("Z1", 3), ("Z2", 2), ("Z3", 1), ("TG", 2), ("S1", 6), ("V", 2), ("TG", 3), ("GT", 2, 0, 4), ("GT", 3, 0, 4),
    ("GT", 1, 0, 4), ("P", 7), ("S2", 5), ("Z1", 4), ("V", 3), ("P", 8), ("S2", 6), ("Z2", 3), ("S1", 7), ("Z3", 2), ("P", 9), ("V", 4),
    ("GT", 2, 1, 4), ("GT", 3, 1, 4), ("S3", 5), ("S1", 8), ("GT", 1, 1, 4), ("V", 5), ("GT", 2, 2, 4), ("V", 6), ("GT", 3, 2, 4),
    ("Z2", 4), ("S3", 6), ("S1", 9), ("Z3", 3), ("Z1", 5), ("S2", 7), ("P", 10), ("S2", 8), ("P", 11), ("GT", 1, 2, 4), ("GT", 2, 3, 4),
    ("S2", 9), ("GT", 3, 3, 4), ("GT", 1, 3, 4), ("Z1", 6), ("S3", 7), ("S1", 10), ("Z2", 5), ("Z3", 4), ("S3", 8), ("S1", 11),
    ("Z1", 7), ("S2", 10), ("Z2", 6), ("S3", 9), ("Z1", 8), ("Z3", 5), ("S2", 11), ("Z2", 7), ("Z3", 6), ("Z1", 9), ("S3", 10),
    ("Z2", 8), ("Z3", 7), ("S3", 11), ("Z1", 10), ("Z2", 9), ("Z3", 8), ("Z1", 11), ("Z2", 10), ("Z3", 9), ("Z2", 11), ("Z3", 10),
    ("Z3", 11),
)
ROW = 64
TILE = 256
BQ, BV, BO, BI, BU, G1, S1, G2, S2 = range(9)
INNER = 16


def forward_kernel(
    tok, cot, labels, vec, wq, wk, wv, wo, wi, wu,
    x_out, wq_all, wk_all, wv_all, wo_all, wi_all, wu_all, q_out, k_out, v_out, p_out, ctx_out, low_out,
    n1_out, scale_out, hid_out, slope_out, gsec_out, gout_out, lay_out, vec_out, part_out,
    x, seed, packed, vecs, part, w_in, wu_in, q, k, v, bias, probs, ctx, n1, scale1, low, hidden, slope, res, gsec, gout, lay,
    local, zs, zr, xs, xr, cs, cr, a_send, a_recv, a_local, w_sem, p_sem, o_sem,
):
    me = Place()
    sems = (local, zs, zr, xs, xr, cs, cr)
    a_sems = (a_send, a_recv, a_local)
    d = x.shape[1]
    length = x.shape[0]
    units, pieces = [], []

    def add(src, ref, columns, to=None):
        src = src if columns is None else src.at[:, columns]
        u = len(units)
        units.append(Gather(me, src, rows_of(ref, columns), src.shape[0], sems, u, u in FINE))
        pieces.append(None if to is None else pltpu.make_async_copy(ref if columns is None else ref.at[:, columns], to, w_sem.at[u]))

    add(wq, wq_all, pl.ds(0, d // 2), w_in.at[0, :, pl.ds(0, d // 2)])
    add(vec, packed, None)
    add(wq, wq_all, pl.ds(d // 2, d // 2), w_in.at[0, :, pl.ds(d // 2, d // 2)])
    for i, (src, ref) in enumerate(((wk, wk_all), (wv, wv_all), (wo, wo_all))):
        add(src, ref, None, w_in.at[1 + i])
    width = wi.shape[1] // QUARTERS
    for j in range(QUARTERS):
        add(wi, wi_all, pl.ds(j * width, width), w_in.at[4 + j])
    outer_at = []
    for j, parts in enumerate(OUTER_PARTS):
        width = d // QUARTERS // parts
        for i in range(parts):
            add(wu, wu_all, pl.ds(j * TILE + i * width, width), wu_in.at[j, :, pl.ds(i * width, width)])
            outer_at.append((j, i * width, width))
    n = len(units)
    saves = []

    def save(src, dst):
        copy = pltpu.make_async_copy(src, dst, o_sem.at[len(saves)])
        copy.start()
        saves.append(copy)

    def row(i):
        return vecs[pl.ds(i, 1), :]

    def unpack():
        p = packed[...]
        piece = d // (RING * LINE)
        spread = (iota((LANES, d), 1) % piece == iota((LANES, d), 0)).astype(BF)
        wide = mm(p, spread).reshape(RING * LINE, 16, d)
        here = iota((RING * LINE, 1, d), 0) == iota((RING * LINE, 1, d), 2) // piece
        vecs[pl.ds(0, 16), :] = jnp.sum(jnp.where(here, wide, 0.0), axis=0)
        p = p.astype(F32).reshape(RING * LINE, 16, LANES)
        p = jnp.sum(jnp.where(iota(p.shape, 1) == BI, p, 0.0), axis=1).astype(BF)
        spread = (iota((LANES, d), 1) % LANES == iota((LANES, d), 0)).astype(BF)
        per = RING * LINE // QUARTERS
        wide = mm(p, spread).reshape(QUARTERS, per, d)
        here = iota((1, per, d), 1) == iota((1, per, d), 2) // LANES
        inner = jnp.sum(jnp.where(here, wide, 0.0), axis=1)
        vecs[pl.ds(INNER, 8), :] = jnp.concatenate([inner, jnp.zeros_like(inner)], axis=0)

    def mask():
        own = labels[pl.ds(me.s, 1), :]
        marks = jnp.where(own != 0, own, -1 - iota(own.shape, 1)).astype(F32)
        down = jnp.broadcast_to(marks, (LANES, length)).T[:, :1]
        bias[...] = jnp.where(down == marks, 0.0, -1e30)

    def project(slot):
        out, b, factor = ((q, BQ, 1.0 / math.sqrt(HD)), (k, None, None), (v, BV, None))[slot]

        def step(j, _):
            tile = at_tile(j, TILE)
            y = mm(x[...], w_in[slot, :, tile])
            if b is not None:
                y = y + vecs[pl.ds(b, 1), tile]
            y = y.astype(BF)
            if factor is not None:
                y = (y.astype(F32) * factor).astype(BF)
            out[2 * j] = y[:, :LANES]
            out[2 * j + 1] = y[:, LANES:]
            return 0

        steps(0, d // TILE, step, 0)

    def p_save(h, slot):
        return pltpu.make_async_copy(probs.at[slot], p_out.at[h], p_sem.at[slot])

    def attend(pair):
        masks = half_masks()
        kp, vp, qp = k[pair], v[pair], q[pair]
        out = None
        for h in range(2):
            slot = (2 * pair + h) % 4
            if pair >= 2:
                p_save(2 * pair + h, slot).wait()
            scores = mm(qp * masks[h].astype(BF), kp, 1, 1) + bias[...]
            e = jnp.exp(scores - jnp.max(scores, axis=1, keepdims=True))
            p = (e * (1.0 / jnp.sum(e, axis=1, keepdims=True))).astype(BF)
            probs[slot] = p
            p_save(2 * pair + h, slot).start()
            term = mm(p, vp) * masks[h]
            out = term if out is None else out + term
        ctx[:, pl.ds(pair * LANES, LANES)] = out.astype(BF)

    def project_context():
        def step(j, _):
            tile = at_tile(j, TILE)
            y = mm(ctx[...], w_in[3, :, tile]) + vecs[pl.ds(BO, 1), tile]
            n1[:, tile] = y + x[:, tile].astype(F32)
            return 0

        steps(0, d // TILE, step, 0)

    def first_norm():
        def norm(j, _):
            rows = at_tile(j, ROW)
            centred, scale = stats(n1[rows, :])
            n1[rows, :] = centred
            scale1[rows, :] = jnp.broadcast_to(scale, (ROW, LANES))
            first = centred * row(G1) + row(S1)
            low[rows, :] = first.astype(BF)
            res[rows, :] = first + row(BU)
            return 0

        steps(0, length // ROW, norm, 0)

    def inner(quarter, part):
        half = d // TILE // 2

        def step(j, _):
            tile = at_tile(j, TILE)
            u = mm(low[...], w_in[4 + quarter, :, tile]) + vecs[pl.ds(INNER + quarter, 1), tile]
            act, grad = gelu_parts(u)
            hidden[quarter, :, tile] = act.astype(BF)
            slope[quarter, :, tile] = grad.astype(BF)
            return 0

        steps(part * half, (part + 1) * half, step, 0)

    def outer(i):
        j, offset, width = outer_at[i]
        tile = pl.ds(j * TILE + offset, width)
        y = res[:, tile]
        for quarter in range(QUARTERS):
            y = y + mm(hidden[quarter], wu_in[j, pl.ds(quarter * d, d), pl.ds(offset, width)])
        res[:, tile] = y

    def second_norm():
        def step(j, sums):
            rows = at_tile(j, ROW)
            centred, scale = stats(res[rows, :])
            lay[rows, :] = (centred * row(G2) + row(S2)).astype(BF)
            g = seed[rows, :].astype(F32)
            grad = norm_back(g * row(G2), centred, scale)
            gsec[rows, :] = grad
            rounded = grad.astype(BF)
            gout[rows, :] = rounded
            return sums[0] + eighths(g * centred), sums[1] + eighths(g), sums[2] + eighths(rounded.astype(F32))

        zero = jnp.zeros((8, d), F32)
        sums = steps(0, length // ROW, step, (zero, zero, zero))
        for i, s in enumerate(sums):
            part[pl.ds(i, 1), :] = jnp.sum(s, axis=0, keepdims=True)

    greet(me)
    tokens = Exchange(me, x, tok, a_sems, 0, False)
    seeds = Exchange(me, seed, cot, a_sems, 1, False)
    part[...] = jnp.zeros_like(part)
    mask()
    seen = set()

    def need(*us):
        for u in us:
            if u not in seen:
                seen.add(u)
                pieces[u].wait()

    for op, *at in FORWARD_ORDER:
        i = at[0] if at else 0
        if op == "ST":
            units[i].start()
        elif op == "R":
            units[i].hop(at[1])
        elif op == "SP":
            units[i].spread()
        elif op == "CX":
            units[i].cross()
        elif op == "CO":
            units[i].corner()
        elif op == "WH":
            units[i].whole()
            if pieces[i] is not None:
                pieces[i].start()
        elif op in ("TK", "SD"):
            (tokens if op == "TK" else seeds).start(*at)
        elif op == "UN":
            unpack()
            save(vecs, vec_out)
        elif op == "QP":
            if i == 0:
                tokens.wait()
                save(x, x_out)
                need(0, 2)
            else:
                need(2 + i)
            project(i)
            save((q, k, v)[i], (q_out, k_out, v_out)[i])
        elif op == "AT":
            attend(i)
            if i == 7:
                save(ctx, ctx_out)
        elif op == "F0":
            need(5)
            project_context()
        elif op == "FN":
            first_norm()
            for src, dst in ((n1, n1_out), (scale1, scale_out), (low, low_out)):
                save(src, dst)
        elif op == "IN":
            need(6 + i)
            inner(*at)
            if at == [QUARTERS - 1, 1]:
                save(hidden, hid_out)
                save(slope, slope_out)
        elif op == "OU":
            need(10 + i)
            outer(i)
        elif op == "N2":
            seeds.wait()
            second_norm()
            for src, dst in ((gsec, gsec_out), (gout, gout_out), (lay, lay_out), (part, part_out)):
                save(src, dst)
    for unit in units:
        unit.sent()
    tokens.sent()
    seeds.sent()
    for slot in range(4):
        p_save(12 + slot, slot).wait()
    for copy in saves:
        copy.wait()


def forward_all(tok, cot, labels, vec, weights):
    d = tok.shape[2]
    length = tok.shape[1] * LINE
    pairs = d // LANES
    quarter = weights[4].shape[1] // QUARTERS
    shape = jax.ShapeDtypeStruct
    bf, wide = shape((length, d), BF), shape((length, d), F32)
    heads = shape((pairs, length, LANES), BF)
    mlp = shape((QUARTERS, length, quarter), BF)
    outs = (
        [bf]
        + [shape((w.shape[0] * RING * LINE, w.shape[1]), BF) for w in weights]
        + [heads, heads, heads, shape((2 * pairs, length, length), BF), bf, bf]
        + [wide, shape((length, LANES), F32), mlp, mlp, wide, bf, bf, shape((24, d), F32), shape((8, d), F32)]
    )
    n = UNITS + 1 + 2
    dma = pltpu.SemaphoreType.DMA

    def vm(s):
        return pltpu.VMEM(s.shape, s.dtype)

    vmem = pl.BlockSpec(memory_space=pltpu.VMEM)
    return pl.pallas_call(
        forward_kernel,
        out_shape=outs,
        in_specs=[ANY, ANY, vmem] + [ANY] * 7,
        out_specs=[ANY] * len(outs),
        scratch_shapes=[
            vm(bf), vm(bf), pltpu.VMEM((vec.shape[0] * RING * LINE, LANES), BF), pltpu.VMEM((24, d), F32), pltpu.VMEM((8, d), F32),
            pltpu.VMEM((8, d, d), BF), pltpu.VMEM((QUARTERS, QUARTERS * quarter, d // QUARTERS), BF),
            vm(heads), vm(heads), vm(heads), pltpu.VMEM((length, length), F32), pltpu.VMEM((4, length, length), BF),
            vm(bf), vm(wide), pltpu.VMEM((length, LANES), F32), vm(bf), vm(mlp), vm(mlp), vm(wide), vm(wide), vm(bf), vm(bf),
            dma((n,)), dma((n, 6)), dma((n, 4)), dma((n, 4)), dma((n, 4)), dma((n, 4)), dma((n, 4)),
            dma((2, 4)), dma((2, 4)), dma((2,)), dma((n,)), dma((4,)), dma((16,)),
        ],
        compiler_params=pltpu.CompilerParams(collective_id=0, has_side_effects=True, vmem_limit_bytes=58 << 20),
        name="forward",
    )(tok, cot, labels, vec, *weights)


def backward_kernel(
    x_in, wq, wk, wv, wo, wi, wu, q_in, k_in, v_in, p_in, ctx_in, low_in,
    n1_in, scale_in, hid_in, slope_in, gsec_in, gout_in, lay_in, vec_in, part_in,
    lay_out, gtok_out, oq, ok, ov, oo, oi, ou, vec_out,
    from_core, half, plane, line, own, to_send, acc, zsum, ztot, vbuf, vrecv,
    hidden, gout, slope, ginner, gfirst, n1, scale1, low, dk, dv, probs, w_in, vecs, part, sums,
    credit, cs, cr, hs, hr, ps, pr, zs, zr, out_sem, vs, vr, a_send, a_recv, a_local, i_sem, w_sem, p_sem,
):
    me = Place()
    a_sems = (a_send, a_recv, a_local)
    length, d = gout.shape
    rows = d // RING
    q, k, v, x = hidden.at[0], hidden.at[1], hidden.at[2], hidden.at[3]
    gattn, gctx, ctx, gtok = slope.at[0], slope.at[1], slope.at[2], slope.at[3]
    dq = gout

    units = []

    def whole(ref):
        return lambda lo: ref[:, at_tile(lo, rows)]

    def tall(j):
        return lambda lo: hidden[lo // 2, :, pl.ds(pl.multiple_of(lax.rem(lo, 2) * (QUARTERS * rows) + j * rows, rows), rows)]

    for j in range(QUARTERS):
        units.append((tall(j), lambda at: gout[:, at], lambda o, w, j=j: ou.at[pl.ds(j * rows, rows), pl.ds(o, w)]))
    for j in range(QUARTERS):
        units.append((whole(low), lambda at, j=j: ginner[j, :, at], lambda o, w, j=j: oi.at[:, pl.ds(j * d + o, w)]))
    for left, right, out in ((ctx, gattn, oo), (x, dv, ov), (x, dk, ok), (x, dq, oq)):
        units.append((whole(left), lambda at, right=right: right[:, at], lambda o, w, out=out: out.at[:, pl.ds(o, w)]))
    parts, members = [], []
    for unit, count in enumerate(BACK_PARTS):
        members.append([])
        for i in range(count):
            members[unit].append(len(parts))
            parts.append((unit, i * (d // count), d // count))
    n = len(parts)

    def at_of(i):
        return pl.ds(parts[i][1], parts[i][2])

    def leads(i, slots):
        unit = parts[i][0]
        return members[unit - slots] if i == members[unit][0] and unit >= slots else ()

    core_slots, acc_slots, z_slots = from_core.shape[0], acc.shape[0], zsum.shape[0]

    def load(src, dst, i):
        return pltpu.make_async_copy(src, dst, i_sem.at[i])

    pieces = []
    for j in range(QUARTERS):
        pieces += [wu.at[pl.ds(j * d, d)], wi.at[:, pl.ds(j * d, d)]]
    pieces += [wo, wq, wk, wv]

    def w_load(i):
        return pltpu.make_async_copy(pieces[i], w_in.at[i % 3], w_sem.at[i % 3])

    def core_all(i):
        here = from_core.at[parts[i][0] % core_slots, :, :, at_of(i)]
        return send(here, here, cs.at[i], cr.at[i], me.at_c)

    def part_of(ref, i, *index):
        return ref.at[(parts[i][0] % ref.shape[0], *index, at_of(i))]

    low_rows, high_rows, all_rows = pl.ds(0, rows // 2), pl.ds(rows // 2, rows // 2), pl.ds(0, rows)

    def half_x(i):
        return send(part_of(acc, i, me.chip_d, low_rows), part_of(half, i, 0, low_rows), hs.at[i, 0], hr.at[i, 0], me.at_x)

    def half_y(i):
        return send(part_of(acc, i, me.chip_d, high_rows), part_of(half, i, 1, low_rows), hs.at[i, 1], hr.at[i, 1], me.at_y)

    def plane_x(i):
        return send(part_of(acc, i, me.chip_x, all_rows), part_of(plane, i, 0, all_rows), ps.at[i, 0], pr.at[i, 0], me.at_x)

    def plane_y(i):
        return send(part_of(acc, i, me.chip_y, all_rows), part_of(plane, i, 1, all_rows), ps.at[i, 1], pr.at[i, 1], me.at_y)

    end = (me.s == 0) | (me.s == 3)
    mid = (me.s == 1) | (me.s == 2)
    partner = me.along(me.s + 1 - 2 * lax.rem(me.s, 2))
    other = me.along(3 - me.s)

    def line_in(i):
        return send(part_of(zsum, i, all_rows), part_of(line, i, 0, all_rows), zs.at[i, 0], zr.at[i, 0], partner)

    def line_swap(i):
        return send(part_of(zsum, i, all_rows), part_of(line, i, 1, all_rows), zs.at[i, 0], zr.at[i, 1], other)

    def line_back(i):
        return send(part_of(ztot, i, all_rows), part_of(line, i, 0, all_rows), zs.at[i, 1], zr.at[i, 0], partner)

    def out_of(i):
        unit, offset, width = parts[i]
        return units[unit][2](offset, width)

    def out_mid(i):
        return pltpu.make_async_copy(part_of(ztot, i, all_rows), out_of(i), out_sem.at[i])

    def out_end(i):
        return pltpu.make_async_copy(part_of(line, i, 0, all_rows), out_of(i), out_sem.at[i])

    def wide(a):
        return a.astype(F32)

    def add(dst, a, b):
        dst[...] = (wide(a[...]) + wide(b[...])).astype(BF)

    def produce(i):
        unit = parts[i][0]
        left, right, _ = units[unit]
        at, slot = at_of(i), unit % 2
        for m in leads(i, 2):
            core_all(m).wait_send()
        if leads(i, core_slots):
            pl.semaphore_wait(credit, 1)

        def step(j, _):
            to_send[slot, j, :, at] = mm(left(2 * j + 1 - me.c), right(at), 0, 0).astype(BF)
            there = from_core.at[unit % core_slots, j, :, at]
            send(to_send.at[slot, j, :, at], there, cs.at[i], cr.at[i], me.at_c).start()
            return 0

        steps(0, 4, step, 0)

        def keep(j, _):
            own[slot, j, :, at] = mm(left(2 * j + me.c), right(at), 0, 0).astype(BF)
            return 0

        steps(0, 4, keep, 0)

    def s1(i):
        unit = parts[i][0]
        for m in leads(i, acc_slots):
            sent_acc(m)
        core_all(i).wait_recv()

        def step(j, _):
            here = (j, all_rows)
            add(part_of(acc, i, *here), part_of(own, i, *here), part_of(from_core, i, *here))
            return 0

        steps(0, 4, step, 0)
        half_x(i).start()
        half_y(i).start()
        if i == members[unit][-1] and unit + core_slots < len(units):
            pl.semaphore_signal(credit, inc=1, device_id=me.at_c, device_id_type=MESH)

    def s2(i):
        half_x(i).wait_recv()
        here = part_of(acc, i, me.chip_y, low_rows)
        add(here, here, part_of(half, i, 0, low_rows))
        plane_y(i).start()
        half_y(i).wait_recv()
        here = part_of(acc, i, me.chip_x, high_rows)
        add(here, here, part_of(half, i, 1, low_rows))
        plane_x(i).start()

    def s3(i):
        for m in leads(i, z_slots):
            pl.when(end)(lambda m=m: line_in(m).wait_send())
            pl.when(mid)(lambda m=m: line_swap(m).wait_send())
        plane_x(i).wait_recv()
        plane_y(i).wait_recv()
        got = wide(part_of(plane, i, 0, all_rows)[...]) + wide(part_of(plane, i, 1, all_rows)[...])
        part_of(zsum, i, all_rows)[...] = (wide(part_of(acc, i, me.chip, all_rows)[...]) + got).astype(BF)
        pl.when(end)(lambda: line_in(i).start())

    def z1(i):
        @pl.when(mid)
        def _():
            line_in(i).wait_recv()
            here = part_of(zsum, i, all_rows)
            add(here, here, part_of(line, i, 0, all_rows))
            line_swap(i).start()

    def z2(i):
        @pl.when(mid)
        def _():
            for m in leads(i, z_slots):
                line_back(m).wait_send()
                out_mid(m).wait()
            line_swap(i).wait_recv()
            add(part_of(ztot, i, all_rows), part_of(zsum, i, all_rows), part_of(line, i, 1, all_rows))
            line_back(i).start()
            out_mid(i).start()

    def z3(i):
        @pl.when(end)
        def _():
            line_back(i).wait_recv()
            out_end(i).start()

    def sent_acc(i):
        half_x(i).wait_send()
        half_y(i).wait_send()
        plane_x(i).wait_send()
        plane_y(i).wait_send()

    def v_swap(i, to):
        return send(vbuf.at[i], vrecv.at[i], vs.at[i], vr.at[i], to)

    v_to = (me.at_c, me.at_x, me.at_y)

    def v_step(i):
        if i == 0:
            vbuf[0] = sums[...]
            v_swap(0, v_to[0]).start()
        elif i < 4:
            v_swap(i - 1, v_to[i - 1]).wait_recv()
            vbuf[i] = vbuf[i - 1] + vrecv[i - 1]
            if i < 3:
                v_swap(i, v_to[i]).start()
            else:
                pl.when(end)(lambda: v_swap(3, partner).start())
        elif i == 4:

            @pl.when(mid)
            def _():
                v_swap(3, partner).wait_recv()
                vbuf[4] = vbuf[3] + vrecv[3]
                v_swap(4, other).start()

        elif i == 5:

            @pl.when(mid)
            def _():
                v_swap(4, other).wait_recv()
                vbuf[5] = vbuf[4] + vrecv[4]
                v_swap(5, partner).start()
                vec_out[...] = vbuf[5]

        elif i == 6:

            @pl.when(end)
            def _():
                v_swap(5, partner).wait_recv()
                vec_out[...] = vrecv[5]

    def put(i, value, tile=slice(None)):
        sums[pl.ds(i, 1), tile] = jnp.sum(value, axis=0, keepdims=True)

    def inner_grad(quarter, slot):
        def step(j, _):
            tile = at_tile(j, TILE)
            y = mm(gout[...], w_in[slot, tile, :], 1, 1) * wide(slope[quarter, :, tile])
            y = y.astype(BF)
            ginner[quarter, :, tile] = y
            put(8 + quarter, wide(y), tile)
            return 0

        steps(0, d // TILE, step, 0)

    def first_grad(quarter, slot):
        def step(j, _):
            tile = at_tile(j, TILE)
            gfirst[:, tile] = gfirst[:, tile] + mm(ginner[quarter], w_in[slot, tile, :], 1, 1)
            return 0

        steps(0, d // TILE, step, 0)

    def first_norm_back():
        gain = vecs[pl.ds(G1, 1), :]

        def step(j, carry):
            at = at_tile(j, ROW)
            g, centred = gfirst[at, :], n1[at, :]
            grad = norm_back(g * gain, centred, scale1[at, :1])
            gfirst[at, :] = grad
            rounded = grad.astype(BF)
            gattn[at, :] = rounded
            return carry[0] + eighths(g * centred), carry[1] + eighths(g), carry[2] + eighths(wide(rounded))

        zero = jnp.zeros((8, d), F32)
        gains, shifts, biases = steps(0, length // ROW, step, (zero, zero, zero))
        put(4, gains)
        put(5, shifts)
        put(2, biases)

    def context_grad(slot):
        def step(j, _):
            tile = at_tile(j, TILE)
            gctx[:, tile] = mm(gattn[...], w_in[slot, tile, :], 1, 1).astype(BF)
            return 0

        steps(0, d // TILE, step, 0)

    def p_load(pair, h, slot):
        return pltpu.make_async_copy(p_in.at[2 * pair + h], probs.at[slot, h], p_sem.at[slot, h])

    def attend_back(pair):
        slot = pair % 2
        if pair + 1 < d // LANES:
            for h in range(2):
                p_load(pair + 1, h, 1 - slot).start()
        masks = half_masks()
        at = pl.ds(pair * LANES, LANES)
        qp, kp, vp, gp = q[:, at], k[:, at], v[:, at], gctx[:, at]
        outs = None
        for h in range(2):
            p_load(pair, h, slot).wait()
            p = wide(probs[slot, h])
            g = mm(gp * masks[h].astype(BF), vp, 1, 1)
            w = p * g
            s = (w - p * jnp.sum(w, axis=1, keepdims=True)).astype(BF)
            got = (
                mm(s, kp) * (masks[h] * (1.0 / math.sqrt(HD))),
                mm(s, qp, 0, 0) * masks[h],
                mm(probs[slot, h], gp, 0, 0) * masks[h],
            )
            outs = got if outs is None else tuple(a + b for a, b in zip(outs, got))
        for ref, y, i in ((dq, outs[0], 0), (dk, outs[1], None), (dv, outs[2], 1)):
            y = y.astype(BF)
            ref[:, at] = y
            if i is not None:
                put(i, wide(y), at)

    def token_grad(j):
        tile = pl.ds(j * TILE, TILE)
        y = gfirst[:, tile]
        for ref, i in ((dq, 9), (dk, 10), (dv, 11)):
            y = y + mm(ref[...], w_in[i % 3, tile, :], 1, 1)
        gtok[:, tile] = y.astype(BF)

    for quarter in range(QUARTERS):
        load(hid_in.at[quarter], hidden.at[quarter], quarter).start()
    load(gout_in, gout, 4).start()
    w_load(0).start()
    load(slope_in, slope, 5).start()
    w_load(1).start()
    load(gsec_in, gfirst, 6).start()
    later = ((low_in, low, 7), (n1_in, n1, 8), (scale_in, scale1, 9), (vec_in, vecs, 10), (part_in, part, 11))
    for src, dst, i in later:
        load(src, dst, i).start()
    greet(me)
    lay_back = Exchange(me, lay_in, lay_out, a_sems, 0, True)
    tok_back = Exchange(me, gtok, gtok_out, a_sems, 1, True)
    for quarter in range(QUARTERS):
        load(hid_in.at[quarter], hidden.at[quarter], quarter).wait()
    load(gout_in, gout, 4).wait()
    sums[...] = jnp.zeros_like(sums)
    stages = {"P": produce, "S1": s1, "S2": s2, "S3": s3, "Z1": z1, "Z2": z2, "Z3": z3, "V": v_step, "AB": attend_back, "TG": token_grad}
    for op, *at in BACK_ORDER:
        i = at[0] if at else 0
        if op == "V" and i == 0:
            for row, j in ((0, 6), (1, 7), (2, 3)):
                sums[pl.ds(j, 1), :] = part[pl.ds(row, 1), :]
        if op in stages:
            stages[op](i)
        elif op in ("LO", "GT"):
            (lay_back if op == "LO" else tok_back).start(*at)
        elif op == "IG":
            if i == 0:
                load(slope_in, slope, 5).wait()
                load(gsec_in, gfirst, 6).wait()
                load(low_in, low, 7).wait()
            w_load(2 * i + 2).start()
            w_load(2 * i).wait()
            inner_grad(i, (2 * i) % 3)
        elif op == "FG":
            w_load(2 * i + 3).start()
            w_load(2 * i + 1).wait()
            first_grad(i, (2 * i + 1) % 3)
        elif op == "LD":
            for src, dst, j in ((q_in, q, 0), (k_in, k, 1), (v_in, v, 2)):
                for pair in range(d // LANES):
                    load(src.at[pair], dst.at[:, pl.ds(pair * LANES, LANES)], j).start()
            load(x_in, x, 3).start()
            load(ctx_in, ctx, 5).start()
            for h in range(2):
                p_load(0, h, 0).start()
        elif op == "LW":
            for dst, j in ((q, 0), (k, 1), (v, 2)):
                load(x_in, dst, j).wait()
            load(x_in, x, 3).wait()
            load(ctx_in, ctx, 5).wait()
        elif op == "NB":
            for src, dst, j in later[1:]:
                load(src, dst, j).wait()
            first_norm_back()
        elif op == "CG":
            w_load(10).start()
            w_load(8).wait()
            context_grad(8 % 3)
            w_load(11).start()
        elif op == "TW":
            for j in (9, 10, 11):
                w_load(j).wait()
    for unit in members[-2:]:
        for i in unit:
            core_all(i).wait_send()
    for unit in members[-acc_slots:]:
        for i in unit:
            sent_acc(i)
    for i in range(n):
        pl.when(end)(lambda i=i: out_end(i).wait())
    for unit in members[-z_slots:]:
        for i in unit:
            pl.when(end)(lambda i=i: line_in(i).wait_send())

            @pl.when(mid)
            def _(i=i):
                line_swap(i).wait_send()
                line_back(i).wait_send()
                out_mid(i).wait()

    for i in range(3):
        v_swap(i, v_to[i]).wait_send()
    pl.when(end)(lambda: v_swap(3, partner).wait_send())

    @pl.when(mid)
    def _():
        v_swap(4, other).wait_send()
        v_swap(5, partner).wait_send()

    for exchange in (lay_back, tok_back):
        exchange.wait()
        exchange.sent()


def backward_all(saved, block):
    length, d = saved[0].shape
    rows = d // RING
    units, n = len(BACK_PARTS), sum(BACK_PARTS)
    core_slots, acc_slots, z_slots = 3, 3, 3
    dma = pltpu.SemaphoreType.DMA
    shape = jax.ShapeDtypeStruct

    def vm(*s, dtype=BF):
        return pltpu.VMEM(s, dtype)

    split = shape((LINE, block, d), BF)
    sq = shape((rows, d), BF)
    sums = (16, d)
    outs = [split, split, sq, sq, sq, sq, shape((rows, QUARTERS * d), BF), shape((QUARTERS * rows, d), BF), shape(sums, F32)]
    mat = (length, d)
    mlp = (QUARTERS, length, d)
    return pl.pallas_call(
        backward_kernel,
        out_shape=outs,
        in_specs=[ANY] * len(saved),
        out_specs=[ANY] * 8 + [pl.BlockSpec(memory_space=pltpu.VMEM)],
        scratch_shapes=[
            vm(core_slots, 4, rows, d), vm(units, 2, rows // 2, d), vm(units, 2, rows, d), vm(units, 2, rows, d),
            vm(2, 4, rows, d), vm(2, 4, rows, d), vm(acc_slots, 4, rows, d), vm(z_slots, rows, d), vm(z_slots, rows, d),
            vm(6, *sums, dtype=F32), vm(6, *sums, dtype=F32),
            vm(*mlp), vm(*mat), vm(*mlp), vm(*mlp), vm(*mat, dtype=F32), vm(*mat, dtype=F32), vm(length, LANES, dtype=F32), vm(*mat),
            vm(*mat), vm(*mat), vm(2, 2, length, length), vm(3, d, d), vm(24, d, dtype=F32), vm(8, d, dtype=F32), vm(*sums, dtype=F32),
            pltpu.SemaphoreType.REGULAR,
            dma((n,)), dma((n,)), dma((n, 2)), dma((n, 2)), dma((n, 2)), dma((n, 2)), dma((n, 2)), dma((n, 2)),
            dma((n,)), dma((6,)), dma((6,)), dma((2, 4)), dma((2, 4)), dma((2,)), dma((12,)), dma((3,)), dma((2, 2)),
        ],
        compiler_params=pltpu.CompilerParams(collective_id=1, has_side_effects=True, vmem_limit_bytes=62 << 20),
        name="backward",
    )(*saved)


def pack_kernel(*refs):
    out = refs[-1]
    rows = []
    for ref in refs[:-1]:
        row = ref[...].astype(F32).reshape(1, ref.shape[0])
        if ref.shape[0] < LANES:
            row = jnp.concatenate([row, jnp.zeros((1, LANES - ref.shape[0]), F32)], axis=1)
        rows.append(row)
    rows.append(jnp.zeros((out.shape[0] - len(rows), LANES), F32))
    out[...] = jnp.concatenate(rows, axis=0).astype(BF)


def pack(vectors):
    vmem = pl.BlockSpec(memory_space=pltpu.VMEM)
    return pl.pallas_call(
        pack_kernel,
        in_specs=[vmem] * len(vectors),
        out_specs=vmem,
        out_shape=jax.ShapeDtypeStruct((16, LANES), BF),
        name="pack",
    )(*vectors)


def finish_kernel(lay, gtok, *rest):
    mats, sums, outs = rest[:6], rest[6], rest[7:]
    outs[0][...] = lay[...]
    outs[1][...] = gtok[...]
    for src, dst in zip(mats, outs[2:8]):
        dst[...] = src[...].astype(F32)
    lo = lax.axis_index("grp")
    for i, dst in zip((0, 1, 2, 8, 3, 4, 5, 6, 7), outs[8:]):
        n = dst.shape[0]
        if i < 8:
            row, column = i, lo * n
        else:
            per = sums.shape[1] // n
            row, column = 8 + lo // per, lax.rem(lo, per) * n
        dst[...] = sums[pl.ds(row, 1), pl.ds(pl.multiple_of(column, LANES), n)].reshape(n)


def finish(out):
    count = out[0].shape[0]
    shape = jax.ShapeDtypeStruct

    def rows(a, dtype):
        block = (a.shape[0] // count,) + a.shape[1:]
        return pl.BlockSpec(block, lambda i: (i,) + (0,) * (len(block) - 1)), shape(a.shape, dtype)

    d = out[8].shape[1]
    ins = [rows(a, a.dtype)[0] for a in out[:8]] + [pl.BlockSpec(out[8].shape, lambda i: (0, 0))]
    big = [rows(a, a.dtype if k < 2 else F32) for k, a in enumerate(out[:8])]
    sizes = [d // RING] * 3 + [QUARTERS * d // RING] + [d // RING] * 5
    small = [(pl.BlockSpec((n,), lambda i: (0,)), shape((n,), F32)) for n in sizes]
    specs, shapes = zip(*(big + small))
    return tuple(
        pl.pallas_call(
            finish_kernel,
            grid=(count,),
            in_specs=ins,
            out_specs=list(specs),
            out_shape=list(shapes),
            compiler_params=pltpu.CompilerParams(vmem_limit_bytes=62 << 20),
            name="finish",
        )(*out)
    )


def local(tokens, labels, *rest):
    weights, vectors, cotangent = rest[:6], rest[6:15], rest[15]
    groups = lax.axis_size("grp") // RING
    g, s = lax.axis_index("grp"), lax.axis_index("seq")
    lo = lax.rem(g, RING)
    if groups > 1:
        def regroup(w):
            full = lax.all_gather(w, ("grp", "seq"), axis=0, tiled=True)
            n = full.shape[0] // (RING * LINE)
            return lax.dynamic_slice_in_dim(full, (lo * LINE + s) * n, n, 0)

        weights = tuple(regroup(w) for w in weights)
        vectors = tuple(regroup(v) for v in vectors)
    packed = pack(vectors)
    saved = forward_all(tokens, cotangent, labels, packed, weights)
    out = backward_all(saved, tokens.shape[1])
    if groups == 1:
        return finish(out)
    layer_out, grad_tokens = out[:2]
    mats = [m.astype(F32) for m in out[2:8]]
    vec = out[8]
    flat = [vec[i] for i in range(8)]
    flat.insert(3, vec[8 : 8 + QUARTERS].reshape(-1))
    same = [[l + RING * h for h in range(groups)] for l in range(RING)]
    eight = [[l + RING * h for l in range(RING)] for h in range(groups)]

    def rejoin(m):
        m = lax.psum(m, "grp", axis_index_groups=same)
        m = lax.all_gather(m, "grp", axis=0, tiled=True, axis_index_groups=eight)
        n = m.shape[0] // (RING * groups)
        return lax.dynamic_slice_in_dim(m, g * n, n, 0)

    mats = [rejoin(m) for m in mats]
    flat = [lax.psum(v, "grp", axis_index_groups=same) for v in flat]
    flat = [lax.dynamic_slice_in_dim(v, g * (v.shape[0] // (RING * groups)), v.shape[0] // (RING * groups), 0) for v in flat]
    return (layer_out, grad_tokens, *mats, *flat)


def solution(mesh):
    both = ("grp", "seq")
    rows = P("grp", "seq", None)
    return jax.shard_map(
        local,
        mesh=mesh,
        in_specs=(rows, P("grp", None)) + (P(both, None),) * 6 + (P(both),) * 9 + (rows,),
        out_specs=(rows, rows) + (P("grp", None),) * 6 + (P("grp"),) * 9,
        check_vma=False,
    )
```

```python
import functools
import math

import jax
import jax.numpy as jnp
from jax import lax
from jax.experimental import pallas as pl
from jax.experimental.pallas import tpu as pltpu
from jax.sharding import PartitionSpec as P

H = 16
HD = 64
LINE = 4
RING = 8
UNITS = 12
QUARTERS = 4
LANES = 128
MESH = pl.DeviceIdType.MESH
BF = jnp.bfloat16
F32 = jnp.float32
ANY = pl.BlockSpec(memory_space=pl.ANY)


class Place:
    def __init__(self):
        self.g = lax.axis_index("grp")
        self.s = lax.axis_index("seq")
        self.lo = lax.rem(self.g, RING)
        self.c = lax.rem(self.lo, 2)
        xb = lax.rem(self.lo // 2, 2)
        yb = self.lo // 4
        self.dc, self.dx, self.dy = 1 - 2 * self.c, 2 - 4 * xb, 4 - 8 * yb
        self.at_c = (self.g + self.dc, self.s)
        self.at_x = (self.g + self.dx, self.s)
        self.at_y = (self.g + self.dy, self.s)
        self.chip = self.lo // 2
        self.chip_x = self.chip + 1 - 2 * xb
        self.chip_y = self.chip + 2 - 4 * yb
        self.chip_d = self.chip_x + 2 - 4 * yb

    def along(self, t):
        return (self.g, t)


def send(src, dst, send_sem, recv_sem, to):
    return pltpu.make_async_remote_copy(
        src_ref=src, dst_ref=dst, send_sem=send_sem, recv_sem=recv_sem, device_id=to, device_id_type=MESH
    )


def greet(me):
    barrier = pltpu.get_barrier_semaphore()

    def signal(to):
        pl.semaphore_signal(barrier, inc=1, device_id=to, device_id_type=MESH)

    for to in (me.at_c, me.at_x, me.at_y):
        signal(to)
    for t in range(LINE):
        pl.when(me.s != t)(lambda t=t: signal(me.along(t)))
    pl.semaphore_wait(barrier, 3 + LINE - 1)


class Exchange:
    def __init__(self, me, whole, split, sems, index, back):
        self.me, self.whole, self.split, self.index, self.back = me, whole, split, index, back
        self.send_sem, self.recv_sem, self.local_sem = sems

    def rows(self, t, part=0, parts=1):
        n = self.split.shape[1]
        return self.whole.at[pl.ds(t * n + part * (n // parts), n // parts)]

    def ends(self, t, part=0, parts=1):
        n = self.split.shape[1] // parts
        here = pl.ds(part * n, n)
        if self.back:
            return self.rows(t, part, parts), self.split.at[self.me.s, here]
        return self.split.at[t, here], self.rows(self.me.s, part, parts)

    def copy(self, t, part=0, parts=1):
        src, dst = self.ends(t, part, parts)
        return send(src, dst, self.send_sem.at[self.index, t], self.recv_sem.at[self.index, self.me.s], self.me.along(t))

    def landed(self, t):
        dst = self.split.at[t] if self.back else self.rows(t)
        return send(dst, dst, self.send_sem.at[self.index, t], self.recv_sem.at[self.index, t], self.me.along(t))

    def own(self):
        src, dst = self.ends(self.me.s)
        return pltpu.make_async_copy(src, dst, self.local_sem.at[self.index])

    def start(self, distance, part=0, parts=1):
        s = self.me.s
        if distance == 1 and part == 0:
            self.own().start()
        for t in range(LINE):
            pl.when((s - t == distance) | (t - s == distance))(lambda t=t: self.copy(t, part, parts).start())

    def wait(self):
        self.own().wait()
        for t in range(LINE):
            pl.when(self.me.s != t)(lambda t=t: self.landed(t).wait_recv())

    def sent(self):
        for t in range(LINE):
            pl.when(self.me.s != t)(lambda t=t: self.copy(t).wait_send())


class Gather:
    def __init__(self, me, src, dst, rows, sems, u, fine):
        self.me, self.src, self.dst, self.rows, self.u, self.fine = me, src, dst, rows, u, fine
        self.local, self.zs, self.zr, self.xs, self.xr, self.cs, self.cr = sems

    def own(self):
        me = self.me
        return pltpu.make_async_copy(self.src, self.dst((me.lo * LINE + me.s) * self.rows, self.rows), self.local.at[self.u])

    def shard(self, source):
        return self.dst((self.me.lo * LINE + source) * self.rows, self.rows)

    def z_send(self, source, step, slot):
        there = self.shard(source)
        src = self.src if slot < 2 else there
        return send(src, there, self.zs.at[self.u, slot], self.zr.at[self.u, source], self.me.along(self.me.s + step))

    def z_recv(self, source):
        there = self.shard(source)
        send(there, there, self.zs.at[self.u, 0], self.zr.at[self.u, source], self.me.at_c).wait_recv()

    def xy_shard(self, source, own):
        there = self.shard(source)
        for k, to in ((0, self.me.at_x), (1, self.me.at_y)):
            send(self.src if own else there, there, self.xs.at[self.u, k], self.xr.at[self.u, k], to).start()

    def start(self):
        me = self.me
        self.own().start()
        pl.when(me.s < LINE - 1)(lambda: self.z_send(me.s, 1, 0).start())
        pl.when(me.s > 0)(lambda: self.z_send(me.s, -1, 1).start())
        if self.fine:
            self.xy_shard(me.s, True)

    def hop(self, h):
        me = self.me

        @pl.when(me.s >= h)
        def _():
            self.z_recv(me.s - h)
            if h < LINE - 1:
                pl.when(me.s < LINE - 1)(lambda: self.z_send(me.s - h, 1, 2 * h).start())
            if self.fine:
                self.xy_shard(me.s - h, False)

        @pl.when(me.s < LINE - h)
        def _():
            self.z_recv(me.s + h)
            if h < LINE - 1:
                pl.when(me.s > 0)(lambda: self.z_send(me.s + h, -1, 2 * h + 1).start())
            if self.fine:
                self.xy_shard(me.s + h, False)

    def block(self, lo, half=None):
        rows = self.rows * LINE
        if half is None:
            return self.dst(lo * rows, rows)
        return self.dst(lo * rows + half * (rows // 2), rows // 2)

    def x1(self, lo):
        return send(self.block(lo), self.block(lo), self.xs.at[self.u, 0], self.xr.at[self.u, 0], self.me.at_x)

    def y1(self, lo):
        return send(self.block(lo), self.block(lo), self.xs.at[self.u, 1], self.xr.at[self.u, 1], self.me.at_y)

    def x2(self, lo):
        return send(self.block(lo, 1), self.block(lo, 1), self.xs.at[self.u, 2], self.xr.at[self.u, 2], self.me.at_x)

    def y2(self, lo):
        return send(self.block(lo, 0), self.block(lo, 0), self.xs.at[self.u, 3], self.xr.at[self.u, 3], self.me.at_y)

    def core(self, lo, k):
        return send(self.block(lo), self.block(lo), self.cs.at[self.u, k], self.cr.at[self.u, k], self.me.at_c)

    def spread(self):
        me = self.me
        self.own().wait()
        if not self.fine:
            self.x1(me.lo).start()
            self.y1(me.lo).start()
        self.core(me.lo, 0).start()

    def cross(self):
        me = self.me
        lo_x, lo_y = me.lo + me.dx, me.lo + me.dy
        self.x1(lo_x).wait_recv()
        self.y2(lo_x).start()
        self.core(lo_x, 1).start()
        self.y1(lo_y).wait_recv()
        self.x2(lo_y).start()
        self.core(lo_y, 2).start()

    def corner(self):
        me = self.me
        lo_d = me.lo + me.dx + me.dy
        self.x2(lo_d).wait_recv()
        self.y2(lo_d).wait_recv()
        self.core(lo_d, 3).start()

    def whole(self):
        me = self.me
        for k, lo in enumerate((me.lo, me.lo + me.dx, me.lo + me.dy, me.lo + me.dx + me.dy)):
            self.core(lo + me.dc, k).wait_recv()

    def sent(self):
        me = self.me
        for h in range(LINE - 1):
            right = (me.s >= h) & (me.s < LINE - 1)
            left = (me.s < LINE - h) & (me.s > 0)
            pl.when(right)(lambda h=h: self.z_send(me.s - h, 1, 2 * h).wait_send())
            pl.when(left)(lambda h=h: self.z_send(me.s + h, -1, 2 * h + 1).wait_send())
        self.x1(me.lo).wait_send()
        self.y1(me.lo).wait_send()
        self.x2(me.lo + me.dy).wait_send()
        self.y2(me.lo + me.dx).wait_send()
        for k, lo in enumerate((me.lo, me.lo + me.dx, me.lo + me.dy, me.lo + me.dx + me.dy)):
            self.core(lo, k).wait_send()


def rows_of(ref, columns=None):
    if columns is None:
        return lambda row, n: ref.at[pl.ds(row, n)]
    return lambda row, n: ref.at[pl.ds(row, n), columns]


def rows_of(ref, columns=None):
    if columns is None:
        return lambda row, n: ref.at[pl.ds(row, n)]
    return lambda row, n: ref.at[pl.ds(row, n), columns]


def mm(a, b, ca=1, cb=0):
    return lax.dot_general(a, b, (((ca,), (cb,)), ((), ())), preferred_element_type=F32)


def at_tile(j, tile):
    if isinstance(j, int):
        return pl.ds(j * tile, tile)
    return pl.ds(pl.multiple_of(j * tile, tile), tile)


def steps(first, last, step, carry=0):
    for j in range(first, last):
        carry = step(j, carry)
    return carry


def iota(shape, dim):
    return lax.broadcasted_iota(jnp.int32, shape, dim)


def half_masks():
    low = (iota((1, LANES), 1) < HD).astype(F32)
    return low, 1.0 - low


def gelu_parts(u):
    t = 1.0 / (1.0 + (0.3275911 * 0.7071067811865476) * jnp.abs(u))
    poly = t * (0.254829592 + t * (-0.284496736 + t * (1.421413741 + t * (-1.453152027 + t * 1.061405429))))
    bell = jnp.exp(-0.5 * u * u)
    tail = 0.5 * poly * bell
    cdf = jnp.where(u >= 0.0, 1.0 - tail, tail)
    return u * cdf, cdf + u * (bell * 0.3989422804014327)


def stats(r):
    centered = r - jnp.mean(r, axis=-1, keepdims=True)
    scale = lax.rsqrt(jnp.mean(centered * centered, axis=-1, keepdims=True) + 1e-06)
    return centered * scale, scale


def norm_back(u, n, scale):
    return (u - jnp.mean(u, axis=-1, keepdims=True) - n * jnp.mean(u * n, axis=-1, keepdims=True)) * scale


def eighths(x):
    return jnp.sum(x.reshape(x.shape[0] // 8, 8, x.shape[1]), axis=0)


FINE = (0, 2, 3, 4)
OUTER_PARTS = (1, 1, 1, 1)
FORWARD_ORDER = (
    ("ST", 0), ("ST", 1), ("ST", 2), ("ST", 3), ("ST", 4), ("ST", 5), ("R", 0, 1), ("R", 1, 1), ("R", 2, 1), ("R", 3, 1), ("R", 4, 1),
    ("R", 5, 1), ("R", 0, 2), ("R", 1, 2), ("R", 2, 2), ("R", 3, 2), ("R", 4, 2), ("R", 5, 2), ("R", 0, 3), ("SP", 0), ("R", 1, 3),
    ("SP", 1), ("R", 2, 3), ("SP", 2), ("R", 3, 3), ("SP", 3), ("CX", 0), ("ST", 6), ("R", 4, 3), ("SP", 4), ("CX", 2), ("ST", 7),
    ("R", 5, 3), ("CX", 1), ("SP", 5), ("ST", 8), ("CX", 3), ("ST", 9), ("R", 6, 1), ("CO", 0), ("R", 7, 1), ("CX", 4), ("WH", 0),
    ("ST", 10), ("R", 8, 1), ("CO", 2), ("CO", 1), ("R", 9, 1), ("WH", 2), ("WH", 1), ("R", 6, 2), ("TK", 2, 0, 4), ("UN",),
    ("R", 7, 2), ("R", 10, 1), ("CX", 5), ("R", 8, 2), ("R", 9, 2), ("CO", 3), ("R", 6, 3), ("SP", 6), ("TK", 3, 0, 4), ("WH", 3),
    ("TK", 1, 0, 4), ("CO", 4), ("TK", 2, 1, 4), ("WH", 4), ("TK", 3, 1, 4), ("R", 7, 3), ("SP", 7), ("CO", 5), ("TK", 1, 1, 4),
    ("R", 10, 2), ("WH", 5), ("R", 8, 3), ("SP", 8), ("TK", 2, 2, 4), ("R", 9, 3), ("SP", 9), ("TK", 3, 2, 4), ("CX", 6),
    ("TK", 1, 2, 4), ("TK", 2, 3, 4), ("TK", 3, 3, 4), ("CX", 7), ("TK", 1, 3, 4), ("R", 10, 3), ("SP", 10), ("ST", 11), ("ST", 12),
    ("CX", 8), ("ST", 13), ("SD", 2, 0, 4), ("QP", 0), ("CX", 9), ("R", 11, 1), ("QP", 1), ("R", 12, 1), ("SD", 3, 0, 4), ("QP", 2),
    ("R", 13, 1), ("CO", 6), ("AT", 0), ("CO", 7), ("WH", 6), ("SD", 1, 0, 4), ("AT", 1), ("R", 11, 2), ("WH", 7), ("AT", 2),
    ("R", 12, 2), ("SD", 2, 1, 4), ("AT", 3), ("CX", 10), ("AT", 4), ("R", 13, 2), ("SD", 3, 1, 4), ("AT", 5), ("R", 11, 3), ("SP", 11),
    ("CO", 8), ("AT", 6), ("R", 12, 3), ("SP", 12), ("CO", 9), ("SD", 1, 1, 4), ("WH", 8), ("AT", 7), ("F0",), ("R", 13, 3), ("SP", 13),
    ("CO", 10), ("WH", 9), ("SD", 2, 2, 4), ("FN",), ("IN", 0, 0), ("WH", 10), ("SD", 3, 2, 4), ("IN", 0, 1), ("CX", 11), ("IN", 1, 0),
    ("SD", 1, 2, 4), ("IN", 1, 1), ("IN", 2, 0), ("CX", 12), ("SD", 2, 3, 4), ("IN", 2, 1), ("IN", 3, 0), ("SD", 3, 3, 4), ("IN", 3, 1),
    ("CX", 13), ("OU", 0), ("CO", 11), ("SD", 1, 3, 4), ("WH", 11), ("CO", 12), ("OU", 1), ("WH", 12), ("CO", 13), ("OU", 2),
    ("WH", 13), ("OU", 3), ("N2",),
)
BACK_PARTS = (1, 1, 1, 1, 1, 1, 1, 1, 1, 1, 1, 1)
BACK_ORDER = (
    ("LO", 2, 0, 4), ("LO", 2, 1, 4), ("LO", 2, 2, 4), ("P", 0), ("P", 1), ("IG", 0), ("S1", 0), ("FG", 0), ("S1", 1), ("LO", 2, 3, 4),
    ("IG", 1), ("LO", 3, 0, 4), ("P", 2), ("S2", 0), ("LO", 3, 1, 4), ("FG", 1), ("LO", 3, 2, 4), ("IG", 2), ("S2", 1), ("S1", 2),
    ("LO", 3, 3, 4), ("LO", 1, 0, 4), ("FG", 2), ("LO", 1, 1, 4), ("IG", 3), ("LO", 1, 2, 4), ("S3", 0), ("FG", 3), ("P", 3),
    ("LO", 1, 3, 4), ("LD",), ("NB",), ("P", 4), ("S1", 3), ("S3", 1), ("CG",), ("S2", 2), ("LW",), ("AB", 0), ("S1", 4), ("S2", 3),
    ("Z1", 0), ("AB", 1), ("AB", 2), ("AB", 3), ("S3", 2), ("Z1", 1), ("AB", 4), ("Z2", 0), ("S2", 4), ("AB", 5), ("AB", 6), ("AB", 7),
    ("S3", 3), ("Z1", 2), ("Z2", 1), ("V", 0), ("TW",), ("TG", 0), ("Z3", 0), ("P", 5), ("P", 6), ("S3", 4), ("V", 1), ("TG", 1),
    ("S1", 5), ("Z1", 3), ("Z2", 2), ("Z3", 1), ("TG", 2), ("S1", 6), ("V", 2), ("TG", 3), ("GT", 2, 0, 4), ("GT", 3, 0, 4),
    ("GT", 1, 0, 4), ("P", 7), ("S2", 5), ("Z1", 4), ("V", 3), ("P", 8), ("S2", 6), ("Z2", 3), ("S1", 7), ("Z3", 2), ("P", 9), ("V", 4),
    ("GT", 2, 1, 4), ("GT", 3, 1, 4), ("S3", 5), ("S1", 8), ("GT", 1, 1, 4), ("V", 5), ("GT", 2, 2, 4), ("V", 6), ("GT", 3, 2, 4),
    ("Z2", 4), ("S3", 6), ("S1", 9), ("Z3", 3), ("Z1", 5), ("S2", 7), ("P", 10), ("S2", 8), ("P", 11), ("GT", 1, 2, 4), ("GT", 2, 3, 4),
    ("S2", 9), ("GT", 3, 3, 4), ("GT", 1, 3, 4), ("Z1", 6), ("S3", 7), ("S1", 10), ("Z2", 5), ("Z3", 4), ("S3", 8), ("S1", 11),
    ("Z1", 7), ("S2", 10), ("Z2", 6), ("S3", 9), ("Z1", 8), ("Z3", 5), ("S2", 11), ("Z2", 7), ("Z3", 6), ("Z1", 9), ("S3", 10),
    ("Z2", 8), ("Z3", 7), ("S3", 11), ("Z1", 10), ("Z2", 9), ("Z3", 8), ("Z1", 11), ("Z2", 10), ("Z3", 9), ("Z2", 11), ("Z3", 10),
    ("Z3", 11),
)
ROW = 64
TILE = 256
BQ, BV, BO, BI, BU, G1, S1, G2, S2 = range(9)
INNER = 16


def forward_kernel(
    tok, cot, labels, vec, wq, wk, wv, wo, wi, wu,
    x_out, wq_all, wk_all, wv_all, wo_all, wi_all, wu_all, q_out, k_out, v_out, p_out, ctx_out, low_out,
    n1_out, scale_out, hid_out, slope_out, gsec_out, gout_out, lay_out, vec_out, part_out,
    x, seed, packed, vecs, part, w_in, wu_in, q, k, v, bias, probs, ctx, n1, scale1, low, hidden, slope, res, gsec, gout, lay,
    local, zs, zr, xs, xr, cs, cr, a_send, a_recv, a_local, w_sem, p_sem, o_sem,
):
    me = Place()
    sems = (local, zs, zr, xs, xr, cs, cr)
    a_sems = (a_send, a_recv, a_local)
    d = x.shape[1]
    length = x.shape[0]
    units, pieces = [], []

    def add(src, ref, columns, to=None):
        src = src if columns is None else src.at[:, columns]
        u = len(units)
        units.append(Gather(me, src, rows_of(ref, columns), src.shape[0], sems, u, u in FINE))
        pieces.append(None if to is None else pltpu.make_async_copy(ref if columns is None else ref.at[:, columns], to, w_sem.at[u]))

    add(wq, wq_all, pl.ds(0, d // 2), w_in.at[0, :, pl.ds(0, d // 2)])
    add(vec, packed, None)
    add(wq, wq_all, pl.ds(d // 2, d // 2), w_in.at[0, :, pl.ds(d // 2, d // 2)])
    for i, (src, ref) in enumerate(((wk, wk_all), (wv, wv_all), (wo, wo_all))):
        add(src, ref, None, w_in.at[1 + i])
    width = wi.shape[1] // QUARTERS
    for j in range(QUARTERS):
        add(wi, wi_all, pl.ds(j * width, width), w_in.at[4 + j])
    outer_at = []
    for j, parts in enumerate(OUTER_PARTS):
        width = d // QUARTERS // parts
        for i in range(parts):
            add(wu, wu_all, pl.ds(j * TILE + i * width, width), wu_in.at[j, :, pl.ds(i * width, width)])
            outer_at.append((j, i * width, width))
    n = len(units)
    saves = []

    def save(src, dst):
        copy = pltpu.make_async_copy(src, dst, o_sem.at[len(saves)])
        copy.start()
        saves.append(copy)

    def row(i):
        return vecs[pl.ds(i, 1), :]

    def unpack():
        p = packed[...]
        piece = d // (RING * LINE)
        spread = (iota((LANES, d), 1) % piece == iota((LANES, d), 0)).astype(BF)
        wide = mm(p, spread).reshape(RING * LINE, 16, d)
        here = iota((RING * LINE, 1, d), 0) == iota((RING * LINE, 1, d), 2) // piece
        vecs[pl.ds(0, 16), :] = jnp.sum(jnp.where(here, wide, 0.0), axis=0)
        p = p.astype(F32).reshape(RING * LINE, 16, LANES)
        p = jnp.sum(jnp.where(iota(p.shape, 1) == BI, p, 0.0), axis=1).astype(BF)
        spread = (iota((LANES, d), 1) % LANES == iota((LANES, d), 0)).astype(BF)
        per = RING * LINE // QUARTERS
        wide = mm(p, spread).reshape(QUARTERS, per, d)
        here = iota((1, per, d), 1) == iota((1, per, d), 2) // LANES
        inner = jnp.sum(jnp.where(here, wide, 0.0), axis=1)
        vecs[pl.ds(INNER, 8), :] = jnp.concatenate([inner, jnp.zeros_like(inner)], axis=0)

    def mask():
        own = labels[pl.ds(me.s, 1), :]
        marks = jnp.where(own != 0, own, -1 - iota(own.shape, 1)).astype(F32)
        down = jnp.broadcast_to(marks, (LANES, length)).T[:, :1]
        bias[...] = jnp.where(down == marks, 0.0, -1e30)

    def project(slot):
        out, b, factor = ((q, BQ, 1.0 / math.sqrt(HD)), (k, None, None), (v, BV, None))[slot]

        def step(j, _):
            tile = at_tile(j, TILE)
            y = mm(x[...], w_in[slot, :, tile])
            if b is not None:
                y = y + vecs[pl.ds(b, 1), tile]
            y = y.astype(BF)
            if factor is not None:
                y = (y.astype(F32) * factor).astype(BF)
            out[2 * j] = y[:, :LANES]
            out[2 * j + 1] = y[:, LANES:]
            return 0

        lax.fori_loop(0, d // TILE, step, 0)

    def p_save(h, slot):
        return pltpu.make_async_copy(probs.at[slot], p_out.at[h], p_sem.at[slot])

    def attend(pair):
        masks = half_masks()
        kp, vp, qp = k[pair], v[pair], q[pair]
        out = None
        for h in range(2):
            slot = (2 * pair + h) % 4
            if pair >= 2:
                p_save(2 * pair + h, slot).wait()
            scores = mm(qp * masks[h].astype(BF), kp, 1, 1) + bias[...]
            e = jnp.exp(scores - jnp.max(scores, axis=1, keepdims=True))
            p = (e * (1.0 / jnp.sum(e, axis=1, keepdims=True))).astype(BF)
            probs[slot] = p
            p_save(2 * pair + h, slot).start()
            term = mm(p, vp) * masks[h]
            out = term if out is None else out + term
        ctx[:, pl.ds(pair * LANES, LANES)] = out.astype(BF)

    def project_context():
        def step(j, _):
            tile = at_tile(j, TILE)
            y = mm(ctx[...], w_in[3, :, tile]) + vecs[pl.ds(BO, 1), tile]
            n1[:, tile] = y + x[:, tile].astype(F32)
            return 0

        lax.fori_loop(0, d // TILE, step, 0)

    def first_norm():
        def norm(j, _):
            rows = at_tile(j, ROW)
            centred, scale = stats(n1[rows, :])
            n1[rows, :] = centred
            scale1[rows, :] = jnp.broadcast_to(scale, (ROW, LANES))
            first = centred * row(G1) + row(S1)
            low[rows, :] = first.astype(BF)
            res[rows, :] = first + row(BU)
            return 0

        lax.fori_loop(0, length // ROW, norm, 0)

    def inner(quarter, part):
        half = d // TILE // 2

        def step(j, _):
            tile = at_tile(j, TILE)
            u = mm(low[...], w_in[4 + quarter, :, tile]) + vecs[pl.ds(INNER + quarter, 1), tile]
            act, grad = gelu_parts(u)
            hidden[quarter, :, tile] = act.astype(BF)
            slope[quarter, :, tile] = grad.astype(BF)
            return 0

        lax.fori_loop(part * half, (part + 1) * half, step, 0)

    def outer(i):
        j, offset, width = outer_at[i]
        tile = pl.ds(j * TILE + offset, width)
        y = res[:, tile]
        for quarter in range(QUARTERS):
            y = y + mm(hidden[quarter], wu_in[j, pl.ds(quarter * d, d), pl.ds(offset, width)])
        res[:, tile] = y

    def second_norm():
        def step(j, sums):
            rows = at_tile(j, ROW)
            centred, scale = stats(res[rows, :])
            lay[rows, :] = (centred * row(G2) + row(S2)).astype(BF)
            g = seed[rows, :].astype(F32)
            grad = norm_back(g * row(G2), centred, scale)
            gsec[rows, :] = grad
            rounded = grad.astype(BF)
            gout[rows, :] = rounded
            return sums[0] + eighths(g * centred), sums[1] + eighths(g), sums[2] + eighths(rounded.astype(F32))

        zero = jnp.zeros((8, d), F32)
        sums = lax.fori_loop(0, length // ROW, step, (zero, zero, zero))
        for i, s in enumerate(sums):
            part[pl.ds(i, 1), :] = jnp.sum(s, axis=0, keepdims=True)

    greet(me)
    tokens = Exchange(me, x, tok, a_sems, 0, False)
    seeds = Exchange(me, seed, cot, a_sems, 1, False)
    part[...] = jnp.zeros_like(part)
    mask()
    seen = set()

    def need(*us):
        for u in us:
            if u not in seen:
                seen.add(u)
                pieces[u].wait()

    for op, *at in FORWARD_ORDER:
        i = at[0] if at else 0
        if op == "ST":
            units[i].start()
        elif op == "R":
            units[i].hop(at[1])
        elif op == "SP":
            units[i].spread()
        elif op == "CX":
            units[i].cross()
        elif op == "CO":
            units[i].corner()
        elif op == "WH":
            units[i].whole()
            if pieces[i] is not None:
                pieces[i].start()
        elif op in ("TK", "SD"):
            (tokens if op == "TK" else seeds).start(*at)
        elif op == "UN":
            unpack()
            save(vecs, vec_out)
        elif op == "QP":
            if i == 0:
                tokens.wait()
                save(x, x_out)
                need(0, 2)
            else:
                need(2 + i)
            project(i)
            save((q, k, v)[i], (q_out, k_out, v_out)[i])
        elif op == "AT":
            attend(i)
            if i == 7:
                save(ctx, ctx_out)
        elif op == "F0":
            need(5)
            project_context()
        elif op == "FN":
            first_norm()
            for src, dst in ((n1, n1_out), (scale1, scale_out), (low, low_out)):
                save(src, dst)
        elif op == "IN":
            need(6 + i)
            inner(*at)
            if at == [QUARTERS - 1, 1]:
                save(hidden, hid_out)
                save(slope, slope_out)
        elif op == "OU":
            need(10 + i)
            outer(i)
        elif op == "N2":
            seeds.wait()
            second_norm()
            for src, dst in ((gsec, gsec_out), (gout, gout_out), (lay, lay_out), (part, part_out)):
                save(src, dst)
    for unit in units:
        unit.sent()
    tokens.sent()
    seeds.sent()
    for slot in range(4):
        p_save(12 + slot, slot).wait()
    for copy in saves:
        copy.wait()


def forward_all(tok, cot, labels, vec, weights):
    d = tok.shape[2]
    length = tok.shape[1] * LINE
    pairs = d // LANES
    quarter = weights[4].shape[1] // QUARTERS
    shape = jax.ShapeDtypeStruct
    bf, wide = shape((length, d), BF), shape((length, d), F32)
    heads = shape((pairs, length, LANES), BF)
    mlp = shape((QUARTERS, length, quarter), BF)
    outs = (
        [bf]
        + [shape((w.shape[0] * RING * LINE, w.shape[1]), BF) for w in weights]
        + [heads, heads, heads, shape((2 * pairs, length, length), BF), bf, bf]
        + [wide, shape((length, LANES), F32), mlp, mlp, wide, bf, bf, shape((24, d), F32), shape((8, d), F32)]
    )
    n = UNITS + 1 + 2
    dma = pltpu.SemaphoreType.DMA

    def vm(s):
        return pltpu.VMEM(s.shape, s.dtype)

    vmem = pl.BlockSpec(memory_space=pltpu.VMEM)
    return pl.pallas_call(
        forward_kernel,
        out_shape=outs,
        in_specs=[ANY, ANY, vmem] + [ANY] * 7,
        out_specs=[ANY] * len(outs),
        scratch_shapes=[
            vm(bf), vm(bf), pltpu.VMEM((vec.shape[0] * RING * LINE, LANES), BF), pltpu.VMEM((24, d), F32), pltpu.VMEM((8, d), F32),
            pltpu.VMEM((8, d, d), BF), pltpu.VMEM((QUARTERS, QUARTERS * quarter, d // QUARTERS), BF),
            vm(heads), vm(heads), vm(heads), pltpu.VMEM((length, length), F32), pltpu.VMEM((4, length, length), BF),
            vm(bf), vm(wide), pltpu.VMEM((length, LANES), F32), vm(bf), vm(mlp), vm(mlp), vm(wide), vm(wide), vm(bf), vm(bf),
            dma((n,)), dma((n, 6)), dma((n, 4)), dma((n, 4)), dma((n, 4)), dma((n, 4)), dma((n, 4)),
            dma((2, 4)), dma((2, 4)), dma((2,)), dma((n,)), dma((4,)), dma((16,)),
        ],
        compiler_params=pltpu.CompilerParams(collective_id=0, has_side_effects=True, vmem_limit_bytes=58 << 20),
        name="forward",
    )(tok, cot, labels, vec, *weights)


def backward_kernel(
    x_in, wq, wk, wv, wo, wi, wu, q_in, k_in, v_in, p_in, ctx_in, low_in,
    n1_in, scale_in, hid_in, slope_in, gsec_in, gout_in, lay_in, vec_in, part_in,
    lay_out, gtok_out, oq, ok, ov, oo, oi, ou, vec_out,
    from_core, half, plane, line, own, to_send, acc, zsum, ztot, vbuf, vrecv,
    hidden, gout, slope, ginner, gfirst, n1, scale1, low, dk, dv, probs, w_in, vecs, part, sums,
    credit, cs, cr, hs, hr, ps, pr, zs, zr, out_sem, vs, vr, a_send, a_recv, a_local, i_sem, w_sem, p_sem,
):
    me = Place()
    a_sems = (a_send, a_recv, a_local)
    length, d = gout.shape
    rows = d // RING
    q, k, v, x = hidden.at[0], hidden.at[1], hidden.at[2], hidden.at[3]
    gattn, gctx, ctx, gtok = slope.at[0], slope.at[1], slope.at[2], slope.at[3]
    dq = gout

    units = []

    def whole(ref):
        return lambda lo: ref[:, at_tile(lo, rows)]

    def tall(j):
        return lambda lo: hidden[lo // 2, :, pl.ds(pl.multiple_of(lax.rem(lo, 2) * (QUARTERS * rows) + j * rows, rows), rows)]

    for j in range(QUARTERS):
        units.append((tall(j), lambda at: gout[:, at], lambda o, w, j=j: ou.at[pl.ds(j * rows, rows), pl.ds(o, w)]))
    for j in range(QUARTERS):
        units.append((whole(low), lambda at, j=j: ginner[j, :, at], lambda o, w, j=j: oi.at[:, pl.ds(j * d + o, w)]))
    for left, right, out in ((ctx, gattn, oo), (x, dv, ov), (x, dk, ok), (x, dq, oq)):
        units.append((whole(left), lambda at, right=right: right[:, at], lambda o, w, out=out: out.at[:, pl.ds(o, w)]))
    parts, members = [], []
    for unit, count in enumerate(BACK_PARTS):
        members.append([])
        for i in range(count):
            members[unit].append(len(parts))
            parts.append((unit, i * (d // count), d // count))
    n = len(parts)

    def at_of(i):
        return pl.ds(parts[i][1], parts[i][2])

    def leads(i, slots):
        unit = parts[i][0]
        return members[unit - slots] if i == members[unit][0] and unit >= slots else ()

    core_slots, acc_slots, z_slots = from_core.shape[0], acc.shape[0], zsum.shape[0]

    def load(src, dst, i):
        return pltpu.make_async_copy(src, dst, i_sem.at[i])

    pieces = []
    for j in range(QUARTERS):
        pieces += [wu.at[pl.ds(j * d, d)], wi.at[:, pl.ds(j * d, d)]]
    pieces += [wo, wq, wk, wv]

    def w_load(i):
        return pltpu.make_async_copy(pieces[i], w_in.at[i % 3], w_sem.at[i % 3])

    def core_all(i):
        here = from_core.at[parts[i][0] % core_slots, :, :, at_of(i)]
        return send(here, here, cs.at[i], cr.at[i], me.at_c)

    def part_of(ref, i, *index):
        return ref.at[(parts[i][0] % ref.shape[0], *index, at_of(i))]

    low_rows, high_rows, all_rows = pl.ds(0, rows // 2), pl.ds(rows // 2, rows // 2), pl.ds(0, rows)

    def half_x(i):
        return send(part_of(acc, i, me.chip_d, low_rows), part_of(half, i, 0, low_rows), hs.at[i, 0], hr.at[i, 0], me.at_x)

    def half_y(i):
        return send(part_of(acc, i, me.chip_d, high_rows), part_of(half, i, 1, low_rows), hs.at[i, 1], hr.at[i, 1], me.at_y)

    def plane_x(i):
        return send(part_of(acc, i, me.chip_x, all_rows), part_of(plane, i, 0, all_rows), ps.at[i, 0], pr.at[i, 0], me.at_x)

    def plane_y(i):
        return send(part_of(acc, i, me.chip_y, all_rows), part_of(plane, i, 1, all_rows), ps.at[i, 1], pr.at[i, 1], me.at_y)

    end = (me.s == 0) | (me.s == 3)
    mid = (me.s == 1) | (me.s == 2)
    partner = me.along(me.s + 1 - 2 * lax.rem(me.s, 2))
    other = me.along(3 - me.s)

    def line_in(i):
        return send(part_of(zsum, i, all_rows), part_of(line, i, 0, all_rows), zs.at[i, 0], zr.at[i, 0], partner)

    def line_swap(i):
        return send(part_of(zsum, i, all_rows), part_of(line, i, 1, all_rows), zs.at[i, 0], zr.at[i, 1], other)

    def line_back(i):
        return send(part_of(ztot, i, all_rows), part_of(line, i, 0, all_rows), zs.at[i, 1], zr.at[i, 0], partner)

    def out_of(i):
        unit, offset, width = parts[i]
        return units[unit][2](offset, width)

    def out_mid(i):
        return pltpu.make_async_copy(part_of(ztot, i, all_rows), out_of(i), out_sem.at[i])

    def out_end(i):
        return pltpu.make_async_copy(part_of(line, i, 0, all_rows), out_of(i), out_sem.at[i])

    def wide(a):
        return a.astype(F32)

    def add(dst, a, b):
        dst[...] = (wide(a[...]) + wide(b[...])).astype(BF)

    def produce(i):
        unit = parts[i][0]
        left, right, _ = units[unit]
        at, slot = at_of(i), unit % 2
        for m in leads(i, 2):
            core_all(m).wait_send()
        if leads(i, core_slots):
            pl.semaphore_wait(credit, 1)

        def step(j, _):
            to_send[slot, j, :, at] = mm(left(2 * j + 1 - me.c), right(at), 0, 0).astype(BF)
            there = from_core.at[unit % core_slots, j, :, at]
            send(to_send.at[slot, j, :, at], there, cs.at[i], cr.at[i], me.at_c).start()
            return 0

        steps(0, 4, step, 0)

        def keep(j, _):
            own[slot, j, :, at] = mm(left(2 * j + me.c), right(at), 0, 0).astype(BF)
            return 0

        steps(0, 4, keep, 0)

    def s1(i):
        unit = parts[i][0]
        for m in leads(i, acc_slots):
            sent_acc(m)
        core_all(i).wait_recv()

        def step(j, _):
            here = (j, all_rows)
            add(part_of(acc, i, *here), part_of(own, i, *here), part_of(from_core, i, *here))
            return 0

        steps(0, 4, step, 0)
        half_x(i).start()
        half_y(i).start()
        if i == members[unit][-1] and unit + core_slots < len(units):
            pl.semaphore_signal(credit, inc=1, device_id=me.at_c, device_id_type=MESH)

    def s2(i):
        half_x(i).wait_recv()
        here = part_of(acc, i, me.chip_y, low_rows)
        add(here, here, part_of(half, i, 0, low_rows))
        plane_y(i).start()
        half_y(i).wait_recv()
        here = part_of(acc, i, me.chip_x, high_rows)
        add(here, here, part_of(half, i, 1, low_rows))
        plane_x(i).start()

    def s3(i):
        for m in leads(i, z_slots):
            pl.when(end)(lambda m=m: line_in(m).wait_send())
            pl.when(mid)(lambda m=m: line_swap(m).wait_send())
        plane_x(i).wait_recv()
        plane_y(i).wait_recv()
        got = wide(part_of(plane, i, 0, all_rows)[...]) + wide(part_of(plane, i, 1, all_rows)[...])
        part_of(zsum, i, all_rows)[...] = (wide(part_of(acc, i, me.chip, all_rows)[...]) + got).astype(BF)
        pl.when(end)(lambda: line_in(i).start())

    def z1(i):
        @pl.when(mid)
        def _():
            line_in(i).wait_recv()
            here = part_of(zsum, i, all_rows)
            add(here, here, part_of(line, i, 0, all_rows))
            line_swap(i).start()

    def z2(i):
        @pl.when(mid)
        def _():
            for m in leads(i, z_slots):
                line_back(m).wait_send()
                out_mid(m).wait()
            line_swap(i).wait_recv()
            add(part_of(ztot, i, all_rows), part_of(zsum, i, all_rows), part_of(line, i, 1, all_rows))
            line_back(i).start()
            out_mid(i).start()

    def z3(i):
        @pl.when(end)
        def _():
            line_back(i).wait_recv()
            out_end(i).start()

    def sent_acc(i):
        half_x(i).wait_send()
        half_y(i).wait_send()
        plane_x(i).wait_send()
        plane_y(i).wait_send()

    def v_swap(i, to):
        return send(vbuf.at[i], vrecv.at[i], vs.at[i], vr.at[i], to)

    v_to = (me.at_c, me.at_x, me.at_y)

    def v_step(i):
        if i == 0:
            vbuf[0] = sums[...]
            v_swap(0, v_to[0]).start()
        elif i < 4:
            v_swap(i - 1, v_to[i - 1]).wait_recv()
            vbuf[i] = vbuf[i - 1] + vrecv[i - 1]
            if i < 3:
                v_swap(i, v_to[i]).start()
            else:
                pl.when(end)(lambda: v_swap(3, partner).start())
        elif i == 4:

            @pl.when(mid)
            def _():
                v_swap(3, partner).wait_recv()
                vbuf[4] = vbuf[3] + vrecv[3]
                v_swap(4, other).start()

        elif i == 5:

            @pl.when(mid)
            def _():
                v_swap(4, other).wait_recv()
                vbuf[5] = vbuf[4] + vrecv[4]
                v_swap(5, partner).start()
                vec_out[...] = vbuf[5]

        elif i == 6:

            @pl.when(end)
            def _():
                v_swap(5, partner).wait_recv()
                vec_out[...] = vrecv[5]

    def put(i, value, tile=slice(None)):
        sums[pl.ds(i, 1), tile] = jnp.sum(value, axis=0, keepdims=True)

    def inner_grad(quarter, slot):
        def step(j, _):
            tile = at_tile(j, TILE)
            y = mm(gout[...], w_in[slot, tile, :], 1, 1) * wide(slope[quarter, :, tile])
            y = y.astype(BF)
            ginner[quarter, :, tile] = y
            put(8 + quarter, wide(y), tile)
            return 0

        steps(0, d // TILE, step, 0)

    def first_grad(quarter, slot):
        def step(j, _):
            tile = at_tile(j, TILE)
            gfirst[:, tile] = gfirst[:, tile] + mm(ginner[quarter], w_in[slot, tile, :], 1, 1)
            return 0

        steps(0, d // TILE, step, 0)

    def first_norm_back():
        gain = vecs[pl.ds(G1, 1), :]

        def step(j, carry):
            at = at_tile(j, ROW)
            g, centred = gfirst[at, :], n1[at, :]
            grad = norm_back(g * gain, centred, scale1[at, :1])
            gfirst[at, :] = grad
            rounded = grad.astype(BF)
            gattn[at, :] = rounded
            return carry[0] + eighths(g * centred), carry[1] + eighths(g), carry[2] + eighths(wide(rounded))

        zero = jnp.zeros((8, d), F32)
        gains, shifts, biases = steps(0, length // ROW, step, (zero, zero, zero))
        put(4, gains)
        put(5, shifts)
        put(2, biases)

    def context_grad(slot):
        def step(j, _):
            tile = at_tile(j, TILE)
            gctx[:, tile] = mm(gattn[...], w_in[slot, tile, :], 1, 1).astype(BF)
            return 0

        steps(0, d // TILE, step, 0)

    def p_load(pair, h, slot):
        return pltpu.make_async_copy(p_in.at[2 * pair + h], probs.at[slot, h], p_sem.at[slot, h])

    def attend_back(pair):
        slot = pair % 2
        if pair + 1 < d // LANES:
            for h in range(2):
                p_load(pair + 1, h, 1 - slot).start()
        masks = half_masks()
        at = pl.ds(pair * LANES, LANES)
        qp, kp, vp, gp = q[:, at], k[:, at], v[:, at], gctx[:, at]
        outs = None
        for h in range(2):
            p_load(pair, h, slot).wait()
            p = wide(probs[slot, h])
            g = mm(gp * masks[h].astype(BF), vp, 1, 1)
            w = p * g
            s = (w - p * jnp.sum(w, axis=1, keepdims=True)).astype(BF)
            got = (
                mm(s, kp) * (masks[h] * (1.0 / math.sqrt(HD))),
                mm(s, qp, 0, 0) * masks[h],
                mm(probs[slot, h], gp, 0, 0) * masks[h],
            )
            outs = got if outs is None else tuple(a + b for a, b in zip(outs, got))
        for ref, y, i in ((dq, outs[0], 0), (dk, outs[1], None), (dv, outs[2], 1)):
            y = y.astype(BF)
            ref[:, at] = y
            if i is not None:
                put(i, wide(y), at)

    def token_grad(j):
        tile = pl.ds(j * TILE, TILE)
        y = gfirst[:, tile]
        for ref, i in ((dq, 9), (dk, 10), (dv, 11)):
            y = y + mm(ref[...], w_in[i % 3, tile, :], 1, 1)
        gtok[:, tile] = y.astype(BF)

    for quarter in range(QUARTERS):
        load(hid_in.at[quarter], hidden.at[quarter], quarter).start()
    load(gout_in, gout, 4).start()
    w_load(0).start()
    load(slope_in, slope, 5).start()
    w_load(1).start()
    load(gsec_in, gfirst, 6).start()
    later = ((low_in, low, 7), (n1_in, n1, 8), (scale_in, scale1, 9), (vec_in, vecs, 10), (part_in, part, 11))
    for src, dst, i in later:
        load(src, dst, i).start()
    greet(me)
    lay_back = Exchange(me, lay_in, lay_out, a_sems, 0, True)
    tok_back = Exchange(me, gtok, gtok_out, a_sems, 1, True)
    for quarter in range(QUARTERS):
        load(hid_in.at[quarter], hidden.at[quarter], quarter).wait()
    load(gout_in, gout, 4).wait()
    sums[...] = jnp.zeros_like(sums)
    stages = {"P": produce, "S1": s1, "S2": s2, "S3": s3, "Z1": z1, "Z2": z2, "Z3": z3, "V": v_step, "AB": attend_back, "TG": token_grad}
    for op, *at in BACK_ORDER:
        i = at[0] if at else 0
        if op == "V" and i == 0:
            for row, j in ((0, 6), (1, 7), (2, 3)):
                sums[pl.ds(j, 1), :] = part[pl.ds(row, 1), :]
        if op in stages:
            stages[op](i)
        elif op in ("LO", "GT"):
            (lay_back if op == "LO" else tok_back).start(*at)
        elif op == "IG":
            if i == 0:
                load(slope_in, slope, 5).wait()
                load(gsec_in, gfirst, 6).wait()
                load(low_in, low, 7).wait()
            w_load(2 * i + 2).start()
            w_load(2 * i).wait()
            inner_grad(i, (2 * i) % 3)
        elif op == "FG":
            w_load(2 * i + 3).start()
            w_load(2 * i + 1).wait()
            first_grad(i, (2 * i + 1) % 3)
        elif op == "LD":
            for src, dst, j in ((q_in, q, 0), (k_in, k, 1), (v_in, v, 2)):
                for pair in range(d // LANES):
                    load(src.at[pair], dst.at[:, pl.ds(pair * LANES, LANES)], j).start()
            load(x_in, x, 3).start()
            load(ctx_in, ctx, 5).start()
            for h in range(2):
                p_load(0, h, 0).start()
        elif op == "LW":
            for dst, j in ((q, 0), (k, 1), (v, 2)):
                load(x_in, dst, j).wait()
            load(x_in, x, 3).wait()
            load(ctx_in, ctx, 5).wait()
        elif op == "NB":
            for src, dst, j in later[1:]:
                load(src, dst, j).wait()
            first_norm_back()
        elif op == "CG":
            w_load(10).start()
            w_load(8).wait()
            context_grad(8 % 3)
            w_load(11).start()
        elif op == "TW":
            for j in (9, 10, 11):
                w_load(j).wait()
    for unit in members[-2:]:
        for i in unit:
            core_all(i).wait_send()
    for unit in members[-acc_slots:]:
        for i in unit:
            sent_acc(i)
    for i in range(n):
        pl.when(end)(lambda i=i: out_end(i).wait())
    for unit in members[-z_slots:]:
        for i in unit:
            pl.when(end)(lambda i=i: line_in(i).wait_send())

            @pl.when(mid)
            def _(i=i):
                line_swap(i).wait_send()
                line_back(i).wait_send()
                out_mid(i).wait()

    for i in range(3):
        v_swap(i, v_to[i]).wait_send()
    pl.when(end)(lambda: v_swap(3, partner).wait_send())

    @pl.when(mid)
    def _():
        v_swap(4, other).wait_send()
        v_swap(5, partner).wait_send()

    for exchange in (lay_back, tok_back):
        exchange.wait()
        exchange.sent()


def backward_all(saved, block):
    length, d = saved[0].shape
    rows = d // RING
    units, n = len(BACK_PARTS), sum(BACK_PARTS)
    core_slots, acc_slots, z_slots = 3, 3, 3
    dma = pltpu.SemaphoreType.DMA
    shape = jax.ShapeDtypeStruct

    def vm(*s, dtype=BF):
        return pltpu.VMEM(s, dtype)

    split = shape((LINE, block, d), BF)
    sq = shape((rows, d), BF)
    sums = (16, d)
    outs = [split, split, sq, sq, sq, sq, shape((rows, QUARTERS * d), BF), shape((QUARTERS * rows, d), BF), shape(sums, F32)]
    mat = (length, d)
    mlp = (QUARTERS, length, d)
    return pl.pallas_call(
        backward_kernel,
        out_shape=outs,
        in_specs=[ANY] * len(saved),
        out_specs=[ANY] * 8 + [pl.BlockSpec(memory_space=pltpu.VMEM)],
        scratch_shapes=[
            vm(core_slots, 4, rows, d), vm(units, 2, rows // 2, d), vm(units, 2, rows, d), vm(units, 2, rows, d),
            vm(2, 4, rows, d), vm(2, 4, rows, d), vm(acc_slots, 4, rows, d), vm(z_slots, rows, d), vm(z_slots, rows, d),
            vm(6, *sums, dtype=F32), vm(6, *sums, dtype=F32),
            vm(*mlp), vm(*mat), vm(*mlp), vm(*mlp), vm(*mat, dtype=F32), vm(*mat, dtype=F32), vm(length, LANES, dtype=F32), vm(*mat),
            vm(*mat), vm(*mat), vm(2, 2, length, length), vm(3, d, d), vm(24, d, dtype=F32), vm(8, d, dtype=F32), vm(*sums, dtype=F32),
            pltpu.SemaphoreType.REGULAR,
            dma((n,)), dma((n,)), dma((n, 2)), dma((n, 2)), dma((n, 2)), dma((n, 2)), dma((n, 2)), dma((n, 2)),
            dma((n,)), dma((6,)), dma((6,)), dma((2, 4)), dma((2, 4)), dma((2,)), dma((12,)), dma((3,)), dma((2, 2)),
        ],
        compiler_params=pltpu.CompilerParams(collective_id=1, has_side_effects=True, vmem_limit_bytes=62 << 20),
        name="backward",
    )(*saved)


def pack_kernel(*refs):
    out = refs[-1]
    rows = []
    for ref in refs[:-1]:
        row = ref[...].astype(F32).reshape(1, ref.shape[0])
        if ref.shape[0] < LANES:
            row = jnp.concatenate([row, jnp.zeros((1, LANES - ref.shape[0]), F32)], axis=1)
        rows.append(row)
    rows.append(jnp.zeros((out.shape[0] - len(rows), LANES), F32))
    out[...] = jnp.concatenate(rows, axis=0).astype(BF)


def pack(vectors):
    vmem = pl.BlockSpec(memory_space=pltpu.VMEM)
    return pl.pallas_call(
        pack_kernel,
        in_specs=[vmem] * len(vectors),
        out_specs=vmem,
        out_shape=jax.ShapeDtypeStruct((16, LANES), BF),
        name="pack",
    )(*vectors)


def finish_kernel(lay, gtok, *rest):
    mats, sums, outs = rest[:6], rest[6], rest[7:]
    outs[0][...] = lay[...]
    outs[1][...] = gtok[...]
    for src, dst in zip(mats, outs[2:8]):
        dst[...] = src[...].astype(F32)
    lo = lax.axis_index("grp")
    for i, dst in zip((0, 1, 2, 8, 3, 4, 5, 6, 7), outs[8:]):
        n = dst.shape[0]
        if i < 8:
            row, column = i, lo * n
        else:
            per = sums.shape[1] // n
            row, column = 8 + lo // per, lax.rem(lo, per) * n
        dst[...] = sums[pl.ds(row, 1), pl.ds(pl.multiple_of(column, LANES), n)].reshape(n)


def finish(out):
    count = out[0].shape[0]
    shape = jax.ShapeDtypeStruct

    def rows(a, dtype):
        block = (a.shape[0] // count,) + a.shape[1:]
        return pl.BlockSpec(block, lambda i: (i,) + (0,) * (len(block) - 1)), shape(a.shape, dtype)

    d = out[8].shape[1]
    ins = [rows(a, a.dtype)[0] for a in out[:8]] + [pl.BlockSpec(out[8].shape, lambda i: (0, 0))]
    big = [rows(a, a.dtype if k < 2 else F32) for k, a in enumerate(out[:8])]
    sizes = [d // RING] * 3 + [QUARTERS * d // RING] + [d // RING] * 5
    small = [(pl.BlockSpec((n,), lambda i: (0,)), shape((n,), F32)) for n in sizes]
    specs, shapes = zip(*(big + small))
    return tuple(
        pl.pallas_call(
            finish_kernel,
            grid=(count,),
            in_specs=ins,
            out_specs=list(specs),
            out_shape=list(shapes),
            compiler_params=pltpu.CompilerParams(vmem_limit_bytes=62 << 20),
            name="finish",
        )(*out)
    )


def local(tokens, labels, *rest):
    weights, vectors, cotangent = rest[:6], rest[6:15], rest[15]
    groups = lax.axis_size("grp") // RING
    g, s = lax.axis_index("grp"), lax.axis_index("seq")
    lo = lax.rem(g, RING)
    if groups > 1:
        def regroup(w):
            full = lax.all_gather(w, ("grp", "seq"), axis=0, tiled=True)
            n = full.shape[0] // (RING * LINE)
            return lax.dynamic_slice_in_dim(full, (lo * LINE + s) * n, n, 0)

        weights = tuple(regroup(w) for w in weights)
        vectors = tuple(regroup(v) for v in vectors)
    packed = pack(vectors)
    saved = forward_all(tokens, cotangent, labels, packed, weights)
    out = backward_all(saved, tokens.shape[1])
    if groups == 1:
        return finish(out)
    layer_out, grad_tokens = out[:2]
    mats = [m.astype(F32) for m in out[2:8]]
    vec = out[8]
    flat = [vec[i] for i in range(8)]
    flat.insert(3, vec[8 : 8 + QUARTERS].reshape(-1))
    same = [[l + RING * h for h in range(groups)] for l in range(RING)]
    eight = [[l + RING * h for l in range(RING)] for h in range(groups)]

    def rejoin(m):
        m = lax.psum(m, "grp", axis_index_groups=same)
        m = lax.all_gather(m, "grp", axis=0, tiled=True, axis_index_groups=eight)
        n = m.shape[0] // (RING * groups)
        return lax.dynamic_slice_in_dim(m, g * n, n, 0)

    mats = [rejoin(m) for m in mats]
    flat = [lax.psum(v, "grp", axis_index_groups=same) for v in flat]
    flat = [lax.dynamic_slice_in_dim(v, g * (v.shape[0] // (RING * groups)), v.shape[0] // (RING * groups), 0) for v in flat]
    return (layer_out, grad_tokens, *mats, *flat)


def solution(mesh):
    both = ("grp", "seq")
    rows = P("grp", "seq", None)
    return jax.shard_map(
        local,
        mesh=mesh,
        in_specs=(rows, P("grp", None)) + (P(both, None),) * 6 + (P(both),) * 9 + (rows,),
        out_specs=(rows, rows) + (P("grp", None),) * 6 + (P("grp"),) * 9,
        check_vma=False,
    )
```
